32 devices in a mesh: dp: 8 (over z, y), ctx: 4 (over x, core).
Axes of the slice: x: 2, y: 2, z: 4, core: 2. Of those that a mesh axis runs over, the one named last changes fastest.
Arguments:
- tokens: bfloat16 [8, 2048, 768], P('dp', 'ctx'), may hold values from -6 to 6
- attn_gain: bfloat16 [768], P('dp'), may hold values from 0.5 to 1.5
- attn_shift: bfloat16 [768], P('dp'), may hold values from -2 to 2
- w_qkv: bfloat16 [768, 2304], P('dp'), may hold values from -0.21875 to 0.21875
- w_out: bfloat16 [768, 768], P('dp'), may hold values from -6 to 6
- ffn_gain: bfloat16 [768], P('dp'), may hold values from 0.5 to 1.5
- ffn_shift: bfloat16 [768], P('dp'), may hold values from -2 to 2
- w_in: bfloat16 [768, 3072], P('dp'), may hold values from -0.21875 to 0.21875
- b_in: bfloat16 [3072], P('dp'), may hold values from -2 to 2
- w_down: bfloat16 [3072, 768], P('dp'), may hold values from -0.109375 to 0.109375
- b_down: bfloat16 [768], P('dp'), may hold values from -2 to 2
- cotangent: bfloat16 [8, 2048, 768], P('dp', 'ctx'), may hold values from -6 to 6
- lengths: int32 [8], P('dp'), may hold values from 512 to 2048, as said below
- block_order: int32 [8, 4], P('dp'), may hold values from 0 to 3, each once within a row
Outputs:
- layer_out: bfloat16 [8, 2048, 768], P('dp', 'ctx')
- input_grad: bfloat16 [8, 2048, 768], P('dp', 'ctx')
- grad_attn_gain: float32 [768], P('dp')
- grad_attn_shift: float32 [768], P('dp')
- grad_w_qkv: float32 [768, 2304], P('dp')
- grad_w_out: float32 [768, 768], P('dp')
- grad_ffn_gain: float32 [768], P('dp')
- grad_ffn_shift: float32 [768], P('dp')
- grad_w_in: float32 [768, 3072], P('dp')
- grad_b_in: float32 [3072], P('dp')
- grad_w_down: float32 [3072, 768], P('dp')
- grad_b_down: float32 [768], P('dp')
The draws below stay inside these ranges and needn't reach their ends.
Inputs may be any that keep to these rules, and one draw needn't show every extreme that they name: `lengths`: valid positions form the head of each sequence; one sequence has 2048 of them and one has 512. Each row is a permutation; index c of ctx holds positions block_order[s, c] * 512 to block_order[s, c] * 512 + 511 of sequence s.
All inputs are finite; a program needn't handle non-finite values.
Results may differ from the reference program's by a relative error of at most 0.013.
Values may be sent and summed in bfloat16 or wider, within the bound.
No kernel may reach another device: no remote copies, remote signals or barrier semaphores. Data moves between devices by JAX's collectives and lax.ppermute only.
A program may use at most 128 MiB of HBM per device.

```python
import jax
import jax.numpy as jnp
from jax import lax

D = 768
H = 12
FF = 3072
CH = 512
DH = 64
LEN = 2048
SEQS = 8
N_CTX = 4


def draw_lengths(key, part):
    first_key, second_key = jax.random.split(jax.random.fold_in(key, 17))
    drawn = jax.random.randint(first_key, (SEQS,), LEN // 4, LEN + 1, dtype=jnp.int32)
    order = jax.random.permutation(second_key, SEQS)
    drawn = jnp.where(order == 0, LEN, drawn)
    drawn = jnp.where(order == 1, LEN // 4, drawn)
    return drawn.astype(jnp.int32)


def steps_of(stream_key, extent, cuts, least, high):
    loudness = 1.0
    for dim, parts in cuts:
        draws = jax.random.uniform(jax.random.fold_in(jax.random.fold_in(stream_key, 6), dim), (parts,), jnp.float32, least / len(cuts), high / len(cuts))
        loudness = loudness * jnp.repeat(jnp.exp(draws), extent[dim] // parts).reshape((-1,) + (1,) * (len(extent) - 1 - dim))
    return loudness


def normal_values(own_key, extent, scale, reach, pieces=(), kind=jnp.bfloat16):
    array = jax.random.normal(own_key, extent, jnp.float32) * scale
    if len(pieces) > 0:
        array = steps_of(own_key, extent, pieces, -0.22, 0.18) * array
    return jnp.clip(array, min=-reach, max=reach).astype(kind)


def setup_inputs(seed: int = 0) -> dict:
    splits = jax.random.split(jax.random.key(seed), 15)
    return {
        "tokens": normal_values(splits[0], (SEQS, LEN, D), 1.0, 6.0, ((0, 8), (1, 4))),
        "attn_gain": jnp.clip(1.0 + 0.1 * jax.random.normal(splits[1], (D,), jnp.float32), 0.5, 1.5).astype(jnp.bfloat16),
        "attn_shift": normal_values(splits[2], (D,), 0.3, 2.0, ((0, 8),)),
        "w_qkv": normal_values(splits[3], (D, 3 * D), D ** -0.5, 0.21875, ((0, 8),)),
        "w_out": normal_values(splits[4], (D, D), (max(1, 4 * D // LEN)) ** -0.5, 6.0, ((0, 8),)),
        "ffn_gain": jnp.clip(1.0 + 0.1 * jax.random.normal(splits[5], (D,), jnp.float32), 0.5, 1.5).astype(jnp.bfloat16),
        "ffn_shift": normal_values(splits[6], (D,), 0.3, 2.0, ((0, 8),)),
        "w_in": normal_values(splits[7], (D, FF), D ** -0.5, 0.21875, ((0, 8),)),
        "b_in": normal_values(splits[8], (FF,), 0.3, 2.0, ((0, 8),)),
        "w_down": normal_values(splits[9], (FF, D), FF ** -0.5, 0.109375, ((0, 8),)),
        "b_down": normal_values(splits[10], (D,), 0.3, 2.0, ((0, 8),)),
        "cotangent": normal_values(splits[11], (SEQS, LEN, D), 1.0, 6.0, ((0, 8), (1, 4))),
        "lengths": draw_lengths(jax.random.fold_in(splits[14], 71), 0),
        "block_order": jax.vmap(lambda own: jax.random.permutation(own, N_CTX))(jax.random.split(splits[13], SEQS)).reshape((SEQS, N_CTX)).astype(jnp.int32),
    }


@jax.custom_vjp
def low(v):
    return lax.optimization_barrier(v.astype(jnp.bfloat16)).astype(jnp.float32)

@jax.custom_vjp
def low_back(v):
    return v

def low_keep(v):
    return (low(v), None)

def low_pass(kept, grad):
    return (grad,)

def back_keep(v):
    return (v, None)

def back_low(kept, grad):
    return (low(grad),)
low.defvjp(low_keep, low_pass)
low_back.defvjp(back_keep, back_low)
epsilon = 1e-05
masked_score = -1000000000.0
highest = lax.Precision.HIGHEST
gelu_coeff = 0.7978845608
cubic_term = 0.044715

def smooth_gate(values):
    return 0.5 * values * (1.0 + jnp.tanh(gelu_coeff * (values + cubic_term * values * values * values)))

def layer_norm(values, gain, shift):
    center = values - lax.optimization_barrier(jnp.mean(values, axis=-1, keepdims=True))
    spread = lax.optimization_barrier(jnp.mean(center * center, axis=-1, keepdims=True))
    return center * lax.rsqrt(spread + epsilon) * gain + shift

def matmul(left, right):
    return jnp.dot(left, right, precision=highest)

def forward_seq(params, inputs, valid):
    attn_gain, attn_shift, w_qkv, w_out, ffn_gain, ffn_shift, w_in, b_in, w_down, b_down = params
    scale = DH ** (-0.5)
    first = low(layer_norm(inputs, attn_gain, attn_shift))
    qkv = low_back(low(matmul(first, w_qkv)))
    query = qkv[:, :D].reshape(N_CTX, CH, H, DH)
    key_heads = qkv[:, D:2 * D].reshape(LEN, H, DH)
    value_heads = qkv[:, 2 * D:].reshape(LEN, H, DH)
    key_valid = valid > 0.5

    def attend(query_block):
        scores = jnp.einsum('qhd,khd->hqk', query_block, key_heads, precision=highest) * scale
        scores = low_back(scores)
        scores = jnp.where(key_valid[None, None, :], scores, masked_score)
        probs = jax.nn.softmax(scores, axis=-1)
        return jnp.einsum('hqk,khd->qhd', probs, value_heads, precision=highest)
    attended = lax.map(jax.checkpoint(attend), query).reshape(LEN, D)
    attended = low_back(low(attended))
    mixed = inputs + low_back(matmul(attended, w_out))
    second = low(layer_norm(mixed, ffn_gain, ffn_shift))
    hidden = low_back(matmul(second, w_in) + b_in)
    active = low(smooth_gate(hidden))
    branch = low_back(matmul(active, w_down) + b_down)
    return (mixed + branch) * valid[:, None]

def reference(tokens, attn_gain, attn_shift, w_qkv, w_out, ffn_gain, ffn_shift, w_in, b_in, w_down, b_down, cotangent, lengths, block_order):
    params = tuple((item.astype(jnp.float32) for item in (attn_gain, attn_shift, w_qkv, w_out, ffn_gain, ffn_shift, w_in, b_in, w_down, b_down)))
    offsets = jnp.tile(jnp.arange(CH, dtype=jnp.int32), N_CTX)

    def per_sequence(totals, seq_item):
        inputs, tangent, length, order_row = seq_item
        starts = order_row.astype(jnp.int32) * CH
        places = jnp.repeat(starts, CH) + offsets
        valid = (places < length).astype(jnp.float32)

        def run_layer(weights, values):
            return forward_seq(weights, values, valid)
        result, pullback = jax.vjp(run_layer, params, inputs)
        grads, input_grad = pullback(tangent)
        totals = jax.tree.map(lambda left, right: left + right, totals, grads)
        return (totals, (result.astype(jnp.bfloat16), input_grad.astype(jnp.bfloat16)))
    zero_grads = jax.tree.map(jnp.zeros_like, params)
    totals, (layer_out, input_grad) = lax.scan(per_sequence, zero_grads, (tokens.astype(jnp.float32), cotangent.astype(jnp.float32), lengths.astype(jnp.int32), block_order.astype(jnp.int32)))
    return (layer_out, input_grad, totals[0], totals[1], totals[2], totals[3], totals[4], totals[5], totals[6], totals[7], totals[8], totals[9])
```

```python
import functools
import math

import jax
import jax.numpy as jnp
from jax import lax
from jax.experimental import pallas as pl
from jax.experimental.pallas import tpu as pltpu
from jax.sharding import PartitionSpec as P

H = 12

epsilon = 1e-05
gelu_coeff = 0.7978845608
cubic_term = 0.044715
excluded = -1073741824.0
bf16 = jnp.bfloat16
f32 = jnp.float32
LANES = 128
GROUP = 4
VMEM_BYTES = 52 * 1024 * 1024

nt_dims = (((1,), (1,)), ((), ()))
tn_dims = (((0,), (0,)), ((), ()))


def mm(left, right):
    return jnp.dot(left, right, preferred_element_type=f32)


def mm_nt(left, right):
    return lax.dot_general(left, right, nt_dims, preferred_element_type=f32)


def mm_tn(left, right):
    return lax.dot_general(left, right, tn_dims, preferred_element_type=f32)


def whole(memory_space=pltpu.VMEM):
    return pl.BlockSpec(memory_space=memory_space)


def lanes_of(shape):
    return lax.broadcasted_iota(jnp.int32, shape, 1)


def norm_parts(values):
    center = values - jnp.mean(values, axis=-1, keepdims=True)
    spread = jnp.mean(center * center, axis=-1, keepdims=True)
    inverse = lax.rsqrt(spread + epsilon)
    return center * inverse, inverse


def norm_back(scaled, unit, inverse):
    return inverse * (
        scaled
        - jnp.mean(scaled, axis=-1, keepdims=True)
        - unit * jnp.mean(scaled * unit, axis=-1, keepdims=True)
    )


def three_parts(value):
    first = value.astype(bf16).astype(f32)
    rest = value - first
    second = rest.astype(bf16).astype(f32)
    return first, second, rest - second


def with_parts(base, value):
    lane = lanes_of(base.shape)
    one, two, three = three_parts(value)
    return jnp.where(
        lane == 64, one, jnp.where(lane == 65, two, jnp.where(lane == 66, three, base))
    )


def unpack_rows(packed, rows):
    tail = jnp.concatenate([packed[rows:, :64], packed[rows:, 64:]], axis=0)
    return packed[:rows], tail


def swap(value, axis, bit):
    size = lax.axis_size(axis)
    return lax.ppermute(value, axis, [(i, i ^ bit) for i in range(size)])


def gather_dp(piece):
    far = [piece]
    for k in range(1, lax.axis_size("dp") // 2):
        far.append(swap(piece, "dp", 2 * k))
    near = jnp.stack(far)
    return near, swap(near, "dp", 1)


def scatter_dp(even, odd):
    received = swap(odd, "dp", 1)
    parts = []
    for k in range(even.shape[0]):
        parts.append((even[k].astype(f32) + received[k].astype(f32)).astype(bf16))
    total = parts[0].astype(f32)
    for k in range(1, even.shape[0]):
        total = total + swap(parts[k], "dp", 2 * k).astype(f32)
    return total


def sum_far_ctx(value, start):
    bit = start
    while bit < lax.axis_size("ctx"):
        low = value.astype(bf16)
        value = low.astype(f32) + swap(low, "ctx", bit).astype(f32)
        bit *= 2
    return value


def position_of(order_ref, slot, rows):
    index = lax.axis_index("ctx")
    return order_ref[0, lax.bitwise_xor(index, slot)] * rows


def qkv_kernel(length_ref, order_ref, *refs):
    tokens = refs[:GROUP]
    near, cross = refs[GROUP : GROUP + 2]
    q_ref, k_ref, v_ref, first_ref, small_ref, w_ref, sems = refs[GROUP + 2 :]
    halves, rows, _ = near.shape
    row_count, width = tokens[0].shape
    me = lax.axis_index("dp")
    copies = []
    for parity, source in ((0, near), (1, cross)):
        for k in range(halves):
            owner = lax.bitwise_xor(me, 2 * k + parity)
            copies.append(
                pltpu.make_async_copy(
                    source.at[k],
                    w_ref.at[pl.ds(pl.multiple_of(owner * rows, 16), rows)],
                    sems.at[2 * k + parity],
                )
            )
    for copy in copies:
        copy.start()
    for copy in copies:
        copy.wait()
    small = w_ref[:, 512:640].astype(f32).T
    small_ref[...] = small[64:80]
    gain, shift = small[64:65], small[65:66]
    length = length_ref[0]
    lane = lanes_of((row_count, LANES))
    ones = jnp.where((lane >= 64) & (lane < 67), 1.0, 0.0)
    bias_lane = jnp.where(lane == 67, 1.0, 0.0)
    for d in range(GROUP):
        unit, _ = norm_parts(tokens[d][...].astype(f32))
        first = (unit * gain + shift).astype(bf16)
        part = pl.ds(d * row_count, row_count)
        first_ref[part] = first
        qkv = mm(first, w_ref[...]).astype(bf16).astype(f32)

        def head(place):
            block = qkv[:, place // 2 * LANES : (place // 2 + 1) * LANES]
            if place % 2:
                block = pltpu.roll(block, 64, 1)
            return jnp.where(lane < 64, block, 0.0)

        stored = lax.broadcasted_iota(jnp.int32, (row_count, LANES), 0)
        position = position_of(order_ref, d, row_count) + stored
        bias = jnp.where(position < length, 0.0, excluded) * bias_lane
        for h in range(3):
            q_ref[h, part] = (head(2 * h) * 0.125 + bias_lane).astype(bf16)
            k_ref[h, part] = (head(2 * h + 1) + ones + bias).astype(bf16)
            v_ref[h, part] = (head(6 + h) + ones).astype(bf16)


def project(length, order, tokens, near, cross):
    row_count, width = tokens[0].shape
    total = GROUP * row_count
    wide = near.shape[2]
    head_out = jax.ShapeDtypeStruct((3, total, LANES), bf16)
    return pl.pallas_call(
        qkv_kernel,
        out_shape=(
            head_out,
            head_out,
            head_out,
            jax.ShapeDtypeStruct((total, width), bf16),
            jax.ShapeDtypeStruct((16, width), f32),
            jax.ShapeDtypeStruct((width, wide), bf16),
        ),
        in_specs=[whole(pltpu.SMEM)] * 2 + [whole()] * GROUP + [whole(pl.ANY)] * 2,
        out_specs=[whole()] * 6,
        scratch_shapes=[pltpu.SemaphoreType.DMA((2 * near.shape[0],))],
        compiler_params=pltpu.CompilerParams(vmem_limit_bytes=VMEM_BYTES),
        cost_estimate=pl.CostEstimate(
            flops=2 * total * width * wide, bytes_accessed=20 * total * width, transcendentals=0
        ),
    )(length, order, *tokens, near, cross)


def attend_kernel(block_rows, q_ref, k_ref, v_ref, packed_ref, q_out_ref):
    row_count = q_ref.shape[1]
    half = row_count // 2
    lane = lanes_of((block_rows, LANES))
    for i in range(row_count // block_rows):
        part = pl.ds(i * block_rows, block_rows)
        heads = []
        for h in range(3):
            query = q_ref[h, part]
            scores = mm_nt(query, k_ref[h])
            top = jnp.max(scores, axis=1, keepdims=True)
            weights = jnp.exp(scores - top).astype(bf16)
            result = mm(weights, v_ref[h])
            denom = result[:, 64:65]
            heads.append(jnp.where(lane < 64, result / denom, 0.0))
            log_total = top + jnp.log(denom)
            q_out_ref[h, part] = with_parts(query.astype(f32), -log_total).astype(bf16)
        packed_ref[0, part] = (heads[0] + pltpu.roll(heads[1], 64, 1)).astype(bf16)
        for r in range(0, block_rows, half):
            size = min(half, block_rows)
            row = i * block_rows + r
            side, place = row // half, row % half
            packed_ref[
                0, pl.ds(row_count + place, size), 64 * side : 64 * side + 64
            ] = heads[2][r : r + size, :64].astype(bf16)


def attend(query, keys, values, first_slot, slots, row_count):
    total = keys.shape[1]
    block_rows = min(row_count // 2, 256)
    return pl.pallas_call(
        functools.partial(attend_kernel, block_rows),
        grid=(slots,),
        out_shape=(
            jax.ShapeDtypeStruct((slots, row_count * 3 // 2, LANES), bf16),
            jax.ShapeDtypeStruct((3, slots * row_count, LANES), bf16),
        ),
        in_specs=[
            pl.BlockSpec((3, row_count, LANES), lambda s: (0, s + first_slot, 0)),
            whole(),
            whole(),
        ],
        out_specs=(
            pl.BlockSpec((1, row_count * 3 // 2, LANES), lambda s: (s, 0, 0)),
            pl.BlockSpec((3, row_count, LANES), lambda s: (0, s, 0)),
        ),
        compiler_params=pltpu.CompilerParams(vmem_limit_bytes=VMEM_BYTES),
        cost_estimate=pl.CostEstimate(
            flops=3 * slots * row_count * total * 64 * 4 * 4,
            bytes_accessed=3 * total * LANES * 8,
            transcendentals=3 * slots * row_count * total,
        ),
    )(query, keys, values)


def ffn_kernel(length_ref, order_ref, *refs):
    token_ref, cot_ref = refs[:2]
    attn_refs = refs[2 : 2 + GROUP]
    small_ref, bias_ref = refs[6:8]
    pieces = refs[8:16]
    out_ref, dmixed_ref, dattn_ref = refs[16:19]
    even_in, odd_in, sib_in, even_down, odd_down, sib_down = refs[19:25]
    small_grad_ref, bias_grad_ref = refs[25:27]
    w_o, w_i, w_d, g_o, g_i, g_d, second_t, second_ref, dlow_ref, out_acc, ds_acc, sems = refs[27:]
    row_count, width = token_ref.shape
    ff = w_i.shape[1]
    halves, rows, _ = pieces[0].shape
    frows = pieces[4].shape[1]
    me = lax.axis_index("dp")
    index = lax.axis_index("ctx")
    core = lax.rem(index, 2)
    low = lax.rem(index, GROUP)
    half_o, half_i, half_d = width // 2, ff // 2, width // 2

    loads = ([], [], [])
    for side in range(2):
        here = core if side == 0 else 1 - core
        for parity in range(2):
            in_piece = pieces[2 * side + parity]
            down_piece = pieces[4 + 2 * side + parity]
            for k in range(halves):
                owner = lax.bitwise_xor(me, 2 * k + parity)
                at_rows = pl.ds(pl.multiple_of(owner * rows, 16), rows)
                loads[0].append(
                    (
                        in_piece.at[k, :, pl.ds(0, half_o)],
                        w_o.at[at_rows, pl.ds(pl.multiple_of(here * half_o, LANES), half_o)],
                    )
                )
                loads[1].append(
                    (
                        in_piece.at[k, :, pl.ds(half_o, half_i)],
                        w_i.at[at_rows, pl.ds(pl.multiple_of(here * half_i, LANES), half_i)],
                    )
                )
                loads[2].append(
                    (
                        down_piece.at[k],
                        w_d.at[
                            pl.ds(pl.multiple_of(owner * frows, 16), frows),
                            pl.ds(pl.multiple_of(here * half_d, LANES), half_d),
                        ],
                    )
                )
    number = len(loads[0])
    copies = [
        [pltpu.make_async_copy(a, b, sems.at[g * number + i]) for i, (a, b) in enumerate(group)]
        for g, group in enumerate(loads)
    ]
    for group in copies:
        for copy in group:
            copy.start()
    for copy in copies[0]:
        copy.wait()

    def out_rows(d):
        return pl.ds(pl.multiple_of(lax.bitwise_xor(low, d) * 192, 16), 192)

    attn = []
    for d in range(GROUP):
        packed = attn_refs[d][...]
        attn.append(jnp.concatenate(unpack_rows(packed, row_count), axis=1))
    mixed = token_ref[...].astype(f32)
    for d in range(GROUP):
        mixed = mixed + mm(attn[d], w_o[out_rows(d), :])
    unit, inverse = norm_parts(mixed)
    gain = small_ref[2:3]
    second = unit * gain + small_ref[3:4]
    second_ref[...] = second.astype(bf16)
    second_t[...] = second.T.astype(bf16)
    stored = lax.broadcasted_iota(jnp.int32, (row_count, LANES), 0)[:, :1]
    position = position_of(order_ref, 0, row_count) + stored
    valid = jnp.where(position < length_ref[0], 1.0, 0.0)
    dout = cot_ref[...].astype(f32) * valid
    dlow_ref[...] = dout.astype(bf16)
    out_acc[...] = mixed + small_ref[4:5]
    ds_acc[...] = jnp.zeros_like(ds_acc)
    for group in copies[1:]:
        for copy in group:
            copy.wait()
    chunk = 512

    def step(f, carry):
        cols = pl.ds(pl.multiple_of(f * chunk, chunk), chunk)
        hidden = mm(second_ref[...], w_i[:, cols]) + bias_ref[:, cols]
        squared = hidden * hidden
        bent = jnp.tanh(hidden * (gelu_coeff + gelu_coeff * cubic_term * squared))
        plus = 0.5 + 0.5 * bent
        active = (hidden * plus).astype(bf16)
        slope = plus + hidden * (plus * (1.0 - bent)) * (
            gelu_coeff + gelu_coeff * 3.0 * cubic_term * squared
        )
        out_acc[...] += mm(active, w_d[cols, :])
        dhid = (mm_nt(dlow_ref[...], w_d[cols, :]) * slope).astype(bf16)
        g_d[cols, :] = mm_tn(active, dlow_ref[...]).astype(bf16)
        g_i[:, cols] = mm(second_t[...], dhid).astype(bf16)
        bias_grad_ref[:, cols] = jnp.sum(dhid.astype(f32), axis=0, keepdims=True)
        ds_acc[...] += mm_nt(dhid, w_i[:, cols])
        return carry

    lax.fori_loop(0, ff // chunk, step, 0)

    def store(g, index_of, source, target):
        copy = pltpu.make_async_copy(source, target, sems.at[g * number + index_of])
        copy.start()
        return copy

    stores = []
    for side in range(2):
        here = core if side == 0 else 1 - core
        for parity in range(2):
            for k in range(halves):
                owner = lax.bitwise_xor(me, 2 * k + parity)
                at = (side * 2 + parity) * halves + k
                if side == 0:
                    to_in = (even_in, odd_in)[parity].at[k]
                    to_down = (even_down, odd_down)[parity].at[k]
                else:
                    to_in, to_down = sib_in.at[parity, k], sib_down.at[parity, k]
                at_rows = pl.ds(pl.multiple_of(owner * rows, 16), rows)
                stores.append(
                    store(
                        1,
                        at,
                        g_i.at[at_rows, pl.ds(pl.multiple_of(here * half_i, LANES), half_i)],
                        to_in.at[:, pl.ds(half_o, half_i)],
                    )
                )
                stores.append(
                    store(
                        2,
                        at,
                        g_d.at[
                            pl.ds(pl.multiple_of(owner * frows, 16), frows),
                            pl.ds(pl.multiple_of(here * half_d, LANES), half_d),
                        ],
                        to_down,
                    )
                )

    out_ref[...] = (out_acc[...] * valid).astype(bf16)
    ds = ds_acc[...]
    dmixed = dout + norm_back(ds * gain, unit, inverse)
    dmixed_ref[...] = dmixed
    dbranch = dmixed.astype(bf16)
    for d in range(GROUP):
        dattn = mm_nt(dbranch, w_o[out_rows(d), :])
        dattn_ref[d, pl.ds(0, row_count)] = dattn[:, :LANES].astype(bf16)
        half = row_count // 2
        dattn_ref[d, pl.ds(row_count, half), :64] = dattn[:half, LANES:].astype(bf16)
        dattn_ref[d, pl.ds(row_count, half), 64:] = dattn[half:, LANES:].astype(bf16)
    for d in range(GROUP):
        g_o[out_rows(d), :] = mm_tn(attn[d], dbranch).astype(bf16)
    for side in range(2):
        here = core if side == 0 else 1 - core
        for parity in range(2):
            for k in range(halves):
                owner = lax.bitwise_xor(me, 2 * k + parity)
                at = (side * 2 + parity) * halves + k
                if side == 0:
                    to_in = (even_in, odd_in)[parity].at[k]
                else:
                    to_in = sib_in.at[parity, k]
                stores.append(
                    store(
                        0,
                        at,
                        g_o.at[
                            pl.ds(pl.multiple_of(owner * rows, 16), rows),
                            pl.ds(pl.multiple_of(here * half_o, LANES), half_o),
                        ],
                        to_in.at[:, pl.ds(0, half_o)],
                    )
                )
    small_grad_ref[...] = jnp.zeros_like(small_grad_ref)
    small_grad_ref[2:3] = jnp.sum(ds * unit, axis=0, keepdims=True)
    small_grad_ref[3:4] = jnp.sum(ds, axis=0, keepdims=True)
    small_grad_ref[4:5] = jnp.sum(dout, axis=0, keepdims=True)
    for copy in stores:
        copy.wait()


def feed_forward(length, order, tokens, cotangent, attn, small, bias, in_pieces, down_pieces, ff):
    row_count, width = tokens.shape
    halves, rows, wide = in_pieces[0].shape
    frows, narrow = down_pieces[0].shape[1:]
    in_half = jax.ShapeDtypeStruct((halves, rows, wide), bf16)
    down_half = jax.ShapeDtypeStruct((halves, frows, narrow), bf16)
    return pl.pallas_call(
        ffn_kernel,
        out_shape=(
            jax.ShapeDtypeStruct((row_count, width), bf16),
            jax.ShapeDtypeStruct((row_count, width), f32),
            jax.ShapeDtypeStruct((GROUP, row_count * 3 // 2, LANES), bf16),
            in_half,
            in_half,
            jax.ShapeDtypeStruct((2, halves, rows, wide), bf16),
            down_half,
            down_half,
            jax.ShapeDtypeStruct((2, halves, frows, narrow), bf16),
            jax.ShapeDtypeStruct((16, width), f32),
            jax.ShapeDtypeStruct((1, ff), f32),
        ),
        in_specs=[whole(pltpu.SMEM)] * 2 + [whole()] * 8 + [whole(pl.ANY)] * 8,
        out_specs=[whole()] * 3 + [whole(pl.ANY)] * 6 + [whole()] * 2,
        scratch_shapes=[
            pltpu.VMEM((width, width), bf16),
            pltpu.VMEM((width, ff), bf16),
            pltpu.VMEM((ff, width), bf16),
            pltpu.VMEM((width, width), bf16),
            pltpu.VMEM((width, ff), bf16),
            pltpu.VMEM((ff, width), bf16),
            pltpu.VMEM((width, row_count), bf16),
            pltpu.VMEM((row_count, width), bf16),
            pltpu.VMEM((row_count, width), bf16),
            pltpu.VMEM((row_count, width), f32),
            pltpu.VMEM((row_count, width), f32),
            pltpu.SemaphoreType.DMA((12 * halves,)),
        ],
        compiler_params=pltpu.CompilerParams(vmem_limit_bytes=VMEM_BYTES),
        cost_estimate=pl.CostEstimate(
            flops=2 * row_count * width * (6 * ff + 4 * width),
            bytes_accessed=8 * width * ff + 8 * width * width,
            transcendentals=row_count * ff,
        ),
    )(length, order, tokens, cotangent, *attn, small, bias, *in_pieces, *down_pieces)


def attend_back_kernel(final, row_count, *refs):
    q_ref, k_ref, v_ref, near_attn, far_attn = refs[:5]
    dattn_refs = refs[5 : 5 + GROUP]
    outs = refs[5 + GROUP : -5]
    grad_ref, k_turned, dq_ref, dk_ref, dv_ref = refs[-5:]
    head, slot = pl.program_id(0), pl.program_id(1)
    total = k_ref.shape[1]
    chunk = row_count

    @pl.when((head == 0) & (slot == 0))
    def _():
        lane = lanes_of((row_count, LANES))
        for d in range(GROUP):
            packed = dattn_refs[d][...]
            attn = (near_attn if d < 2 else far_attn)[d % 2]
            top, tail = unpack_rows(packed.astype(f32), row_count)
            top_a, tail_a = unpack_rows(attn.astype(f32), row_count)
            product = top * top_a
            heads = (
                (top, jnp.sum(jnp.where(lane < 64, product, 0.0), axis=1, keepdims=True)),
                (
                    pltpu.roll(top, 64, 1),
                    jnp.sum(jnp.where(lane >= 64, product, 0.0), axis=1, keepdims=True),
                ),
                (
                    jnp.concatenate([tail, tail], axis=1),
                    jnp.sum(tail * tail_a, axis=1, keepdims=True),
                ),
            )
            for h, (block, delta) in enumerate(heads):
                base = jnp.where(lane < 64, block, 0.0)
                grad_ref[h, pl.ds(d * row_count, row_count)] = with_parts(base, -delta).astype(bf16)

    @pl.when(slot == 0)
    def _():
        k_turned[...] = k_ref[0].astype(f32).T.astype(bf16)
        dk_ref[...] = jnp.zeros_like(dk_ref)
        dv_ref[...] = jnp.zeros_like(dv_ref)

    query = q_ref[0]
    part = pl.ds(pl.multiple_of(slot * row_count, row_count), row_count)
    grad = grad_ref[head, part]
    turned = jnp.zeros((LANES, row_count), f32)
    for c in range(total // chunk):
        at = pl.ds(c * chunk, chunk)
        probs = jnp.exp(mm_nt(k_ref[0, at], query))
        dscores = (probs * mm_nt(v_ref[0, at], grad)).astype(bf16)
        dv_ref[at] += mm(probs.astype(bf16), grad)
        dk_ref[at] += mm(dscores, query)
        turned = turned + mm(k_turned[:, at], dscores)
    dq_ref[part] = turned.T * 0.125

    @pl.when(slot == GROUP - 1)
    def _():
        if final:
            one_ref, two_ref = outs
            lane = lanes_of(dq_ref.shape)
            one_ref[0] = jnp.where(
                lane < 64, dq_ref[...], pltpu.roll(dk_ref[...], 64, 1)
            ).astype(bf16)
            two_ref[0] = jnp.where(lane < 64, dv_ref[...], 0.0).astype(bf16)
        else:
            outs[0][0] = dq_ref[...]
            outs[1][0] = dk_ref[...]
            outs[2][0] = dv_ref[...]


def attend_back(query, keys, values, near_attn, far_attn, dattn, final):
    rows = query.shape[1]
    row_count = rows // GROUP
    total = keys.shape[1]

    def per_head(size, kind):
        return (
            jax.ShapeDtypeStruct((3, size, LANES), kind),
            pl.BlockSpec((1, size, LANES), lambda h, s: (h, 0, 0)),
        )

    if final:
        outs = [per_head(rows, bf16), per_head(rows, bf16)]
    else:
        outs = [per_head(rows, f32), per_head(total, f32), per_head(total, f32)]
    return pl.pallas_call(
        functools.partial(attend_back_kernel, final, row_count),
        grid=(3, GROUP),
        out_shape=[shape for shape, _ in outs],
        out_specs=[spec for _, spec in outs],
        in_specs=[
            pl.BlockSpec((1, row_count, LANES), lambda h, s: (h, s, 0)),
            pl.BlockSpec((1, total, LANES), lambda h, s: (h, 0, 0)),
            pl.BlockSpec((1, total, LANES), lambda h, s: (h, 0, 0)),
        ]
        + [whole()] * (2 + GROUP),
        scratch_shapes=[
            pltpu.VMEM((3, rows, LANES), bf16),
            pltpu.VMEM((LANES, total), bf16),
            pltpu.VMEM((rows, LANES), f32),
            pltpu.VMEM((total, LANES), f32),
            pltpu.VMEM((total, LANES), f32),
        ],
        compiler_params=pltpu.CompilerParams(vmem_limit_bytes=VMEM_BYTES),
        cost_estimate=pl.CostEstimate(
            flops=3 * rows * total * 64 * 2 * 5 * 4,
            bytes_accessed=3 * total * LANES * 12,
            transcendentals=3 * rows * total,
        ),
    )(query, keys, values, near_attn, far_attn, *dattn)


def tail_kernel(one_ref, two_ref, first_ref, w_ref, grads_ref, *refs):
    even_ref, odd_ref, keep_ref, send_ref, d_ref, g_ref, sems = refs
    total, width = first_ref.shape
    row_count = total // GROUP
    halves, rows, _ = even_ref.shape
    me = lax.axis_index("dp")
    for h in range(3):
        d_ref[:, h * LANES : (h + 1) * LANES] = one_ref[h]
    moved = pltpu.roll(two_ref[1].astype(f32), 64, 1).astype(bf16)
    d_ref[:, 384:512] = two_ref[0] + moved
    d_ref[:, 512:640] = two_ref[2]
    for d in range(GROUP):
        part = mm_nt(d_ref[d * row_count : (d + 1) * row_count], w_ref[...]).astype(bf16)
        (send_ref if d % 2 else keep_ref)[d // 2] = part
    weights = w_ref[...].astype(f32)
    grad = mm_tn(first_ref[...], d_ref[...])
    columns = jnp.sum(d_ref[...].astype(f32), axis=0, keepdims=True)
    gain, shift = weights[:, 576:577], weights[:, 577:578]
    gain_grad = jnp.sum(weights * (grad - shift * columns), axis=1, keepdims=True) / gain
    shift_grad = jnp.sum(weights * columns, axis=1, keepdims=True)
    g_ref[:, :512] = grad[:, :512].astype(bf16)
    lane = lanes_of((width, LANES))
    turned = jnp.concatenate(
        [jnp.zeros((64, width), f32), grads_ref[...], jnp.zeros((48, width), f32)], axis=0
    ).T
    last = jnp.where(lane < 64, grad[:, 512:640], turned)
    last = jnp.where(lane == 64, gain_grad, jnp.where(lane == 65, shift_grad, last))
    g_ref[:, 512:640] = last.astype(bf16)
    copies = []
    for parity in range(2):
        for k in range(halves):
            owner = lax.bitwise_xor(me, 2 * k + parity)
            copies.append(
                pltpu.make_async_copy(
                    g_ref.at[pl.ds(pl.multiple_of(owner * rows, 16), rows)],
                    (even_ref, odd_ref)[parity].at[k],
                    sems.at[2 * k + parity],
                )
            )
    for copy in copies:
        copy.start()
    for copy in copies:
        copy.wait()


def tail(one, two, first, weights, grads, halves):
    total, width = first.shape
    wide = weights.shape[1]
    rows = width // (2 * halves)
    piece = jax.ShapeDtypeStruct((halves, rows, wide), bf16)
    pair = jax.ShapeDtypeStruct((2, total // GROUP, width), bf16)
    return pl.pallas_call(
        tail_kernel,
        out_shape=(piece, piece, pair, pair),
        in_specs=[whole()] * 5,
        out_specs=[whole(pl.ANY)] * 2 + [whole()] * 2,
        scratch_shapes=[
            pltpu.VMEM((total, wide), bf16),
            pltpu.VMEM((width, wide), bf16),
            pltpu.SemaphoreType.DMA((2 * halves,)),
        ],
        compiler_params=pltpu.CompilerParams(vmem_limit_bytes=VMEM_BYTES),
        cost_estimate=pl.CostEstimate(
            flops=4 * total * width * wide, bytes_accessed=8 * total * width, transcendentals=0
        ),
    )(one, two, first, weights, grads)


def last_kernel(token_ref, one_ref, two_ref, three_ref, dmixed_ref, small_ref, out_ref):
    unit, inverse = norm_parts(token_ref[...].astype(f32))
    df = one_ref[...].astype(f32) + two_ref[...].astype(f32) + three_ref[...].astype(f32)
    back = norm_back(df * small_ref[0:1], unit, inverse)
    out_ref[...] = (dmixed_ref[...] + back).astype(bf16)


def last(tokens, one, two, three, dmixed, small):
    return pl.pallas_call(
        last_kernel,
        out_shape=jax.ShapeDtypeStruct(tokens.shape, bf16),
        in_specs=[whole()] * 6,
        out_specs=whole(),
        compiler_params=pltpu.CompilerParams(vmem_limit_bytes=VMEM_BYTES),
    )(tokens, one, two, three, dmixed, small)


def on_device(
    tokens,
    attn_gain,
    attn_shift,
    w_qkv,
    w_out,
    ffn_gain,
    ffn_shift,
    w_in,
    b_in,
    w_down,
    b_down,
    cotangent,
    lengths,
    block_order,
):
    mine = tokens[0]
    row_count, width = mine.shape
    ctx_size = lax.axis_size("ctx")
    dp_size = lax.axis_size("dp")
    index = lax.axis_index("ctx")
    low = lax.rem(index, GROUP)
    core = lax.rem(index, 2)
    far = ctx_size // GROUP
    rows = w_qkv.shape[0]
    ff = w_in.shape[1]
    per_row = b_in.shape[0] // rows
    assert math.gcd(H, ctx_size) == GROUP

    mine_qkv = lax.dynamic_index_in_dim(w_qkv.reshape(rows, 3, GROUP, 3, 64), low, 2, False)
    columns = [mine_qkv[:, 0, 0], mine_qkv[:, 1, 0], mine_qkv[:, 0, 1], mine_qkv[:, 1, 1]]
    columns += [mine_qkv[:, 0, 2], mine_qkv[:, 1, 2]]
    columns += [mine_qkv[:, 2, 0], mine_qkv[:, 2, 1], mine_qkv[:, 2, 2]]
    smalls = [attn_gain, attn_shift, ffn_gain, ffn_shift, b_down]
    columns += [v[:, None] for v in smalls] + [b_in.reshape(per_row, rows).T]
    columns.append(jnp.zeros((rows, 640 - 576 - 5 - per_row), bf16))
    qkv_piece = jnp.concatenate(columns, axis=1)
    near_qkv, cross_qkv = gather_dp(qkv_piece)

    side = swap(mine, "ctx", 1)
    over = swap(mine, "ctx", 2)
    blocks = [mine, side, over, swap(over, "ctx", 1)]

    half_out = lax.dynamic_slice_in_dim(w_out, core * (width // 2), width // 2, 1)
    half_in = lax.dynamic_slice_in_dim(w_in, core * (ff // 2), ff // 2, 1)
    half_down = lax.dynamic_slice_in_dim(w_down, core * (width // 2), width // 2, 1)
    in_pieces = gather_dp(jnp.concatenate([half_out, half_in], axis=1))
    down_pieces = gather_dp(half_down)
    in_pieces += tuple(swap(p, "ctx", 1) for p in in_pieces)
    down_pieces += tuple(swap(p, "ctx", 1) for p in down_pieces)

    query, keys, values, first, small, qkv_weight = project(
        lengths, block_order, blocks, near_qkv, cross_qkv
    )
    bias = small[5 : 5 + per_row].reshape(per_row, dp_size, rows).transpose(1, 0, 2).reshape(1, ff)
    if far > 1:
        groups = [[g * GROUP + i for g in range(far)] for i in range(GROUP)]
        keys = lax.all_gather(keys, "ctx", axis=1, tiled=True, axis_index_groups=groups)
        values = lax.all_gather(values, "ctx", axis=1, tiled=True, axis_index_groups=groups)
    far_attn, far_query = attend(query, keys, values, 2, 2, row_count)
    near_attn, near_query = attend(query, keys, values, 0, 2, row_count)
    attn = [
        near_attn[0],
        swap(near_attn[1], "ctx", 1),
        swap(far_attn[0], "ctx", 2),
        swap(far_attn[1], "ctx", 3),
    ]
    (
        layer_out,
        dmixed,
        dattn,
        even_in,
        odd_in,
        sib_in,
        even_down,
        odd_down,
        sib_down,
        small_grad,
        bias_grad,
    ) = feed_forward(
        lengths, block_order, mine, cotangent[0], attn, small, bias, in_pieces, down_pieces, ff
    )
    dattn = [dattn[0]] + [swap(dattn[d], "ctx", d) for d in range(1, GROUP)]

    def reduce_pair(even, odd, sib):
        received = swap(sib, "ctx", 1)
        even = (even.astype(f32) + received[0].astype(f32)).astype(bf16)
        odd = (odd.astype(f32) + received[1].astype(f32)).astype(bf16)
        return sum_far_ctx(scatter_dp(even, odd), 2).astype(bf16)

    def both_halves(half):
        other = swap(half, "ctx", 1)
        left = jnp.where(core == 0, half, other).astype(f32)
        right = jnp.where(core == 0, other, half).astype(f32)
        return left, right

    down_left, down_right = both_halves(reduce_pair(even_down, odd_down, sib_down))
    in_left, in_right = both_halves(reduce_pair(even_in, odd_in, sib_in))
    grad_w_down = jnp.concatenate([down_left, down_right], axis=1)
    cut = width // 2
    grad_w_out = jnp.concatenate([in_left[:, :cut], in_right[:, :cut]], axis=1)
    grad_w_in = jnp.concatenate([in_left[:, cut:], in_right[:, cut:]], axis=1)

    all_query = jnp.concatenate([near_query, far_query], axis=1)
    grads = attend_back(all_query, keys, values, near_attn, far_attn, dattn, far == 1)
    if far > 1:
        dq, dk, dv = grads
        dk, dv = (
            lax.psum_scatter(
                v, "ctx", scatter_dimension=1, tiled=True, axis_index_groups=groups
            )
            for v in (dk, dv)
        )
        one = jnp.concatenate([dq[..., :64], dk[..., :64]], axis=-1).astype(bf16)
        two = jnp.concatenate([dv[..., :64], jnp.zeros_like(dv[..., :64])], axis=-1).astype(bf16)
    else:
        one, two = grads
    bias_rows = bias_grad.reshape(dp_size, per_row, rows).transpose(1, 0, 2).reshape(per_row, width)
    small_grads = jnp.concatenate([small_grad[:5], bias_rows, small_grad[5 + per_row :]], axis=0)
    even, odd, keep, send = tail(one, two, first, qkv_weight, small_grads, dp_size // 2)
    back = swap(send[1], "ctx", 1)
    crossing = (keep[1].astype(f32) + back.astype(f32)).astype(bf16)
    near_back = swap(send[0], "ctx", 1)
    input_grad = last(mine, keep[0], near_back, swap(crossing, "ctx", 2), dmixed, small)

    share = sum_far_ctx(scatter_dp(even, odd), GROUP).astype(bf16)
    share_over = swap(share, "ctx", 2)
    shares = jnp.stack([share, swap(share, "ctx", 1), share_over, swap(share_over, "ctx", 1)])
    places = lax.bitwise_xor(low, jnp.arange(GROUP, dtype=jnp.int32))
    shares = jnp.take(shares, places, axis=0).astype(f32)
    heads = shares[:, :, :576].reshape(GROUP, rows, 9, 64)
    pick = [heads[:, :, [0, 2, 4]], heads[:, :, [1, 3, 5]], heads[:, :, [6, 7, 8]]]
    grad_w_qkv = jnp.stack(pick, axis=1).transpose(2, 1, 0, 3, 4).reshape(rows, 3 * width)
    small_sum = jnp.sum(shares[:, :, 576 : 581 + per_row], axis=0)
    small_list = [small_sum[:, i] for i in range(5)]
    grad_b_in = small_sum[:, 5:].T.reshape(-1)
    return (
        layer_out[None],
        input_grad[None],
        small_list[0],
        small_list[1],
        grad_w_qkv,
        grad_w_out,
        small_list[2],
        small_list[3],
        grad_w_in,
        grad_b_in,
        grad_w_down,
        small_list[4],
    )


def solution(mesh):
    placed = (
        P("dp", "ctx", None),
        P("dp"),
        P("dp"),
        P("dp", None),
        P("dp", None),
        P("dp"),
        P("dp"),
        P("dp", None),
        P("dp"),
        P("dp", None),
        P("dp"),
        P("dp", "ctx", None),
        P("dp"),
        P("dp", None),
    )
    return jax.shard_map(
        on_device,
        mesh=mesh,
        in_specs=placed,
        out_specs=(
            P("dp", "ctx", None),
            P("dp", "ctx", None),
            P("dp"),
            P("dp"),
            P("dp", None),
            P("dp", None),
            P("dp"),
            P("dp"),
            P("dp", None),
            P("dp"),
            P("dp", None),
            P("dp"),
        ),
        check_vma=False,
    )
```

```python
import functools
import math

import jax
import jax.numpy as jnp
from jax import lax
from jax.experimental import pallas as pl
from jax.experimental.pallas import tpu as pltpu
from jax.sharding import PartitionSpec as P

H = 12

epsilon = 1e-05
gelu_coeff = 0.7978845608
cubic_term = 0.044715
excluded = -1073741824.0
bf16 = jnp.bfloat16
f32 = jnp.float32
LANES = 128
GROUP = 4
VMEM_BYTES = 52 * 1024 * 1024

nt_dims = (((1,), (1,)), ((), ()))
tn_dims = (((0,), (0,)), ((), ()))


def mm(left, right):
    return jnp.dot(left, right, preferred_element_type=f32)


def mm_nt(left, right):
    return lax.dot_general(left, right, nt_dims, preferred_element_type=f32)


def mm_tn(left, right):
    return lax.dot_general(left, right, tn_dims, preferred_element_type=f32)


def whole(memory_space=pltpu.VMEM):
    return pl.BlockSpec(memory_space=memory_space)


def lanes_of(shape):
    return lax.broadcasted_iota(jnp.int32, shape, 1)


def norm_parts(values):
    center = values - jnp.mean(values, axis=-1, keepdims=True)
    spread = jnp.mean(center * center, axis=-1, keepdims=True)
    inverse = lax.rsqrt(spread + epsilon)
    return center * inverse, inverse


def norm_back(scaled, unit, inverse):
    return inverse * (
        scaled
        - jnp.mean(scaled, axis=-1, keepdims=True)
        - unit * jnp.mean(scaled * unit, axis=-1, keepdims=True)
    )


def three_parts(value):
    first = value.astype(bf16).astype(f32)
    rest = value - first
    second = rest.astype(bf16).astype(f32)
    return first, second, rest - second


def with_parts(base, value):
    lane = lanes_of(base.shape)
    one, two, three = three_parts(value)
    return jnp.where(
        lane == 64, one, jnp.where(lane == 65, two, jnp.where(lane == 66, three, base))
    )


def unpack_rows(packed, rows):
    tail = jnp.concatenate([packed[rows:, :64], packed[rows:, 64:]], axis=0)
    return packed[:rows], tail


def swap(value, axis, bit, name):
    size = lax.axis_size(axis)
    with jax.named_scope(name):
        return lax.ppermute(value, axis, [(i, i ^ bit) for i in range(size)])


def launch(kernel, gates, in_specs, cost=1.0, **options):
    count = len(gates)
    flops = int(cost * 1e9)

    def gated(*refs):
        kernel(*refs[count:])

    call = pl.pallas_call(
        gated,
        in_specs=[whole(pl.ANY)] * count + in_specs,
        compiler_params=pltpu.CompilerParams(vmem_limit_bytes=VMEM_BYTES),
        cost_estimate=pl.CostEstimate(flops=flops, bytes_accessed=1024, transcendentals=0),
        **options,
    )
    return lambda *operands: call(*gates, *operands)


def hold_kernel(value_ref, out_ref):
    pass


def after(value, *gates):
    return launch(
        hold_kernel,
        gates,
        [whole(pl.ANY)],
        out_shape=jax.ShapeDtypeStruct(value.shape, value.dtype),
        out_specs=whole(pl.ANY),
        input_output_aliases={len(gates): 0},
    )(value)


def far_pieces(piece, name):
    found = [piece]
    for k in range(1, lax.axis_size("dp") // 2):
        found.append(swap(piece, "dp", 2 * k, name + "_z"))
    return found


def add(left, right):
    return (left.astype(f32) + right.astype(f32)).astype(bf16)


def scatter_far(even, name):
    begun = None
    while even.shape[0] > 1:
        half = even.shape[0] // 2
        bit = lax.axis_size("dp") // (2 * half)
        pairs = even.reshape(half, 2, *even.shape[1:])
        even = add(pairs[:, 0], swap(pairs[:, 1], "dp", bit, name + "_z"))
        begun = even if begun is None else begun
    return begun, even[0]


def sum_groups(value):
    bit = GROUP
    while bit < lax.axis_size("ctx"):
        other = swap(value, "ctx", bit, "groups")
        value = (value.astype(f32) + other.astype(f32)).astype(bf16)
        bit *= 2
    return value


def gather_group(value, name):
    over = swap(value, "ctx", 2, name + "_x")
    side = swap(value, "ctx", 1, name + "_core")
    return [value, side, over, swap(over, "ctx", 1, name + "_pass")]


def exchange_group(values, name):
    names = ("", "_core", "_x", "_xcore")
    return [values[0]] + [swap(values[d], "ctx", d, name + names[d]) for d in range(1, GROUP)]


def position_of(order_ref, slot, rows):
    index = lax.axis_index("ctx")
    return order_ref[0, lax.bitwise_xor(index, slot)] * rows


def valid_rows(length_ref, order_ref, slot, row_count, offset, rows):
    stored = lax.broadcasted_iota(jnp.int32, (rows, LANES), 0)[:, :1]
    position = position_of(order_ref, slot, row_count) + offset + stored
    return jnp.where(position < length_ref[0], 1.0, 0.0)


def group_index():
    return lax.rem(lax.axis_index("ctx"), GROUP)


def load_pieces(sources, target, sems, first_sem=0):
    me = lax.axis_index("dp")
    copies = []
    for source, differences in sources:
        rows = source.shape[1]
        for k, difference in enumerate(differences):
            owner = lax.bitwise_xor(me, difference)
            copies.append(
                pltpu.make_async_copy(
                    source.at[k],
                    target.at[pl.ds(pl.multiple_of(owner * rows, 16), rows)],
                    sems.at[first_sem + len(copies)],
                )
            )
    for copy in copies:
        copy.start()
    return copies


def near_and_cross(near, cross):
    halves = near.shape[0]
    return [(near, [2 * k for k in range(halves)]), (cross, [2 * k + 1 for k in range(halves)])]


def store_pieces(source, even, odd, sems):
    halves, rows, _ = even.shape
    me = lax.axis_index("dp")
    copies = []
    for parity, target in ((0, even), (1, odd)):
        for k in range(halves):
            owner = lax.bitwise_xor(me, 2 * k + parity)
            copies.append(
                pltpu.make_async_copy(
                    source.at[pl.ds(pl.multiple_of(owner * rows, 16), rows)],
                    target.at[k],
                    sems.at[2 * k + parity],
                )
            )
    for copy in copies:
        copy.start()
    for copy in copies:
        copy.wait()


def pack_kernel(w_hbm, *refs):
    w_ref, sems = refs[-2:]
    count = (len(refs) - 3) // 2
    vectors, out_ref, held = refs[:count], refs[count], refs[count + 1 : -2]
    copies = [pltpu.make_async_copy(w_hbm, w_ref, sems.at[count])]
    for i in range(count):
        copies.append(pltpu.make_async_copy(vectors[i], held[i], sems.at[i]))
    for copy in copies:
        copy.start()
    for copy in copies:
        copy.wait()
    rows = w_ref.shape[0]
    width = w_ref.shape[1] // 3
    low = group_index()
    stacked = [v[...].astype(f32) for v in held]
    used = sum(v.shape[0] for v in stacked)
    stacked.append(jnp.zeros((LANES - used, rows), f32))
    small = jnp.concatenate(stacked, axis=0).T[:, :64].astype(bf16)
    for case in range(GROUP):

        @pl.when(low == case)
        def _():
            def head(kind, h):
                at = kind * width + 192 * case + 64 * h
                return w_ref[:, at : at + 64]

            out_ref[...] = jnp.concatenate(
                [
                    head(0, 0),
                    head(1, 0),
                    head(0, 1),
                    head(1, 1),
                    head(2, 0),
                    head(2, 1),
                    head(0, 2),
                    head(1, 2),
                    head(2, 2),
                    small,
                ],
                axis=1,
            )


def pack(w_qkv, vectors, gates=()):
    rows = w_qkv.shape[0]
    return launch(
        pack_kernel,
        gates,
        cost=1.0,
        out_shape=jax.ShapeDtypeStruct((rows, 640), bf16),
        in_specs=[whole(pl.ANY)] * (1 + len(vectors)),
        out_specs=whole(),
        scratch_shapes=[pltpu.VMEM(v.shape, bf16) for v in vectors]
        + [pltpu.VMEM(w_qkv.shape, bf16), pltpu.SemaphoreType.DMA((1 + len(vectors),))],
    )(w_qkv, *vectors)


def pack_ffn_kernel(out_ref, in_ref, down_ref, one_ref, two_ref):
    rows, ff = in_ref.shape
    width = out_ref.shape[1]
    half = width // 2
    low = group_index()
    per = 4 * rows
    for case in range(GROUP):

        @pl.when(low == case)
        def _():
            at = half * (case % 2)
            parts = [
                in_ref[:, per * i + rows * case : per * i + rows * (case + 1)]
                for i in range(ff // per)
            ]
            one_ref[:, :width] = jnp.concatenate(parts, axis=1)
            one_ref[:, width:] = out_ref[:, at : at + half]
            two_ref[...] = down_ref[rows * case : rows * (case + 1)]


def pack_ffn(w_out, w_in, w_down, gates=()):
    rows, width = w_out.shape
    return launch(
        pack_ffn_kernel,
        gates,
        cost=1.0,
        out_shape=(
            jax.ShapeDtypeStruct((rows, width + width // 2), bf16),
            jax.ShapeDtypeStruct((rows, width), bf16),
        ),
        in_specs=[whole()] * 3,
        out_specs=[whole()] * 2,
    )(w_out, w_in, w_down)


def qkv_kernel(length_ref, order_ref, *refs):
    tokens = refs[:GROUP]
    near, cross = refs[GROUP : GROUP + 2]
    q_ref, k_ref, v_ref, first_ref, small_ref, w_ref, sems = refs[GROUP + 2 :]
    row_count, width = tokens[0].shape
    for copy in load_pieces(near_and_cross(near, cross), w_ref, sems):
        copy.wait()
    small = w_ref[:, 512:640].astype(f32).T
    small_ref[...] = small[64:80]
    gain, shift = small[64:65], small[65:66]
    length = length_ref[0]
    lane = lanes_of((row_count, LANES))
    ones = jnp.where((lane >= 64) & (lane < 67), 1.0, 0.0)
    bias_lane = jnp.where(lane == 67, 1.0, 0.0)
    for d in range(GROUP):
        unit, _ = norm_parts(tokens[d][...].astype(f32))
        first = (unit * gain + shift).astype(bf16)
        part = pl.ds(d * row_count, row_count)
        first_ref[part] = first
        qkv = mm(first, w_ref[...]).astype(bf16).astype(f32)

        def head(place):
            block = qkv[:, place // 2 * LANES : (place // 2 + 1) * LANES]
            if place % 2:
                block = pltpu.roll(block, 64, 1)
            return jnp.where(lane < 64, block, 0.0)

        stored = lax.broadcasted_iota(jnp.int32, (row_count, LANES), 0)
        position = position_of(order_ref, d, row_count) + stored
        bias = jnp.where(position < length, 0.0, excluded) * bias_lane
        for h, (at_q, at_k, at_v) in enumerate(((0, 1, 4), (2, 3, 5), (6, 7, 8))):
            q_ref[h, part] = (head(at_q) * 0.125 + bias_lane).astype(bf16)
            k_ref[h, part] = (head(at_k) + ones + bias).astype(bf16)
            v_ref[h, part] = (head(at_v) + ones).astype(bf16)


def project(length, order, tokens, near, cross, gates=()):
    row_count, width = tokens[0].shape
    total = GROUP * row_count
    wide = near.shape[2]
    head_out = jax.ShapeDtypeStruct((3, total, LANES), bf16)
    return launch(
        qkv_kernel,
        gates,
        cost=10.0,
        out_shape=(
            head_out,
            head_out,
            head_out,
            jax.ShapeDtypeStruct((total, width), bf16),
            jax.ShapeDtypeStruct((16, width), f32),
            jax.ShapeDtypeStruct((width, wide), bf16),
        ),
        in_specs=[whole(pltpu.SMEM)] * 2 + [whole()] * GROUP + [whole(pl.ANY)] * 2,
        out_specs=[whole()] * 6,
        scratch_shapes=[pltpu.SemaphoreType.DMA((2 * near.shape[0],))],
    )(length, order, *tokens, near, cross)


def attend_kernel(block_rows, q_ref, k_ref, v_ref, packed_ref, q_out_ref):
    row_count = q_ref.shape[1]
    half = row_count // 2
    lane = lanes_of((block_rows, LANES))
    for i in range(row_count // block_rows):
        part = pl.ds(i * block_rows, block_rows)
        heads = []
        for h in range(3):
            query = q_ref[h, part]
            scores = mm_nt(query, k_ref[h])
            top = jnp.max(scores, axis=1, keepdims=True)
            weights = jnp.exp(scores - top).astype(bf16)
            result = mm(weights, v_ref[h])
            denom = result[:, 64:65]
            heads.append(jnp.where(lane < 64, result / denom, 0.0))
            log_total = top + jnp.log(denom)
            q_out_ref[h, part] = with_parts(query.astype(f32), -log_total).astype(bf16)
        packed_ref[0, part] = (heads[0] + pltpu.roll(heads[1], 64, 1)).astype(bf16)
        for r in range(0, block_rows, half):
            size = min(half, block_rows)
            row = i * block_rows + r
            side, place = row // half, row % half
            packed_ref[
                0, pl.ds(row_count + place, size), 64 * side : 64 * side + 64
            ] = heads[2][r : r + size, :64].astype(bf16)


def attend(query, keys, values, first_slot, slots, row_count, gates=()):
    total = keys.shape[1]
    block_rows = min(row_count // 2, 256)
    return launch(
        functools.partial(attend_kernel, block_rows),
        gates,
        cost=7.0 * slots,
        grid=(slots,),
        out_shape=(
            jax.ShapeDtypeStruct((slots, row_count * 3 // 2, LANES), bf16),
            jax.ShapeDtypeStruct((3, slots * row_count, LANES), bf16),
        ),
        in_specs=[
            pl.BlockSpec((3, row_count, LANES), lambda s: (0, s + first_slot, 0)),
            whole(),
            whole(),
        ],
        out_specs=(
            pl.BlockSpec((1, row_count * 3 // 2, LANES), lambda s: (s, 0, 0)),
            pl.BlockSpec((3, row_count, LANES), lambda s: (0, s, 0)),
        ),
    )(query, keys, values)


def out_kernel(token_ref, *refs):
    attn_refs, pieces = refs[:GROUP], refs[GROUP : GROUP + 2]
    small_ref, mixed_ref, second_ref, w_o, sems = refs[GROUP + 2 :]
    row_count, width = token_ref.shape
    half = width // 2
    number = pieces[0].shape[0]
    low = group_index()
    core = lax.rem(low, 2)
    differences = [2 * k for k in range(number // 2)] + [2 * k + 1 for k in range(number // 2)]
    copies = []
    for side in range(2):
        column = pl.multiple_of((core if side == 0 else 1 - core) * half, LANES)
        target = w_o.at[:, pl.ds(column, half)]
        copies += load_pieces([(pieces[side], differences)], target, sems, side * number)
    mixed = token_ref[...].astype(f32)
    for copy in copies:
        copy.wait()
    for d in range(GROUP):
        attn = jnp.concatenate(unpack_rows(attn_refs[d][...], row_count), axis=1)
        at = pl.ds(pl.multiple_of(lax.bitwise_xor(low, d) * 192, 16), 192)
        mixed = mixed + mm(attn, w_o[at, :])
    mixed_ref[...] = mixed
    unit, _ = norm_parts(mixed)
    second_ref[...] = (unit * small_ref[2:3] + small_ref[3:4]).astype(bf16)


def project_out(tokens, attn, pieces, small, gates=()):
    row_count, width = tokens.shape
    number = pieces[0].shape[0]
    return launch(
        out_kernel,
        gates,
        cost=4.5,
        out_shape=(
            jax.ShapeDtypeStruct((row_count, width), f32),
            jax.ShapeDtypeStruct((row_count, width), bf16),
            jax.ShapeDtypeStruct((width, width), bf16),
        ),
        in_specs=[whole()] * (1 + GROUP)
        + [whole(pl.ANY)] * 2
        + [whole()],
        out_specs=[whole()] * 3,
        scratch_shapes=[pltpu.SemaphoreType.DMA((2 * number,))],
    )(tokens, *attn, *pieces, small)


def ffn_kernel(slots, offset, gathers, length_ref, order_ref, small_ref, *refs):
    number = len(slots)
    seconds, cots = refs[:number], refs[number : 2 * number]
    refs = refs[2 * number :]
    count = 2 + gathers if gathers else 2
    sources, refs = refs[:count], refs[count:]
    outs = [refs[4 * i : 4 + 4 * i] for i in range(number)]
    refs = refs[4 * number :]
    rows, width = seconds[0].shape
    if gathers:
        w_i, w_d, sems = refs
        near, cross, *downs = sources
        parts = near_and_cross(*(v.at[:, :, pl.ds(0, width)] for v in (near, cross)))
        copies = load_pieces(parts, w_i, sems)
        pairs = [(pair, (2 * k, 2 * k + 1)) for k, pair in enumerate(downs)]
        copies += load_pieces(pairs, w_d, sems, 2 * gathers)
        for copy in copies:
            copy.wait()
    else:
        w_i, w_d = sources
    bias = small_ref[pl.ds(5 + group_index(), 1)]
    for i, slot in enumerate(slots):
        ds_ref, out_ref, active_ref, dhid_ref = outs[i]
        row_count = cots[i].shape[0]
        valid = valid_rows(length_ref, order_ref, slot, row_count, offset, rows)
        dlow = (cots[i][offset : offset + rows].astype(f32) * valid).astype(bf16)
        hidden = mm(seconds[i][...], w_i[...]) + bias
        squared = hidden * hidden
        bent = jnp.tanh(hidden * (gelu_coeff + gelu_coeff * cubic_term * squared))
        plus = 0.5 + 0.5 * bent
        active = (hidden * plus).astype(bf16)
        slope = plus + hidden * (plus * (1.0 - bent)) * (
            gelu_coeff + gelu_coeff * 3.0 * cubic_term * squared
        )
        active_ref[...] = active
        dhid = (mm_nt(dlow, w_d[...]) * slope).astype(bf16)
        dhid_ref[...] = dhid
        ds_ref[...] = mm_nt(dhid, w_i[...]).astype(bf16)
        out_ref[...] = mm(active, w_d[...]).astype(bf16)


def feed_forward(length, order, small, seconds, cots, weights, slots, offset, gates=()):
    rows, width = seconds[0].shape
    gathers = len(weights) - 2
    number = len(slots)
    block = jax.ShapeDtypeStruct((rows, width), bf16)
    square = jax.ShapeDtypeStruct((width, width), bf16)
    results = launch(
        functools.partial(ffn_kernel, slots, offset, gathers),
        gates,
        cost=10.0 * rows / 512,
        out_shape=[block] * (4 * number) + [square] * (2 if gathers else 0),
        in_specs=[whole(pltpu.SMEM)] * 2
        + [whole()] * (1 + 2 * number)
        + [whole(pl.ANY) if gathers else whole()] * len(weights),
        out_specs=[whole()] * (4 * number + (2 if gathers else 0)),
        scratch_shapes=[pltpu.SemaphoreType.DMA((4 * gathers,))] if gathers else [],
    )(length, order, small, *seconds, *cots, *weights)
    grouped = [results[4 * i : 4 * i + 4] for i in range(number)]
    return grouped, results[4 * number :]


def ffn_grad_kernel(blocks, length_ref, order_ref, *refs):
    number = len(blocks)
    cots = refs[:GROUP]
    refs = refs[GROUP:]
    seconds, actives, dhids = refs[:number], refs[number : 2 * number], refs[2 * number : 3 * number]
    even, odd, bias_ref, g_ref, sems = refs[3 * number :]
    row_count, width = cots[0].shape
    total = GROUP * row_count
    bias = jnp.zeros((1, width), f32)
    grad_in = jnp.zeros((width, width), f32)
    for i in range(number):
        dhid = dhids[i][...]
        bias = bias + jnp.sum(dhid.astype(f32), axis=0, keepdims=True)
        grad_in = grad_in + mm_tn(seconds[i][...], dhid)
    g_ref[:, :width] = grad_in.astype(bf16)
    bias_ref[...] = bias
    grad_down = jnp.zeros((width, width), f32)
    for i, (slot, offset) in enumerate(blocks):
        rows = actives[i].shape[0]
        valid = valid_rows(length_ref, order_ref, slot, row_count, offset, rows)
        dlow = (cots[slot][offset : offset + rows].astype(f32) * valid).astype(bf16)
        grad_down = grad_down + mm_tn(actives[i][...], dlow)
    g_ref[:, width:] = grad_down.astype(bf16)
    store_pieces(g_ref, even, odd, sems)


def ffn_grads(length, order, cots, seconds, actives, dhids, blocks, dp_size, gates=()):
    row_count, width = cots[0].shape
    halves = dp_size // 2
    piece = jax.ShapeDtypeStruct((halves, width // dp_size, 2 * width), bf16)
    number = len(blocks)
    return launch(
        functools.partial(ffn_grad_kernel, blocks),
        gates,
        cost=11.0,
        out_shape=(piece, piece, jax.ShapeDtypeStruct((1, width), f32)),
        in_specs=[whole(pltpu.SMEM)] * 2 + [whole()] * (GROUP + 3 * number),
        out_specs=[whole(pl.ANY)] * 2 + [whole()],
        scratch_shapes=[
            pltpu.VMEM((width, 2 * width), bf16),
            pltpu.SemaphoreType.DMA((dp_size,)),
        ],
    )(length, order, *cots, *seconds, *actives, *dhids)


def mixed_back_kernel(length_ref, order_ref, *refs):
    mixed_ref, cot_ref, small_ref, w_o = refs[:4]
    attn_refs = refs[4 : 4 + GROUP]
    ds_own, ds_side, ds_over_one, ds_over_two = refs[8:12]
    dmixed_ref, small_grad_ref = refs[12:14]
    dattn_refs = refs[14 : 14 + GROUP]
    block_refs = refs[18 : 18 + GROUP]
    g_o = refs[22]
    row_count, width = mixed_ref.shape
    half = row_count // 2
    low = group_index()
    unit, inverse = norm_parts(mixed_ref[...])
    over = jnp.concatenate([ds_over_one[...], ds_over_two[...]], axis=0).astype(f32)
    ds = ds_own[...].astype(f32) + ds_side[...].astype(f32) + over
    valid = valid_rows(length_ref, order_ref, 0, row_count, 0, row_count)
    dout = cot_ref[...].astype(f32) * valid
    dmixed = dout + norm_back(ds * small_ref[2:3], unit, inverse)
    dmixed_ref[...] = dmixed
    dbranch = dmixed.astype(bf16)

    def out_rows(d):
        return pl.ds(pl.multiple_of(lax.bitwise_xor(low, d) * 192, 16), 192)

    for d in range(GROUP):
        dattn = mm_nt(dbranch, w_o[out_rows(d), :])
        dattn_refs[d][:row_count] = dattn[:, :LANES].astype(bf16)
        dattn_refs[d][row_count:, :64] = dattn[:half, LANES:].astype(bf16)
        dattn_refs[d][row_count:, 64:] = dattn[half:, LANES:].astype(bf16)
    g_o[:, width:] = jnp.zeros((width, 1024 - width), bf16)
    for d in range(GROUP):
        attn = jnp.concatenate(unpack_rows(attn_refs[d][...], row_count), axis=1)
        g_o[out_rows(d), :width] = mm_tn(attn, dbranch).astype(bf16)
    for d in range(GROUP):
        column = pl.multiple_of(lax.bitwise_xor(low, d) * 256, LANES)
        block_refs[d][...] = g_o[:, pl.ds(column, 256)]
    small_grad_ref[...] = jnp.zeros_like(small_grad_ref)
    small_grad_ref[2:3] = jnp.sum(ds * unit, axis=0, keepdims=True)
    small_grad_ref[3:4] = jnp.sum(ds, axis=0, keepdims=True)
    small_grad_ref[4:5] = jnp.sum(dout, axis=0, keepdims=True)


def mixed_back(length, order, mixed, cot, small, w_o, attn, ds, gates=()):
    row_count, width = mixed.shape
    results = launch(
        mixed_back_kernel,
        gates,
        cost=7.0,
        out_shape=[
            jax.ShapeDtypeStruct((row_count, width), f32),
            jax.ShapeDtypeStruct((16, width), f32),
        ]
        + [jax.ShapeDtypeStruct((row_count * 3 // 2, LANES), bf16)] * GROUP
        + [jax.ShapeDtypeStruct((width, 256), bf16)] * GROUP,
        in_specs=[whole(pltpu.SMEM)] * 2 + [whole()] * 12,
        out_specs=[whole()] * 10,
        scratch_shapes=[pltpu.VMEM((width, 1024), bf16)],
    )(length, order, mixed, cot, small, w_o, *attn, *ds)
    return results[0], results[1], results[2:6], results[6:10]


def layer_out_kernel(length_ref, order_ref, mixed_ref, small_ref, *refs):
    own, side, over, out_ref = refs
    row_count = mixed_ref.shape[0]
    valid = valid_rows(length_ref, order_ref, 0, row_count, 0, row_count)
    total = mixed_ref[...] + own[...].astype(f32) + side[...].astype(f32) + over[...].astype(f32)
    out_ref[...] = ((total + small_ref[4:5]) * valid).astype(bf16)


def finish_out(length, order, mixed, small, parts, gates=()):
    return launch(
        layer_out_kernel,
        gates,
        cost=3.0,
        out_shape=jax.ShapeDtypeStruct(mixed.shape, bf16),
        in_specs=[whole(pltpu.SMEM)] * 2 + [whole()] * 5,
        out_specs=whole(),
    )(length, order, mixed, small, *parts)


def attend_back_kernel(mode, heads, slots, row_count, starts, *refs):
    q_ref, k_ref, v_ref = refs[:3]
    number = len(slots)
    attn_refs, dattn_refs = refs[3 : 3 + number], refs[3 + number : 3 + 2 * number]
    refs = refs[3 + 2 * number :]
    if starts:
        dk_in, dv_in, dq_in = refs[:3]
        refs = refs[3:]
    outs = refs[:-5]
    grad_ref, k_turned, dq_ref, dk_ref, dv_ref = refs[-5:]
    head, step = pl.program_id(0), pl.program_id(1)
    total = k_ref.shape[1]
    chunk = row_count
    first_slot = slots[0] if mode == "final" else 0

    @pl.when((head == 0) & (step == 0))
    def _():
        lane = lanes_of((row_count, LANES))
        for d in range(number):
            top, tail = unpack_rows(dattn_refs[d][...].astype(f32), row_count)
            top_a, tail_a = unpack_rows(attn_refs[d][...].astype(f32), row_count)
            product = top * top_a
            for i, h in enumerate(heads):
                if h == 0:
                    block = top
                    delta = jnp.sum(jnp.where(lane < 64, product, 0.0), axis=1, keepdims=True)
                elif h == 1:
                    block = pltpu.roll(top, 64, 1)
                    delta = jnp.sum(jnp.where(lane >= 64, product, 0.0), axis=1, keepdims=True)
                else:
                    block = jnp.concatenate([tail, tail], axis=1)
                    delta = jnp.sum(tail * tail_a, axis=1, keepdims=True)
                base = jnp.where(lane < 64, block, 0.0)
                grad_ref[i, pl.ds(d * row_count, row_count)] = with_parts(base, -delta).astype(bf16)

    @pl.when(step == 0)
    def _():
        k_turned[...] = k_ref[0].astype(f32).T.astype(bf16)
        if starts:
            dk_ref[...] = dk_in[0]
            dv_ref[...] = dv_in[0]
            dq_ref[: first_slot * row_count] = dq_in[0]
        else:
            dk_ref[...] = jnp.zeros_like(dk_ref)
            dv_ref[...] = jnp.zeros_like(dv_ref)

    query = q_ref[0]
    grad = grad_ref[head, pl.ds(pl.multiple_of(step * row_count, row_count), row_count)]
    turned = jnp.zeros((LANES, row_count), f32)
    for c in range(total // chunk):
        at = pl.ds(c * chunk, chunk)
        probs = jnp.exp(mm_nt(k_ref[0, at], query))
        dscores = (probs * mm_nt(v_ref[0, at], grad)).astype(bf16)
        dv_ref[at] += mm(probs.astype(bf16), grad)
        dk_ref[at] += mm(dscores, query)
        turned = turned + mm(k_turned[:, at], dscores)
    place = pl.multiple_of((first_slot + step) * row_count, row_count)
    dq_ref[pl.ds(place, row_count)] = turned.T * 0.125

    @pl.when(step == number - 1)
    def _():
        if mode != "final":
            outs[0][0] = dk_ref[...]
            outs[1][0] = dv_ref[...]
            outs[2][0] = dq_ref[...]
            return
        lane = lanes_of((row_count, LANES))
        last_at = LANES * len(heads)
        for i in range(len(heads)):

            @pl.when(head == i)
            def _():
                for d in range(GROUP):
                    at = pl.ds(d * row_count, row_count)
                    pair = jnp.where(lane < 64, dq_ref[at], pltpu.roll(dk_ref[at], 64, 1))
                    outs[d][:, i * LANES : (i + 1) * LANES] = pair.astype(bf16)
                    value = dv_ref[at]
                    if i == 0:
                        value = jnp.where(lane < 64, value, 0.0)
                        outs[d][:, last_at : last_at + LANES] = value.astype(bf16)
                    else:
                        outs[d][:, last_at + 64 : last_at + LANES] = value[:, :64].astype(bf16)


def attend_back(query, keys, values, attn, dattn, heads, slots, mode, begun, gates=()):
    row_count = attn[0].shape[0] * 2 // 3
    total = keys.shape[1]
    number = len(slots)
    kept = GROUP if mode == "final" else number
    first_head = heads[0]
    query_head = first_head if query.shape[0] == 3 else 0

    def per_head(size):
        return (
            jax.ShapeDtypeStruct((len(heads), size, LANES), f32),
            pl.BlockSpec((1, size, LANES), lambda h, s: (h, 0, 0)),
        )

    if mode == "final":
        wide = LANES * (len(heads) + 1)
        outs = [
            (
                jax.ShapeDtypeStruct((row_count, wide), bf16),
                pl.BlockSpec((row_count, wide), lambda h, s: (0, 0)),
            )
        ] * GROUP
    else:
        outs = [per_head(total), per_head(total), per_head(number * row_count)]
    begun_specs = []
    if begun:
        begun_specs = [
            pl.BlockSpec((1, v.shape[1], LANES), lambda h, s: (h, 0, 0)) for v in begun
        ]
    return launch(
        functools.partial(attend_back_kernel, mode, heads, slots, row_count, bool(begun)),
        gates,
        cost=3.8 * number * len(heads),
        grid=(len(heads), number),
        out_shape=[shape for shape, _ in outs],
        out_specs=[spec for _, spec in outs],
        in_specs=[
            pl.BlockSpec((1, row_count, LANES), lambda h, s: (h + query_head, s, 0)),
            pl.BlockSpec((1, total, LANES), lambda h, s: (h + first_head, 0, 0)),
            pl.BlockSpec((1, total, LANES), lambda h, s: (h + first_head, 0, 0)),
        ]
        + [whole()] * (2 * number)
        + begun_specs,
        scratch_shapes=[
            pltpu.VMEM((len(heads), number * row_count, LANES), bf16),
            pltpu.VMEM((LANES, total), bf16),
            pltpu.VMEM((kept * row_count, LANES), f32),
            pltpu.VMEM((total, LANES), f32),
            pltpu.VMEM((total, LANES), f32),
        ],
    )(query, keys, values, *attn, *dattn, *begun)


def first_grad_kernel(*refs):
    parts, first_ref, w_ref, block_ref = refs[:4], refs[4], refs[5], refs[6]
    even, odd, side_ref, d_ref, g_ref, sems = refs[7:]
    row_count, wide = parts[0].shape
    for d in range(GROUP):
        d_ref[d * row_count : (d + 1) * row_count] = parts[d][...]
    weights = w_ref[...].astype(f32)
    grad = mm_tn(first_ref[...], d_ref[...])
    g_ref[:, :wide] = grad.astype(bf16)
    columns = jnp.sum(d_ref[...].astype(f32), axis=0, keepdims=True)
    shift = weights[:, 577:578]
    used = weights[:, :wide]
    gain_part = jnp.sum(used * (grad - shift * columns), axis=1, keepdims=True)
    shift_part = jnp.sum(used * columns, axis=1, keepdims=True)
    lane = lanes_of(side_ref.shape)
    side_ref[...] = jnp.where(lane == 64, gain_part, jnp.where(lane == 65, shift_part, 0.0))
    g_ref[:, wide:] = block_ref[...]
    store_pieces(g_ref, even, odd, sems)


def first_grad(parts, first, weights, block, dp_size, gates=()):
    total, width = first.shape
    wide = parts[0].shape[1]
    piece = jax.ShapeDtypeStruct((dp_size // 2, width // dp_size, wide + 256), bf16)
    return launch(
        first_grad_kernel,
        gates,
        cost=5.0,
        out_shape=(piece, piece, jax.ShapeDtypeStruct((width, LANES), f32)),
        in_specs=[whole()] * 7,
        out_specs=[whole(pl.ANY)] * 2 + [whole()],
        scratch_shapes=[
            pltpu.VMEM((total, wide), bf16),
            pltpu.VMEM((width, wide + 256), bf16),
            pltpu.SemaphoreType.DMA((dp_size,)),
        ],
    )(*parts, first, weights, block)


def second_grad_kernel(*refs):
    parts = refs[:4]
    first_ref, w_ref, side_ref, small_grad_ref, bias_grad_ref = refs[4:9]
    even, odd, d_ref, g_ref, turn_ref, sems = refs[9:]
    row_count, wide = parts[0].shape
    width = first_ref.shape[1]
    for d in range(GROUP):
        d_ref[d * row_count : (d + 1) * row_count] = parts[d][...]
    weights = w_ref[...].astype(f32)
    grad = mm_tn(first_ref[...], d_ref[...])
    columns = jnp.sum(d_ref[...].astype(f32), axis=0, keepdims=True)
    gain, shift = weights[:, 576:577], weights[:, 577:578]
    used = weights[:, 640 - wide :]
    gain_part = jnp.sum(used * (grad - shift * columns), axis=1, keepdims=True)
    shift_part = jnp.sum(used * columns, axis=1, keepdims=True)
    gain_part = (gain_part + side_ref[:, 64:65]) / gain
    shift_part = shift_part + side_ref[:, 65:66]
    turn_ref[...] = jnp.zeros_like(turn_ref)
    turn_ref[64:80] = small_grad_ref[...]
    turn_ref[pl.ds(69 + group_index(), 1)] = bias_grad_ref[...]
    lane = lanes_of((width, LANES))
    last = jnp.where(lane < 64, grad[:, wide - LANES :], turn_ref[...].T)
    last = jnp.where(lane == 64, gain_part, jnp.where(lane == 65, shift_part, last))
    g_ref[:, : wide - LANES] = grad[:, : wide - LANES].astype(bf16)
    g_ref[:, wide - LANES :] = last.astype(bf16)
    store_pieces(g_ref, even, odd, sems)


def second_grad(parts, first, weights, side, small_grad, bias_grad, dp_size, gates=()):
    total, width = first.shape
    wide = parts[0].shape[1]
    piece = jax.ShapeDtypeStruct((dp_size // 2, width // dp_size, wide), bf16)
    return launch(
        second_grad_kernel,
        gates,
        cost=5.0,
        out_shape=(piece, piece),
        in_specs=[whole()] * 9,
        out_specs=[whole(pl.ANY)] * 2,
        scratch_shapes=[
            pltpu.VMEM((total, wide), bf16),
            pltpu.VMEM((width, wide), bf16),
            pltpu.VMEM((LANES, width), f32),
            pltpu.SemaphoreType.DMA((dp_size,)),
        ],
    )(*parts, first, weights, side, small_grad, bias_grad)


def part_kernel(*refs):
    ones, twos, weights = refs[:4], refs[4:8], refs[8][...]
    cut = ones[0].shape[1]
    for d in range(GROUP):
        part = mm_nt(ones[d][...], weights[:, :cut]) + mm_nt(twos[d][...], weights[:, cut:])
        refs[9 + d][...] = part.astype(bf16)


def input_parts(ones, twos, weights, gates=()):
    row_count, width = ones[0].shape[0], weights.shape[0]
    return launch(
        part_kernel,
        gates,
        cost=5.0,
        out_shape=[jax.ShapeDtypeStruct((row_count, width), bf16)] * GROUP,
        in_specs=[whole()] * 9,
        out_specs=[whole()] * GROUP,
    )(*ones, *twos, weights)


def last_kernel(token_ref, one_ref, two_ref, three_ref, dmixed_ref, small_ref, out_ref):
    unit, inverse = norm_parts(token_ref[...].astype(f32))
    df = one_ref[...].astype(f32) + two_ref[...].astype(f32) + three_ref[...].astype(f32)
    back = norm_back(df * small_ref[0:1], unit, inverse)
    out_ref[...] = (dmixed_ref[...] + back).astype(bf16)


def finish_input(tokens, parts, dmixed, small, gates=()):
    return launch(
        last_kernel,
        gates,
        cost=4.0,
        out_shape=jax.ShapeDtypeStruct(tokens.shape, bf16),
        in_specs=[whole()] * 6,
        out_specs=whole(),
    )(tokens, *parts, dmixed, small)


def place_ffn_kernel(*refs):
    shares, in_ref, down_ref = refs[:4], refs[4], refs[5]
    rows, ff = in_ref.shape
    width = down_ref.shape[1]
    low = group_index()
    for case in range(GROUP):

        @pl.when(low == case)
        def _():
            for d in range(GROUP):
                whose = case ^ d
                down_ref[rows * whose : rows * (whose + 1)] = shares[d][:, width:].astype(f32)
                part = shares[d][:, :width].astype(f32)
                for i in range(width // rows):
                    at = 4 * rows * i + rows * whose
                    in_ref[:, at : at + rows] = part[:, rows * i : rows * (i + 1)]


def place_ffn(shares, gates=()):
    rows, wide = shares[0].shape
    width = wide // 2
    return launch(
        place_ffn_kernel,
        gates,
        cost=3.0,
        out_shape=(
            jax.ShapeDtypeStruct((rows, 4 * width), f32),
            jax.ShapeDtypeStruct((4 * rows, width), f32),
        ),
        in_specs=[whole()] * 4,
        out_specs=[whole()] * 2,
    )(*shares)


def place_qkv_kernel(*refs):
    ones, twos, qkv_ref, out_ref, small_ref = refs[:4], refs[4:8], refs[8], refs[9], refs[10]
    width = out_ref.shape[1]
    low = group_index()
    vectors = twos[0][:, 128:].astype(f32)
    for d in range(1, GROUP):
        vectors = vectors + twos[d][:, 128:].astype(f32)
    small_ref[...] = vectors.T[64:80]
    for case in range(GROUP):

        @pl.when(low == case)
        def _():
            for d in range(GROUP):
                whose = case ^ d
                one, two = ones[d][...].astype(f32), twos[d][...].astype(f32)

                def put(kind, h, part):
                    at = kind * width + 192 * whose + 64 * h
                    qkv_ref[:, at : at + 64] = part

                for h in range(2):
                    put(0, h, one[:, LANES * h : LANES * h + 64])
                    put(1, h, one[:, LANES * h + 64 : LANES * h + LANES])
                    put(2, h, one[:, 2 * LANES + 64 * h : 2 * LANES + 64 * h + 64])
                for kind in range(3):
                    put(kind, 2, two[:, 64 * kind : 64 * kind + 64])
                if 256 * whose < width:
                    out_ref[:, 256 * whose : 256 * whose + 256] = one[:, 3 * LANES :]


def place_qkv(ones, twos, width, gates=()):
    rows = ones[0].shape[0]
    return launch(
        place_qkv_kernel,
        gates,
        cost=2.0,
        out_shape=(
            jax.ShapeDtypeStruct((rows, 3 * width), f32),
            jax.ShapeDtypeStruct((rows, width), f32),
            jax.ShapeDtypeStruct((16, rows), f32),
        ),
        in_specs=[whole()] * 8,
        out_specs=[whole()] * 3,
    )(*ones, *twos)


def on_device(
    tokens,
    attn_gain,
    attn_shift,
    w_qkv,
    w_out,
    ffn_gain,
    ffn_shift,
    w_in,
    b_in,
    w_down,
    b_down,
    cotangent,
    lengths,
    block_order,
):
    mine = tokens[0]
    row_count, width = mine.shape
    ctx_size = lax.axis_size("ctx")
    dp_size = lax.axis_size("dp")
    far = ctx_size // GROUP
    rows = w_qkv.shape[0]
    half = row_count // 2
    assert math.gcd(H, ctx_size) == GROUP and w_down.shape[0] == GROUP * rows
    where = (lengths, block_order)

    vectors = [attn_gain, attn_shift, ffn_gain, ffn_shift, b_down, b_in]
    vectors = [v.reshape(-1, rows) for v in vectors]
    piece = pack(w_qkv, vectors)
    far_qkv = far_pieces(piece, "qkv")
    tok_over = swap(mine, "ctx", 2, "tokens_x")
    tok_side = swap(mine, "ctx", 1, "tokens_core")
    piece_in, piece_down = pack_ffn(w_out, w_in, w_down, gates=(piece, tok_side))
    down_near = swap(piece_down, "dp", 1, "down_y")
    near_qkv = jnp.stack([after(far_qkv[0], down_near)] + far_qkv[1:])
    cross_qkv = swap(near_qkv, "dp", 1, "qkv_y")
    blocks = [mine, tok_side, tok_over, swap(tok_over, "ctx", 1, "tokens_pass")]
    far_in = far_pieces(after(piece_in, near_qkv), "in")
    cot = cotangent[0]
    cot_over = swap(after(cot, tok_over), "ctx", 2, "cot_x")

    query, keys, values, first, small, qkv_weight = project(
        *where, blocks, near_qkv, cross_qkv
    )
    near_in = jnp.stack([far_in[0]] + [after(v, query) for v in far_in[1:]])
    downs = far_pieces(after(jnp.stack([piece_down, down_near]), query), "down")
    cross_in = swap(near_in, "dp", 1, "in_y")
    cot_side = swap(after(cot, query), "ctx", 1, "cot_core")
    cot_pass = swap(after(cot_over, query), "ctx", 1, "cot_pass")
    if far > 1:
        groups = [[g * GROUP + i for g in range(far)] for i in range(GROUP)]
        keys = lax.all_gather(keys, "ctx", axis=1, tiled=True, axis_index_groups=groups)
        values = lax.all_gather(values, "ctx", axis=1, tiled=True, axis_index_groups=groups)

    def attend_slot(slot, *gates):
        return attend(query, keys, values, slot, 1, row_count, gates=gates)

    attn_two, query_two = attend_slot(2, near_in, cot_side, cot_pass)
    over_attn = swap(attn_two[0], "ctx", 2, "attn_x")
    attn_three, query_three = attend_slot(3, attn_two)
    far_attn = swap(attn_three[0], "ctx", 3, "attn_xcore")
    attn_one, query_one = attend_slot(1, attn_three)
    side_attn = swap(attn_one[0], "ctx", 1, "attn_core")
    attn_zero, query_zero = attend_slot(0, attn_one, over_attn, *downs)
    own_attn = [attn_zero[0], attn_one[0], attn_two[0], attn_three[0]]
    attn = [attn_zero[0], side_attn, over_attn, far_attn]
    near_query = jnp.concatenate([query_zero, query_one], axis=1)
    far_query = jnp.concatenate([query_two, query_three], axis=1)
    cots = [cot, cot_side, cot_over, cot_pass]
    held_in = after(cross_in, attn_one)
    out_piece = jnp.concatenate([near_in[:, :, width:], held_in[:, :, width:]])
    out_pieces = [out_piece, swap(out_piece, "ctx", 1, "out_core")]

    mixed, second, w_o = project_out(mine, attn, out_pieces, small)
    side = swap(second, "ctx", 1, "second_core")
    over = [swap(second[i * half : (i + 1) * half], "ctx", 2, "second_x") for i in range(2)]
    near_parts, weights = feed_forward(
        *where, small, [second, side], cots[:2], [near_in, held_in, *downs], (0, 1), 0
    )
    cross = [swap(after(v, near_parts[0][0]), "ctx", 1, "second_pass") for v in over]
    ds_side = swap(near_parts[1][0], "ctx", 1, "ds_core")
    far_parts, ds_overs = [], []
    previous = near_parts[0][0]
    for i in range(2):
        part = feed_forward(
            *where,
            small,
            [over[i], cross[i]],
            cots[2:],
            weights,
            (2, 3),
            i * half,
            gates=(previous,),
        )[0]
        previous = add(part[0][0], swap(part[1][0], "ctx", 1, "ds_side"))
        ds_overs.append(swap(previous, "ctx", 2, "ds_x"))
        far_parts.append(part)

    spans = ((0, 0), (1, 0), (2, 0), (3, 0), (2, half), (3, half))
    every = near_parts + far_parts[0] + far_parts[1]
    even_ff, odd_ff, bias_grad = ffn_grads(
        *where,
        cots,
        [second, side, over[0], cross[0], over[1], cross[1]],
        [part[2] for part in every],
        [part[3] for part in every],
        spans,
        dp_size,
        gates=(ds_side, previous),
    )
    dmixed, small_grad, dattn, out_blocks = mixed_back(
        *where,
        mixed,
        cot,
        small,
        w_o,
        attn,
        [near_parts[0][0], ds_side] + ds_overs,
        gates=(even_ff,),
    )
    dattn = exchange_group(dattn, "dattn")
    ffn_even = add(even_ff, swap(odd_ff, "dp", 1, "ffn_y"))
    outs_near = near_parts[0][1], near_parts[1][1]
    outs_far = [jnp.concatenate([far_parts[i][s][1] for i in range(2)]) for s in range(2)]

    def blocks_sum(*gates):
        one, three = after(out_blocks[1], *gates), after(out_blocks[3], *gates)
        own = add(out_blocks[0], swap(one, "ctx", 1, "dw_out_core"))
        across = add(out_blocks[2], swap(three, "ctx", 1, "dw_out_side"))
        return own, swap(across, "ctx", 2, "dw_out_x")

    if far > 1:
        all_query = jnp.concatenate([near_query, far_query], axis=1)
        dk, dv, dq = attend_back(
            all_query, keys, values, own_attn, dattn, (0, 1, 2), (0, 1, 2, 3), "raw", ()
        )
        dk, dv = (
            lax.psum_scatter(v, "ctx", scatter_dimension=1, tiled=True, axis_index_groups=groups)
            for v in (dk, dv)
        )
        dq, dk, dv = (v[..., :64].astype(bf16) for v in (dq, dk, dv))
        one = jnp.concatenate([dq[0], dk[0], dq[1], dk[1], dv[0], dv[1]], axis=1)
        two = jnp.concatenate([dq[2], dk[2], dv[2], jnp.zeros_like(dv[2])], axis=1)
        ones = [one[d * row_count : (d + 1) * row_count] for d in range(GROUP)]
        twos = [two[d * row_count : (d + 1) * row_count] for d in range(GROUP)]
        begun = (dq, dk, dv)
        out_block = add(*blocks_sum())
    else:
        begun = attend_back(
            near_query, keys, values, own_attn[:2], dattn[:2], (0, 1), (0, 1), "begin", ()
        )
        out_block = blocks_sum(dattn[2], begun[0])
        ones = attend_back(
            far_query,
            keys,
            values,
            own_attn[2:],
            dattn[2:],
            (0, 1),
            (2, 3),
            "final",
            begun,
            gates=(ffn_even,),
        )
        out_block = add(*out_block)
    outs_side = swap(after(outs_near[1], ones[0]), "ctx", 1, "outs_core")
    outs_back = swap(after(outs_far[1], ones[0]), "ctx", 1, "outs_side")
    outs_sum = add(outs_far[0], outs_back)
    ffn_share = scatter_far(ffn_even, "ffn")

    even, odd, part_sums = first_grad(
        ones, first, qkv_weight, out_block, dp_size, gates=(ffn_share[0], outs_sum, outs_side)
    )
    outs_over = swap(after(outs_sum, even), "ctx", 2, "outs_x")
    one_even = add(even, swap(odd, "dp", 1, "one_y"))
    if far == 1:
        all_query = jnp.concatenate([near_query[2:], far_query[2:]], axis=1)
        twos = attend_back(
            all_query,
            keys,
            values,
            own_attn,
            dattn,
            (2,),
            (0, 1, 2, 3),
            "final",
            (),
            gates=(even,),
        )
    even, odd = second_grad(
        twos,
        first,
        qkv_weight,
        part_sums,
        small_grad,
        bias_grad,
        dp_size,
        gates=(one_even, ffn_share[1], outs_over),
    )
    two_even = add(even, swap(odd, "dp", 1, "two_y"))
    one_share = scatter_far(one_even, "one")
    ffn_shares = gather_group(sum_groups(ffn_share[1]), "ffn")
    parts = input_parts(ones, twos, qkv_weight, gates=(even,))
    layer_out = finish_out(
        *where, mixed, small, [outs_near[0], outs_side, outs_over], gates=(parts[0],)
    )
    part_over = swap(add(parts[2], swap(parts[3], "ctx", 1, "df_side")), "ctx", 2, "df_x")
    part_side = swap(parts[1], "ctx", 1, "df_core")
    grad_w_in, grad_w_down = place_ffn(ffn_shares, gates=(layer_out, two_even))
    two_share = scatter_far(two_even, "two")
    one_shares = gather_group(sum_groups(one_share[1]), "one")
    two_shares = gather_group(sum_groups(two_share[1]), "two")
    input_grad = finish_input(mine, [parts[0], part_side, part_over], dmixed, small)
    grad_w_qkv, grad_w_out, vector_grads = place_qkv(one_shares, two_shares, width)
    return (
        layer_out[None],
        input_grad[None],
        vector_grads[0],
        vector_grads[1],
        grad_w_qkv,
        grad_w_out,
        vector_grads[2],
        vector_grads[3],
        grad_w_in,
        vector_grads[5:9].reshape(-1),
        grad_w_down,
        vector_grads[4],
    )


def solution(mesh):
    placed = (
        P("dp", "ctx", None),
        P("dp"),
        P("dp"),
        P("dp", None),
        P("dp", None),
        P("dp"),
        P("dp"),
        P("dp", None),
        P("dp"),
        P("dp", None),
        P("dp"),
        P("dp", "ctx", None),
        P("dp"),
        P("dp", None),
    )
    return jax.shard_map(
        on_device,
        mesh=mesh,
        in_specs=placed,
        out_specs=(
            P("dp", "ctx", None),
            P("dp", "ctx", None),
            P("dp"),
            P("dp"),
            P("dp", None),
            P("dp", None),
            P("dp"),
            P("dp"),
            P("dp", None),
            P("dp"),
            P("dp", None),
            P("dp"),
        ),
        check_vma=False,
    )
```

```python
import functools
import math

import jax
import jax.numpy as jnp
from jax import lax
from jax.experimental import pallas as pl
from jax.experimental.pallas import tpu as pltpu
from jax.sharding import PartitionSpec as P

H = 12

epsilon = 1e-05
gelu_coeff = 0.7978845608
cubic_term = 0.044715
excluded = -1073741824.0
bf16 = jnp.bfloat16
f32 = jnp.float32
LANES = 128
GROUP = 4
VMEM_SMALL = 16 * 1024 * 1024
VMEM_LARGE = 52 * 1024 * 1024

nt_dims = (((1,), (1,)), ((), ()))
tn_dims = (((0,), (0,)), ((), ()))


def mm(left, right):
    return jnp.dot(left, right, preferred_element_type=f32)


def mm_nt(left, right):
    return lax.dot_general(left, right, nt_dims, preferred_element_type=f32)


def mm_tn(left, right):
    return lax.dot_general(left, right, tn_dims, preferred_element_type=f32)


def whole(memory_space=pltpu.VMEM):
    return pl.BlockSpec(memory_space=memory_space)


def lanes_of(shape):
    return lax.broadcasted_iota(jnp.int32, shape, 1)


def norm_parts(values):
    center = values - jnp.mean(values, axis=-1, keepdims=True)
    spread = jnp.mean(center * center, axis=-1, keepdims=True)
    inverse = lax.rsqrt(spread + epsilon)
    return center * inverse, inverse


def norm_back(scaled, unit, inverse):
    return inverse * (
        scaled
        - jnp.mean(scaled, axis=-1, keepdims=True)
        - unit * jnp.mean(scaled * unit, axis=-1, keepdims=True)
    )


def three_parts(value):
    first = value.astype(bf16).astype(f32)
    rest = value - first
    second = rest.astype(bf16).astype(f32)
    return first, second, rest - second


def with_parts(base, value):
    lane = lanes_of(base.shape)
    one, two, three = three_parts(value)
    return jnp.where(
        lane == 64, one, jnp.where(lane == 65, two, jnp.where(lane == 66, three, base))
    )


def unpack_rows(packed, rows):
    tail = jnp.concatenate([packed[rows:, :64], packed[rows:, 64:]], axis=0)
    return packed[:rows], tail


def swap(value, axis, bit, name):
    size = lax.axis_size(axis)
    with jax.named_scope(name):
        return lax.ppermute(value, axis, [(i, i ^ bit) for i in range(size)])


def launch(kernel, gates, in_specs, cost=1.0, large=False, **options):
    count = len(gates)
    flops = int(cost * 2e7)

    def gated(*refs):
        kernel(*refs[count:])

    call = pl.pallas_call(
        gated,
        in_specs=[whole(pl.ANY)] * count + in_specs,
        compiler_params=pltpu.CompilerParams(
            vmem_limit_bytes=VMEM_LARGE if large else VMEM_SMALL
        ),
        cost_estimate=pl.CostEstimate(flops=flops, bytes_accessed=1024, transcendentals=0),
        **options,
    )
    return lambda *operands: call(*gates, *operands)


def hold_kernel(value_ref, out_ref):
    pass


def after(value, *gates):
    return launch(
        hold_kernel,
        gates,
        [whole(pl.ANY)],
        out_shape=jax.ShapeDtypeStruct(value.shape, value.dtype),
        out_specs=whole(pl.ANY),
        input_output_aliases={len(gates): 0},
    )(value)


def far_pieces(piece, name):
    found = [piece]
    for k in range(1, lax.axis_size("dp") // 2):
        found.append(swap(piece, "dp", 2 * k, name + "_z"))
    return found


def add(left, right):
    return (left.astype(f32) + right.astype(f32)).astype(bf16)


def scatter_far(even, name, gate):
    def step(even, gate):
        half = even.shape[0] // 2
        bit = lax.axis_size("dp") // (2 * half)
        pairs = even.reshape(half, 2, *even.shape[1:])
        received = swap(pairs[:, 1], "dp", bit, name + "_z")
        return add(pairs[:, 0], received if gate is None else after(received, gate))

    begun = step(even, gate)

    def finish(gate):
        total = begun
        while total.shape[0] > 1:
            total = step(total, gate)
        return total[0]

    return begun, finish


def sum_groups(value):
    bit = GROUP
    while bit < lax.axis_size("ctx"):
        other = swap(value, "ctx", bit, "groups")
        value = (value.astype(f32) + other.astype(f32)).astype(bf16)
        bit *= 2
    return value


def gather_group(value, name, gate=None):
    over = swap(value, "ctx", 2, name + "_x")
    if gate is not None:
        over = after(over, gate)
    side = swap(value, "ctx", 1, name + "_core")
    return [value, side, over, swap(over, "ctx", 1, name + "_pass")]


def exchange_group(values, name):
    names = ("", "_core", "_x", "_xcore")
    return [values[0]] + [swap(values[d], "ctx", d, name + names[d]) for d in range(1, GROUP)]


def position_of(order_ref, slot, rows):
    index = lax.axis_index("ctx")
    return order_ref[0, lax.bitwise_xor(index, slot)] * rows


def valid_rows(length_ref, order_ref, slot, rows):
    stored = lax.broadcasted_iota(jnp.int32, (rows, LANES), 0)[:, :1]
    position = position_of(order_ref, slot, rows) + stored
    return jnp.where(position < length_ref[0], 1.0, 0.0)


def group_index():
    return lax.rem(lax.axis_index("ctx"), GROUP)


def load_pieces(sources, target, sems, first_sem=0):
    me = lax.axis_index("dp")
    copies = []
    for source, differences in sources:
        rows = source.shape[1]
        for k, difference in enumerate(differences):
            owner = lax.bitwise_xor(me, difference)
            copies.append(
                pltpu.make_async_copy(
                    source.at[k],
                    target.at[pl.ds(pl.multiple_of(owner * rows, 16), rows)],
                    sems.at[first_sem + len(copies)],
                )
            )
    for copy in copies:
        copy.start()
    return copies


def near_and_cross(near, cross):
    halves = near.shape[0]
    return [(near, [2 * k for k in range(halves)]), (cross, [2 * k + 1 for k in range(halves)])]


def store_pieces(source, even, odd, sems):
    halves, rows, _ = even.shape
    me = lax.axis_index("dp")
    copies = []
    for parity, target in ((0, even), (1, odd)):
        for k in range(halves):
            owner = lax.bitwise_xor(me, 2 * k + parity)
            copies.append(
                pltpu.make_async_copy(
                    source.at[pl.ds(pl.multiple_of(owner * rows, 16), rows)],
                    target.at[k],
                    sems.at[2 * k + parity],
                )
            )
    for copy in copies:
        copy.start()
    for copy in copies:
        copy.wait()


def pack_kernel(w_hbm, *refs):
    w_ref, sems = refs[-2:]
    count = (len(refs) - 3) // 2
    vectors, out_ref, held = refs[:count], refs[count], refs[count + 1 : -2]
    copies = [pltpu.make_async_copy(w_hbm, w_ref, sems.at[count])]
    for i in range(count):
        copies.append(pltpu.make_async_copy(vectors[i], held[i], sems.at[i]))
    for copy in copies:
        copy.start()
    for copy in copies:
        copy.wait()
    rows = w_ref.shape[0]
    width = w_ref.shape[1] // 3
    low = group_index()
    stacked = []
    for v in held:
        flat = v[...].astype(f32).reshape(1, v.shape[0])
        stacked += [flat[:, i : i + rows] for i in range(0, v.shape[0], rows)]
    stacked.append(jnp.zeros((LANES - len(stacked), rows), f32))
    small = jnp.concatenate(stacked, axis=0).T[:, :64].astype(bf16)
    for case in range(GROUP):

        @pl.when(low == case)
        def _():
            def head(kind, h):
                at = kind * width + 192 * case + 64 * h
                return w_ref[:, at : at + 64]

            out_ref[...] = jnp.concatenate(
                [
                    head(0, 0),
                    head(1, 0),
                    head(0, 1),
                    head(1, 1),
                    head(2, 0),
                    head(2, 1),
                    head(0, 2),
                    head(1, 2),
                    head(2, 2),
                    small,
                ],
                axis=1,
            )


def pack(w_qkv, vectors, gates=()):
    rows = w_qkv.shape[0]
    return launch(
        pack_kernel,
        gates,
        cost=1.0,
        out_shape=jax.ShapeDtypeStruct((rows, 640), bf16),
        in_specs=[whole(pltpu.HBM)] * (1 + len(vectors)),
        out_specs=whole(),
        scratch_shapes=[pltpu.VMEM(v.shape, bf16) for v in vectors]
        + [pltpu.VMEM(w_qkv.shape, bf16), pltpu.SemaphoreType.DMA((1 + len(vectors),))],
    )(w_qkv, *vectors)


def pack_ffn_kernel(out_ref, in_ref, down_ref, one_ref, two_ref):
    rows, ff = in_ref.shape
    width = out_ref.shape[1]
    half = width // 2
    low = group_index()
    per = 4 * rows
    for case in range(GROUP):

        @pl.when(low == case)
        def _():
            at = half * (case % 2)
            parts = [
                in_ref[:, per * i + rows * case : per * i + rows * (case + 1)]
                for i in range(ff // per)
            ]
            one_ref[:, :width] = jnp.concatenate(parts, axis=1)
            one_ref[:, width:] = out_ref[:, at : at + half]
            two_ref[...] = down_ref[rows * case : rows * (case + 1)]


def pack_ffn(w_out, w_in, w_down, gates=()):
    rows, width = w_out.shape
    return launch(
        pack_ffn_kernel,
        gates,
        cost=1.0,
        out_shape=(
            jax.ShapeDtypeStruct((rows, width + width // 2), bf16),
            jax.ShapeDtypeStruct((rows, width), bf16),
        ),
        in_specs=[whole()] * 3,
        out_specs=[whole()] * 2,
    )(w_out, w_in, w_down)


def qkv_kernel(length_ref, order_ref, *refs):
    tokens = refs[:GROUP]
    near, cross = refs[GROUP : GROUP + 2]
    q_ref, k_ref, v_ref, first_ref, small_ref, w_ref, sems = refs[GROUP + 2 :]
    row_count, width = tokens[0].shape
    for copy in load_pieces(near_and_cross(near, cross), w_ref, sems):
        copy.wait()
    small = w_ref[:, 512:640].astype(f32).T
    small_ref[...] = small[64:80]
    gain, shift = small[64:65], small[65:66]
    length = length_ref[0]
    lane = lanes_of((row_count, LANES))
    ones = jnp.where((lane >= 64) & (lane < 67), 1.0, 0.0)
    bias_lane = jnp.where(lane == 67, 1.0, 0.0)
    for d in range(GROUP):
        unit, _ = norm_parts(tokens[d][...].astype(f32))
        first = (unit * gain + shift).astype(bf16)
        part = pl.ds(d * row_count, row_count)
        first_ref[part] = first
        qkv = mm(first, w_ref[...]).astype(bf16).astype(f32)

        def head(place):
            block = qkv[:, place // 2 * LANES : (place // 2 + 1) * LANES]
            if place % 2:
                block = pltpu.roll(block, 64, 1)
            return jnp.where(lane < 64, block, 0.0)

        stored = lax.broadcasted_iota(jnp.int32, (row_count, LANES), 0)
        position = position_of(order_ref, d, row_count) + stored
        bias = jnp.where(position < length, 0.0, excluded) * bias_lane
        for h, (at_q, at_k, at_v) in enumerate(((0, 1, 4), (2, 3, 5), (6, 7, 8))):
            q_ref[h, part] = (head(at_q) * 0.125 + bias_lane).astype(bf16)
            k_ref[h, part] = (head(at_k) + ones + bias).astype(bf16)
            v_ref[h, part] = (head(at_v) + ones).astype(bf16)


def project(length, order, tokens, near, cross, gates=()):
    row_count, width = tokens[0].shape
    total = GROUP * row_count
    wide = near.shape[2]
    head_out = jax.ShapeDtypeStruct((3, total, LANES), bf16)
    return launch(
        qkv_kernel,
        gates,
        cost=10.0,
        out_shape=(
            head_out,
            head_out,
            head_out,
            jax.ShapeDtypeStruct((total, width), bf16),
            jax.ShapeDtypeStruct((16, width), f32),
            jax.ShapeDtypeStruct((width, wide), bf16),
        ),
        in_specs=[whole(pltpu.SMEM)] * 2 + [whole()] * GROUP + [whole(pl.ANY)] * 2,
        out_specs=[whole()] * 6,
        scratch_shapes=[pltpu.SemaphoreType.DMA((2 * near.shape[0],))],
    )(length, order, *tokens, near, cross)


def attend_kernel(block_rows, q_ref, k_ref, v_ref, packed_ref, q_out_ref):
    row_count = q_ref.shape[1]
    half = row_count // 2
    lane = lanes_of((block_rows, LANES))
    for i in range(row_count // block_rows):
        part = pl.ds(i * block_rows, block_rows)
        heads = []
        for h in range(3):
            query = q_ref[h, part]
            scores = mm_nt(query, k_ref[h])
            top = jnp.max(scores, axis=1, keepdims=True)
            weights = jnp.exp(scores - top).astype(bf16)
            result = mm(weights, v_ref[h])
            denom = result[:, 64:65]
            heads.append(jnp.where(lane < 64, result / denom, 0.0))
            log_total = top + jnp.log(denom)
            q_out_ref[h, part] = with_parts(query.astype(f32), -log_total).astype(bf16)
        packed_ref[0, part] = (heads[0] + pltpu.roll(heads[1], 64, 1)).astype(bf16)
        for r in range(0, block_rows, half):
            size = min(half, block_rows)
            row = i * block_rows + r
            side, place = row // half, row % half
            packed_ref[
                0, pl.ds(row_count + place, size), 64 * side : 64 * side + 64
            ] = heads[2][r : r + size, :64].astype(bf16)


def attend(query, keys, values, first_slot, slots, row_count, gates=()):
    total = keys.shape[1]
    block_rows = min(row_count // 2, 256)
    return launch(
        functools.partial(attend_kernel, block_rows),
        gates,
        cost=5.0 * slots,
        large=total > GROUP * row_count,
        grid=(slots,),
        out_shape=(
            jax.ShapeDtypeStruct((slots, row_count * 3 // 2, LANES), bf16),
            jax.ShapeDtypeStruct((3, slots * row_count, LANES), bf16),
        ),
        in_specs=[
            pl.BlockSpec((3, row_count, LANES), lambda s: (0, s + first_slot, 0)),
            whole(),
            whole(),
        ],
        out_specs=(
            pl.BlockSpec((1, row_count * 3 // 2, LANES), lambda s: (s, 0, 0)),
            pl.BlockSpec((3, row_count, LANES), lambda s: (0, s, 0)),
        ),
    )(query, keys, values)


def group_attn(refs, row_count):
    near, core, over = refs
    packed = (near[0], core[0], over[0], core[1])
    return [jnp.concatenate(unpack_rows(v, row_count), axis=1) for v in packed]


def out_kernel(token_ref, *refs):
    attn_refs, pieces = refs[:3], refs[3:5]
    small_ref, mixed_ref, second_ref, w_o, sems = refs[5:]
    row_count, width = token_ref.shape
    half = width // 2
    number = pieces[0].shape[0]
    low = group_index()
    core = lax.rem(low, 2)
    differences = [2 * k for k in range(number // 2)] + [2 * k + 1 for k in range(number // 2)]
    copies = []
    for side in range(2):
        column = pl.multiple_of((core if side == 0 else 1 - core) * half, LANES)
        target = w_o.at[:, pl.ds(column, half)]
        copies += load_pieces([(pieces[side], differences)], target, sems, side * number)
    mixed = token_ref[...].astype(f32)
    attn = group_attn(attn_refs, row_count)
    for copy in copies:
        copy.wait()
    for d in range(GROUP):
        at = pl.ds(pl.multiple_of(lax.bitwise_xor(low, d) * 192, 16), 192)
        mixed = mixed + mm(attn[d], w_o[at, :])
    mixed_ref[...] = mixed
    unit, _ = norm_parts(mixed)
    second_ref[...] = (unit * small_ref[2:3] + small_ref[3:4]).astype(bf16)


def project_out(tokens, attn, pieces, small, gates=()):
    row_count, width = tokens.shape
    number = pieces[0].shape[0]
    return launch(
        out_kernel,
        gates,
        cost=4.5,
        out_shape=(
            jax.ShapeDtypeStruct((row_count, width), f32),
            jax.ShapeDtypeStruct((row_count, width), bf16),
            jax.ShapeDtypeStruct((width, width), bf16),
        ),
        in_specs=[whole()] * 4 + [whole(pl.ANY)] * 2 + [whole()],
        out_specs=[whole()] * 3,
        scratch_shapes=[pltpu.SemaphoreType.DMA((2 * number,))],
    )(tokens, *attn, *pieces, small)


def ffn_kernel(slots, gathers, length_ref, order_ref, small_ref, *refs):
    number = len(slots)
    seconds, cots = refs[:number], refs[number : 2 * number]
    refs = refs[2 * number :]
    count = 4 if gathers else 2
    sources, refs = refs[:count], refs[count:]
    outs = [refs[3 * i : 3 + 3 * i] for i in range(number)]
    refs = refs[3 * number :]
    rows, width = seconds[0].shape
    if gathers:
        w_i, w_d, sems = refs
        near, cross, near_down, cross_down = sources
        parts = near_and_cross(*(v.at[:, :, pl.ds(0, width)] for v in (near, cross)))
        in_copies = load_pieces(parts, w_i, sems)
        down_copies = load_pieces(near_and_cross(near_down, cross_down), w_d, sems, 2 * gathers)
        for copy in in_copies:
            copy.wait()
    else:
        w_i, w_d = sources
    bias = small_ref[pl.ds(5 + group_index(), 1)]
    for i, slot in enumerate(slots):
        ds_ref, active_ref, dhid_ref = outs[i]
        row_count = cots[i].shape[0]
        valid = valid_rows(length_ref, order_ref, slot, row_count)
        dlow = (cots[i][...].astype(f32) * valid).astype(bf16)
        hidden = mm(seconds[i][...], w_i[...]) + bias
        squared = hidden * hidden
        bent = jnp.tanh(hidden * (gelu_coeff + gelu_coeff * cubic_term * squared))
        plus = 0.5 + 0.5 * bent
        slope = plus + hidden * (plus * (1.0 - bent)) * (
            gelu_coeff + gelu_coeff * 3.0 * cubic_term * squared
        )
        active_ref[...] = (hidden * plus).astype(bf16)
        if gathers and i == 0:
            for copy in down_copies:
                copy.wait()
        dhid = (mm_nt(dlow, w_d[...]) * slope).astype(bf16)
        dhid_ref[...] = dhid
        ds_ref[...] = mm_nt(dhid, w_i[...]).astype(bf16)


def feed_forward(length, order, small, seconds, cots, weights, slots, gates=()):
    rows, width = seconds[0].shape
    gathers = weights[0].shape[0] if len(weights) == 4 else 0
    number = len(slots)
    block = jax.ShapeDtypeStruct((rows, width), bf16)
    square = jax.ShapeDtypeStruct((width, width), bf16)
    results = launch(
        functools.partial(ffn_kernel, slots, gathers),
        gates,
        cost=3.0 * number,
        out_shape=[block] * (3 * number) + [square] * (2 if gathers else 0),
        in_specs=[whole(pltpu.SMEM)] * 2
        + [whole()] * (1 + 2 * number)
        + [whole(pl.ANY) if gathers else whole()] * len(weights),
        out_specs=[whole()] * (3 * number + (2 if gathers else 0)),
        scratch_shapes=[pltpu.SemaphoreType.DMA((4 * gathers,))] if gathers else [],
    )(length, order, small, *seconds, *cots, *weights)
    grouped = [results[3 * i : 3 * i + 3] for i in range(number)]
    return grouped, results[3 * number :]


def out_part_kernel(*refs):
    w_d = refs[2][...]
    for i in range(2):
        refs[3 + i][...] = mm(refs[i][...], w_d).astype(bf16)


def out_parts(actives, w_down, gates=()):
    return launch(
        out_part_kernel,
        gates,
        cost=2.0,
        out_shape=[jax.ShapeDtypeStruct(v.shape, bf16) for v in actives],
        in_specs=[whole()] * 3,
        out_specs=[whole()] * 2,
    )(*actives, w_down)


def ffn_grad_kernel(length_ref, order_ref, *refs):
    cots, seconds, actives, dhids = (refs[i : i + GROUP] for i in range(0, 4 * GROUP, GROUP))
    even, odd, bias_ref, g_ref, sems = refs[4 * GROUP :]
    row_count, width = cots[0].shape
    bias = jnp.zeros((1, width), f32)
    grad_in = jnp.zeros((width, width), f32)
    for d in range(GROUP):
        dhid = dhids[d][...]
        bias = bias + jnp.sum(dhid.astype(f32), axis=0, keepdims=True)
        grad_in = grad_in + mm_tn(seconds[d][...], dhid)
    g_ref[:, :width] = grad_in.astype(bf16)
    bias_ref[...] = bias
    grad_down = jnp.zeros((width, width), f32)
    for d in range(GROUP):
        valid = valid_rows(length_ref, order_ref, d, row_count)
        dlow = (cots[d][...].astype(f32) * valid).astype(bf16)
        grad_down = grad_down + mm_tn(actives[d][...], dlow)
    g_ref[:, width:] = grad_down.astype(bf16)
    store_pieces(g_ref, even, odd, sems)


def ffn_grads(length, order, cots, seconds, actives, dhids, dp_size, gates=()):
    width = cots[0].shape[1]
    halves = dp_size // 2
    piece = jax.ShapeDtypeStruct((halves, width // dp_size, 2 * width), bf16)
    return launch(
        ffn_grad_kernel,
        gates,
        cost=7.0,
        out_shape=(piece, piece, jax.ShapeDtypeStruct((1, width), f32)),
        in_specs=[whole(pltpu.SMEM)] * 2 + [whole()] * (4 * GROUP),
        out_specs=[whole(pl.ANY)] * 2 + [whole()],
        scratch_shapes=[
            pltpu.VMEM((width, 2 * width), bf16),
            pltpu.SemaphoreType.DMA((dp_size,)),
        ],
    )(length, order, *cots, *seconds, *actives, *dhids)


def mixed_back_kernel(length_ref, order_ref, *refs):
    mixed_ref, cot_ref, small_ref, w_o = refs[:4]
    attn_refs = refs[4:7]
    ds_refs = refs[7:10]
    dmixed_ref, small_grad_ref = refs[10:12]
    own, side, over = refs[12:15]
    dattn_refs = (own, side, over.at[0], over.at[1])
    block_refs = refs[15 : 15 + GROUP]
    g_o = refs[19]
    row_count, width = mixed_ref.shape
    half = row_count // 2
    low = group_index()
    unit, inverse = norm_parts(mixed_ref[...])
    ds = sum(v[...].astype(f32) for v in ds_refs)
    valid = valid_rows(length_ref, order_ref, 0, row_count)
    dout = cot_ref[...].astype(f32) * valid
    dmixed = dout + norm_back(ds * small_ref[2:3], unit, inverse)
    dmixed_ref[...] = dmixed
    dbranch = dmixed.astype(bf16)

    def out_rows(d):
        return pl.ds(pl.multiple_of(lax.bitwise_xor(low, d) * 192, 16), 192)

    for d in range(GROUP):
        dattn = mm_nt(dbranch, w_o[out_rows(d), :])
        dattn_refs[d][pl.ds(0, row_count)] = dattn[:, :LANES].astype(bf16)
        dattn_refs[d][pl.ds(row_count, half), :64] = dattn[:half, LANES:].astype(bf16)
        dattn_refs[d][pl.ds(row_count, half), 64:] = dattn[half:, LANES:].astype(bf16)
    g_o[:, width:] = jnp.zeros((width, 1024 - width), bf16)
    attn = group_attn(attn_refs, row_count)
    for d in range(GROUP):
        g_o[out_rows(d), :width] = mm_tn(attn[d], dbranch).astype(bf16)
    for d in range(GROUP):
        column = pl.multiple_of(lax.bitwise_xor(low, d) * 256, LANES)
        block_refs[d][...] = g_o[:, pl.ds(column, 256)]
    small_grad_ref[...] = jnp.zeros_like(small_grad_ref)
    small_grad_ref[2:3] = jnp.sum(ds * unit, axis=0, keepdims=True)
    small_grad_ref[3:4] = jnp.sum(ds, axis=0, keepdims=True)
    small_grad_ref[4:5] = jnp.sum(dout, axis=0, keepdims=True)


def mixed_back(length, order, mixed, cot, small, w_o, attn, ds, gates=()):
    row_count, width = mixed.shape
    results = launch(
        mixed_back_kernel,
        gates,
        cost=7.0,
        out_shape=[
            jax.ShapeDtypeStruct((row_count, width), f32),
            jax.ShapeDtypeStruct((16, width), f32),
        ]
        + [jax.ShapeDtypeStruct((row_count * 3 // 2, LANES), bf16)] * 2
        + [jax.ShapeDtypeStruct((2, row_count * 3 // 2, LANES), bf16)]
        + [jax.ShapeDtypeStruct((width, 256), bf16)] * GROUP,
        in_specs=[whole(pltpu.SMEM)] * 2 + [whole()] * 10,
        out_specs=[whole()] * 9,
        scratch_shapes=[pltpu.VMEM((width, 1024), bf16)],
    )(length, order, mixed, cot, small, w_o, *attn, *ds)
    return results[0], results[1], results[2:5], results[5:9]


def layer_out_kernel(length_ref, order_ref, mixed_ref, small_ref, *refs):
    own, side, over, out_ref = refs
    row_count = mixed_ref.shape[0]
    valid = valid_rows(length_ref, order_ref, 0, row_count)
    total = mixed_ref[...] + own[...].astype(f32) + side[...].astype(f32) + over[...].astype(f32)
    out_ref[...] = ((total + small_ref[4:5]) * valid).astype(bf16)


def finish_out(length, order, mixed, small, parts, gates=()):
    return launch(
        layer_out_kernel,
        gates,
        cost=3.0,
        out_shape=jax.ShapeDtypeStruct(mixed.shape, bf16),
        in_specs=[whole(pltpu.SMEM)] * 2 + [whole()] * 5,
        out_specs=whole(),
    )(length, order, mixed, small, *parts)


def attend_back_kernel(mode, heads, slots, row_count, starts, *refs):
    number = len(slots)
    pairs = number // 2
    q_refs, (k_ref, v_ref) = refs[:pairs], refs[pairs : pairs + 2]
    refs = refs[pairs + 2 :]
    attn_refs, dattn_refs = refs[:pairs], refs[pairs : pairs + number]
    refs = refs[pairs + number :]
    if starts:
        dk_in, dv_in, dq_in = refs[:3]
        refs = refs[3:]
    outs = refs[:-5]
    grad_ref, k_turned, dq_ref, dk_ref, dv_ref = refs[-5:]
    head, step = pl.program_id(0), pl.program_id(1)
    total = k_ref.shape[1]
    chunk = row_count
    first_slot = slots[0] if mode == "final" else 0

    @pl.when((head == 0) & (step == 0))
    def _():
        lane = lanes_of((row_count, LANES))
        for d in range(number):
            top, tail = unpack_rows(dattn_refs[d][...].astype(f32), row_count)
            top_a, tail_a = unpack_rows(attn_refs[d // 2][d % 2].astype(f32), row_count)
            product = top * top_a
            for i, h in enumerate(heads):
                if h == 0:
                    block = top
                    delta = jnp.sum(jnp.where(lane < 64, product, 0.0), axis=1, keepdims=True)
                elif h == 1:
                    block = pltpu.roll(top, 64, 1)
                    delta = jnp.sum(jnp.where(lane >= 64, product, 0.0), axis=1, keepdims=True)
                else:
                    block = jnp.concatenate([tail, tail], axis=1)
                    delta = jnp.sum(tail * tail_a, axis=1, keepdims=True)
                base = jnp.where(lane < 64, block, 0.0)
                grad_ref[i, pl.ds(d * row_count, row_count)] = with_parts(base, -delta).astype(bf16)

    @pl.when(step == 0)
    def _():
        k_turned[...] = k_ref[0].astype(f32).T.astype(bf16)
        if starts:
            dk_ref[...] = dk_in[0]
            dv_ref[...] = dv_in[0]
            dq_ref[: first_slot * row_count] = dq_in[0]
        else:
            dk_ref[...] = jnp.zeros_like(dk_ref)
            dv_ref[...] = jnp.zeros_like(dv_ref)

    query = q_refs[0][0]
    if pairs > 1:
        query = jnp.where(step < 2, query, q_refs[1][0])
    grad = grad_ref[head, pl.ds(pl.multiple_of(step * row_count, row_count), row_count)]
    turned = jnp.zeros((LANES, row_count), f32)
    for c in range(total // chunk):
        at = pl.ds(c * chunk, chunk)
        probs = jnp.exp(mm_nt(k_ref[0, at], query))
        dscores = (probs * mm_nt(v_ref[0, at], grad)).astype(bf16)
        dv_ref[at] += mm(probs.astype(bf16), grad)
        dk_ref[at] += mm(dscores, query)
        turned = turned + mm(k_turned[:, at], dscores)
    place = pl.multiple_of((first_slot + step) * row_count, row_count)
    dq_ref[pl.ds(place, row_count)] = turned.T * 0.125

    @pl.when(step == number - 1)
    def _():
        if mode != "final":
            outs[0][0] = dk_ref[...]
            outs[1][0] = dv_ref[...]
            outs[2][0] = dq_ref[...]
            return
        lane = lanes_of((row_count, LANES))
        last_at = LANES * len(heads)
        for i in range(len(heads)):

            @pl.when(head == i)
            def _():
                for d in range(GROUP):
                    at = pl.ds(d * row_count, row_count)
                    pair = jnp.where(lane < 64, dq_ref[at], pltpu.roll(dk_ref[at], 64, 1))
                    outs[d][:, i * LANES : (i + 1) * LANES] = pair.astype(bf16)
                    value = dv_ref[at]
                    if i == 0:
                        value = jnp.where(lane < 64, value, 0.0)
                        outs[d][:, last_at : last_at + LANES] = value.astype(bf16)
                    else:
                        outs[d][:, last_at + 64 : last_at + LANES] = value[:, :64].astype(bf16)


def attend_back(queries, keys, values, attn, dattn, heads, slots, mode, begun, gates=()):
    row_count = dattn[0].shape[0] * 2 // 3
    total = keys.shape[1]
    number = len(slots)
    kept = GROUP if mode == "final" else number
    first_head = heads[0]
    if number == 2:
        places = [lambda h, s: (h + first_head, s, 0)]
    else:
        places = [
            lambda h, s: (h + first_head, jnp.minimum(s, 1), 0),
            lambda h, s: (h + first_head, jnp.maximum(s - 2, 0), 0),
        ]

    def per_head(size):
        return (
            jax.ShapeDtypeStruct((len(heads), size, LANES), f32),
            pl.BlockSpec((1, size, LANES), lambda h, s: (h, 0, 0)),
        )

    if mode == "final":
        wide = LANES * (len(heads) + 1)
        outs = [
            (
                jax.ShapeDtypeStruct((row_count, wide), bf16),
                pl.BlockSpec((row_count, wide), lambda h, s: (0, 0)),
            )
        ] * GROUP
    else:
        outs = [per_head(total), per_head(total), per_head(number * row_count)]
    begun_specs = []
    if begun:
        begun_specs = [
            pl.BlockSpec((1, v.shape[1], LANES), lambda h, s: (h, 0, 0)) for v in begun
        ]
    return launch(
        functools.partial(attend_back_kernel, mode, heads, slots, row_count, bool(begun)),
        gates,
        cost=3.2 * number * len(heads),
        large=total > GROUP * row_count,
        grid=(len(heads), number),
        out_shape=[shape for shape, _ in outs],
        out_specs=[spec for _, spec in outs],
        in_specs=[
            pl.BlockSpec((1, row_count, LANES), place) for place in places
        ]
        + [pl.BlockSpec((1, total, LANES), lambda h, s: (h + first_head, 0, 0))] * 2
        + [whole()] * (len(attn) + number)
        + begun_specs,
        scratch_shapes=[
            pltpu.VMEM((len(heads), number * row_count, LANES), bf16),
            pltpu.VMEM((LANES, total), bf16),
            pltpu.VMEM((kept * row_count, LANES), f32),
            pltpu.VMEM((total, LANES), f32),
            pltpu.VMEM((total, LANES), f32),
        ],
    )(*queries, keys, values, *attn, *dattn, *begun)


def first_grad_kernel(*refs):
    parts, first_ref, w_ref, block_refs = refs[:4], refs[4], refs[5], refs[6:8]
    even, odd, side_ref, d_ref, g_ref, sems = refs[8:]
    row_count, wide = parts[0].shape
    for d in range(GROUP):
        d_ref[d * row_count : (d + 1) * row_count] = parts[d][...]
    weights = w_ref[...].astype(f32)
    grad = mm_tn(first_ref[...], d_ref[...])
    g_ref[:, :wide] = grad.astype(bf16)
    columns = jnp.sum(d_ref[...].astype(f32), axis=0, keepdims=True)
    shift = weights[:, 577:578]
    used = weights[:, :wide]
    gain_part = jnp.sum(used * (grad - shift * columns), axis=1, keepdims=True)
    shift_part = jnp.sum(used * columns, axis=1, keepdims=True)
    lane = lanes_of(side_ref.shape)
    side_ref[...] = jnp.where(lane == 64, gain_part, jnp.where(lane == 65, shift_part, 0.0))
    block = block_refs[0][...].astype(f32) + block_refs[1][...].astype(f32)
    g_ref[:, wide:] = block.astype(bf16)
    store_pieces(g_ref, even, odd, sems)


def first_grad(parts, first, weights, blocks, dp_size, gates=()):
    total, width = first.shape
    wide = parts[0].shape[1]
    piece = jax.ShapeDtypeStruct((dp_size // 2, width // dp_size, wide + 256), bf16)
    return launch(
        first_grad_kernel,
        gates,
        cost=5.0,
        out_shape=(piece, piece, jax.ShapeDtypeStruct((width, LANES), f32)),
        in_specs=[whole()] * 8,
        out_specs=[whole(pl.ANY)] * 2 + [whole()],
        scratch_shapes=[
            pltpu.VMEM((total, wide), bf16),
            pltpu.VMEM((width, wide + 256), bf16),
            pltpu.SemaphoreType.DMA((dp_size,)),
        ],
    )(*parts, first, weights, *blocks)


def second_grad_kernel(*refs):
    parts = refs[:4]
    first_ref, w_ref, side_ref, small_grad_ref, bias_grad_ref = refs[4:9]
    even, odd, d_ref, g_ref, turn_ref, sems = refs[9:]
    row_count, wide = parts[0].shape
    width = first_ref.shape[1]
    for d in range(GROUP):
        d_ref[d * row_count : (d + 1) * row_count] = parts[d][...]
    weights = w_ref[...].astype(f32)
    grad = mm_tn(first_ref[...], d_ref[...])
    columns = jnp.sum(d_ref[...].astype(f32), axis=0, keepdims=True)
    gain, shift = weights[:, 576:577], weights[:, 577:578]
    used = weights[:, 640 - wide :]
    gain_part = jnp.sum(used * (grad - shift * columns), axis=1, keepdims=True)
    shift_part = jnp.sum(used * columns, axis=1, keepdims=True)
    gain_part = (gain_part + side_ref[:, 64:65]) / gain
    shift_part = shift_part + side_ref[:, 65:66]
    turn_ref[...] = jnp.zeros_like(turn_ref)
    turn_ref[64:80] = small_grad_ref[...]
    turn_ref[pl.ds(69 + group_index(), 1)] = bias_grad_ref[...]
    lane = lanes_of((width, LANES))
    last = jnp.where(lane < 64, grad[:, wide - LANES :], turn_ref[...].T)
    last = jnp.where(lane == 64, gain_part, jnp.where(lane == 65, shift_part, last))
    g_ref[:, : wide - LANES] = grad[:, : wide - LANES].astype(bf16)
    g_ref[:, wide - LANES :] = last.astype(bf16)
    store_pieces(g_ref, even, odd, sems)


def second_grad(parts, first, weights, side, small_grad, bias_grad, dp_size, gates=()):
    total, width = first.shape
    wide = parts[0].shape[1]
    piece = jax.ShapeDtypeStruct((dp_size // 2, width // dp_size, wide), bf16)
    return launch(
        second_grad_kernel,
        gates,
        cost=5.0,
        out_shape=(piece, piece),
        in_specs=[whole()] * 9,
        out_specs=[whole(pl.ANY)] * 2,
        scratch_shapes=[
            pltpu.VMEM((total, wide), bf16),
            pltpu.VMEM((width, wide), bf16),
            pltpu.VMEM((LANES, width), f32),
            pltpu.SemaphoreType.DMA((dp_size,)),
        ],
    )(*parts, first, weights, side, small_grad, bias_grad)


def part_kernel(*refs):
    ones, twos, weights = refs[:4], refs[4:8], refs[8][...]
    cut = ones[0].shape[1]
    for d in range(GROUP):
        part = mm_nt(ones[d][...], weights[:, :cut]) + mm_nt(twos[d][...], weights[:, cut:])
        refs[9 + d][...] = part.astype(bf16)


def input_parts(ones, twos, weights, gates=()):
    row_count, width = ones[0].shape[0], weights.shape[0]
    return launch(
        part_kernel,
        gates,
        cost=5.0,
        out_shape=[jax.ShapeDtypeStruct((row_count, width), bf16)] * GROUP,
        in_specs=[whole()] * 9,
        out_specs=[whole()] * GROUP,
    )(*ones, *twos, weights)


def last_kernel(token_ref, one_ref, two_ref, three_ref, dmixed_ref, small_ref, out_ref):
    unit, inverse = norm_parts(token_ref[...].astype(f32))
    df = one_ref[...].astype(f32) + two_ref[...].astype(f32) + three_ref[...].astype(f32)
    back = norm_back(df * small_ref[0:1], unit, inverse)
    out_ref[...] = (dmixed_ref[...] + back).astype(bf16)


def finish_input(tokens, parts, dmixed, small, gates=()):
    return launch(
        last_kernel,
        gates,
        cost=4.0,
        out_shape=jax.ShapeDtypeStruct(tokens.shape, bf16),
        in_specs=[whole()] * 6,
        out_specs=whole(),
    )(tokens, *parts, dmixed, small)


def place_ffn_kernel(*refs):
    shares, in_ref, down_ref = refs[:4], refs[4], refs[5]
    rows, ff = in_ref.shape
    width = down_ref.shape[1]
    low = group_index()
    for case in range(GROUP):

        @pl.when(low == case)
        def _():
            for d in range(GROUP):
                whose = case ^ d
                down_ref[rows * whose : rows * (whose + 1)] = shares[d][:, width:].astype(f32)
                part = shares[d][:, :width].astype(f32)
                for i in range(width // rows):
                    at = 4 * rows * i + rows * whose
                    in_ref[:, at : at + rows] = part[:, rows * i : rows * (i + 1)]


def place_ffn(shares, gates=()):
    rows, wide = shares[0].shape
    width = wide // 2
    return launch(
        place_ffn_kernel,
        gates,
        cost=3.0,
        out_shape=(
            jax.ShapeDtypeStruct((rows, 4 * width), f32),
            jax.ShapeDtypeStruct((4 * rows, width), f32),
        ),
        in_specs=[whole()] * 4,
        out_specs=[whole()] * 2,
    )(*shares)


def place_qkv_kernel(*refs):
    ones, twos, qkv_ref, out_ref, small_ref = refs[:4], refs[4:8], refs[8], refs[9], refs[10]
    width = out_ref.shape[1]
    low = group_index()
    vectors = twos[0][:, 128:].astype(f32)
    for d in range(1, GROUP):
        vectors = vectors + twos[d][:, 128:].astype(f32)
    small_ref[...] = vectors.T[64:80]
    for case in range(GROUP):

        @pl.when(low == case)
        def _():
            for d in range(GROUP):
                whose = case ^ d
                one, two = ones[d][...].astype(f32), twos[d][...].astype(f32)

                def put(kind, h, part):
                    at = kind * width + 192 * whose + 64 * h
                    qkv_ref[:, at : at + 64] = part

                for h in range(2):
                    put(0, h, one[:, LANES * h : LANES * h + 64])
                    put(1, h, one[:, LANES * h + 64 : LANES * h + LANES])
                    put(2, h, one[:, 2 * LANES + 64 * h : 2 * LANES + 64 * h + 64])
                for kind in range(3):
                    put(kind, 2, two[:, 64 * kind : 64 * kind + 64])
                if 256 * whose < width:
                    out_ref[:, 256 * whose : 256 * whose + 256] = one[:, 3 * LANES :]


def place_qkv(ones, twos, width, gates=()):
    rows = ones[0].shape[0]
    return launch(
        place_qkv_kernel,
        gates,
        cost=2.0,
        out_shape=(
            jax.ShapeDtypeStruct((rows, 3 * width), f32),
            jax.ShapeDtypeStruct((rows, width), f32),
            jax.ShapeDtypeStruct((16, rows), f32),
        ),
        in_specs=[whole()] * 8,
        out_specs=[whole()] * 3,
    )(*ones, *twos)


def on_device(
    tokens,
    attn_gain,
    attn_shift,
    w_qkv,
    w_out,
    ffn_gain,
    ffn_shift,
    w_in,
    b_in,
    w_down,
    b_down,
    cotangent,
    lengths,
    block_order,
):
    mine = tokens[0]
    row_count, width = mine.shape
    ctx_size = lax.axis_size("ctx")
    dp_size = lax.axis_size("dp")
    far = ctx_size // GROUP
    rows = w_qkv.shape[0]
    half = row_count // 2
    assert math.gcd(H, ctx_size) == GROUP and w_down.shape[0] == GROUP * rows
    where = (lengths, block_order)

    vectors = [attn_gain, attn_shift, ffn_gain, ffn_shift, b_down, b_in]
    piece = pack(w_qkv, vectors)
    far_qkv = far_pieces(piece, "qkv")
    tok_side = swap(mine, "ctx", 1, "tokens_core")
    tok_over = swap(mine, "ctx", 2, "tokens_x")
    piece_in, piece_down = pack_ffn(w_out, w_in, w_down, gates=(piece, tok_side))
    near_qkv = jnp.stack(far_qkv)
    cross_qkv = swap(near_qkv, "dp", 1, "qkv_y")
    tok_over = after(tok_over, near_qkv)
    blocks = [mine, tok_side, tok_over, swap(tok_over, "ctx", 1, "tokens_pass")]
    cot = cotangent[0]

    query, keys, values, first, small, qkv_weight = project(
        *where, blocks, near_qkv, cross_qkv
    )
    far_in = far_pieces(after(piece_in, near_qkv), "in")
    near_in = jnp.stack(far_in)
    held_cot = after(cot, query)
    cot_side = swap(held_cot, "ctx", 1, "cot_core")
    if far > 1:
        groups = [[g * GROUP + i for g in range(far)] for i in range(GROUP)]
        keys = lax.all_gather(keys, "ctx", axis=1, tiled=True, axis_index_groups=groups)
        values = lax.all_gather(values, "ctx", axis=1, tiled=True, axis_index_groups=groups)

    far_attn, far_query = attend(
        query, keys, values, 2, 2, row_count, gates=(near_in,)
    )
    cross_in = swap(near_in, "dp", 1, "in_y")
    cot_over = after(swap(held_cot, "ctx", 2, "cot_x"), far_attn)
    far_down = far_pieces(after(piece_down, near_in), "down")
    near_down = jnp.stack(far_down[:-1] + [after(far_down[-1], far_attn)])
    near_attn, near_query = attend(
        query, keys, values, 0, 2, row_count, gates=(far_attn, near_down, cot_over, cot_side)
    )
    cot_pass = swap(cot_over, "ctx", 1, "cot_pass")
    over_attn = swap(far_attn, "ctx", 2, "attn_x")
    cross_down = swap(near_down, "dp", 1, "down_y")
    held_in = after(cross_in, near_attn)
    out_piece = jnp.concatenate([near_in[:, :, width:], held_in[:, :, width:]])
    out_pieces = [out_piece, swap(out_piece, "ctx", 1, "out_core")]
    core_attn = swap(jnp.stack([near_attn[1], over_attn[1]]), "ctx", 1, "attn_core")
    attn = [near_attn, core_attn, over_attn]

    mixed, second, w_o = project_out(
        mine, attn, out_pieces, small, gates=(cross_down, cot_pass)
    )
    side = swap(second, "ctx", 1, "second_core")
    cots = [cot, cot_side, cot_over, cot_pass]
    (own_part, side_part), weights = feed_forward(
        *where,
        small,
        [second, side],
        cots[:2],
        [near_in, held_in, near_down, cross_down],
        (0, 1),
    )
    outs_near = out_parts([own_part[1], side_part[1]], weights[1])
    over = after(swap(second, "ctx", 2, "second_x"), outs_near[0])
    ds_side = swap(side_part[0], "ctx", 1, "ds_core")
    (over_part,), _ = feed_forward(
        *where, small, [over], cots[2:3], weights, (2,), gates=(outs_near[0], ds_side)
    )
    cross = after(swap(over, "ctx", 1, "second_pass"), over_part[0])
    (cross_part,), _ = feed_forward(*where, small, [cross], cots[3:], weights, (3,))
    parts = [own_part, side_part, over_part, cross_part]
    ds_sum = add(over_part[0], swap(cross_part[0], "ctx", 1, "ds_side"))
    even_ff, odd_ff, bias_grad = ffn_grads(
        *where,
        cots,
        [second, side, over, cross],
        [part[1] for part in parts],
        [part[2] for part in parts],
        dp_size,
        gates=(ds_sum,),
    )
    outs_far = out_parts([over_part[1], cross_part[1]], weights[1], gates=(even_ff,))
    ds_over = swap(ds_sum, "ctx", 2, "ds_x")
    outs_own, outs_one = outs_near
    outs_two, outs_three = outs_far
    dmixed, small_grad, dattn, out_blocks = mixed_back(
        *where,
        mixed,
        cot,
        small,
        w_o,
        attn,
        [own_part[0], ds_side, ds_over],
        gates=(outs_two,),
    )
    dattn_side = swap(dattn[1], "ctx", 1, "dattn_core")
    odd_sent = swap(odd_ff, "dp", 1, "ffn_y")
    outs_side = swap(after(outs_one, dmixed), "ctx", 1, "outs_core")
    outs_back = swap(after(outs_three, dmixed), "ctx", 1, "outs_side")

    def blocks_sum(*gates):
        one, three = after(out_blocks[1], *gates), after(out_blocks[3], *gates)
        own = add(out_blocks[0], swap(one, "ctx", 1, "dw_out_core"))
        across = add(out_blocks[2], swap(three, "ctx", 1, "dw_out_side"))
        return own, across

    if far > 1:
        over = swap(dattn[2], "ctx", 2, "dattn_x")
        dattn = [dattn[0], dattn_side, over[0], swap(over[1], "ctx", 1, "dattn_pass")]
        ffn_even = add(even_ff, odd_sent)
        dk, dv, dq = attend_back(
            [near_query, far_query],
            keys,
            values,
            [near_attn, far_attn],
            dattn,
            (0, 1, 2),
            (0, 1, 2, 3),
            "raw",
            (),
        )
        dk, dv = (
            lax.psum_scatter(v, "ctx", scatter_dimension=1, tiled=True, axis_index_groups=groups)
            for v in (dk, dv)
        )
        dq, dk, dv = (v[..., :64].astype(bf16) for v in (dq, dk, dv))
        one = jnp.concatenate([dq[0], dk[0], dq[1], dk[1], dv[0], dv[1]], axis=1)
        two = jnp.concatenate([dq[2], dk[2], dv[2], jnp.zeros_like(dv[2])], axis=1)
        ones = [one[d * row_count : (d + 1) * row_count] for d in range(GROUP)]
        twos = [two[d * row_count : (d + 1) * row_count] for d in range(GROUP)]
        begun = (dq, dk, dv)
        own_block, across_block = blocks_sum()
    else:
        begun = attend_back(
            [near_query],
            keys,
            values,
            [near_attn],
            [dattn[0], dattn_side],
            (0, 1),
            (0, 1),
            "begin",
            (),
        )
        over = after(swap(dattn[2], "ctx", 2, "dattn_x"), begun[0])
        dattn = [dattn[0], dattn_side, over[0], swap(over[1], "ctx", 1, "dattn_pass")]
        ffn_even = add(even_ff, after(odd_sent, begun[0], outs_side, outs_back))
        own_block, across_block = blocks_sum(over)
        ones = attend_back(
            [far_query],
            keys,
            values,
            [far_attn],
            dattn[2:],
            (0, 1),
            (2, 3),
            "final",
            begun,
            gates=(ffn_even, own_block, across_block),
        )
    out_block = (own_block, after(swap(across_block, "ctx", 2, "dw_out_x"), ones[0]))
    ffn_share = scatter_far(ffn_even, "ffn", ones[0])

    even, odd, part_sums = first_grad(
        ones, first, qkv_weight, out_block, dp_size, gates=(ffn_share[0],)
    )
    if far == 1:
        twos = attend_back(
            [near_query, far_query],
            keys,
            values,
            [near_attn, far_attn],
            dattn,
            (2,),
            (0, 1, 2, 3),
            "final",
            (),
            gates=(even,),
        )
    outs_over = after(swap(add(outs_two, outs_back), "ctx", 2, "outs_x"), twos[0])
    ffn_share = ffn_share[1](twos[0])
    one_even = add(even, after(swap(odd, "dp", 1, "one_y"), twos[0]))
    parts = input_parts(ones, twos, qkv_weight, gates=(one_even, ffn_share, outs_over))
    one_share = scatter_far(one_even, "one", parts[0])
    even, odd = second_grad(
        twos,
        first,
        qkv_weight,
        part_sums,
        small_grad,
        bias_grad,
        dp_size,
        gates=(one_share[0],),
    )
    part_back = swap(parts[3], "ctx", 1, "df_side")
    part_over = swap(add(parts[2], part_back), "ctx", 2, "df_x")
    part_side = swap(parts[1], "ctx", 1, "df_core")
    two_even = add(even, swap(odd, "dp", 1, "two_y"))
    one_share = one_share[1](even)
    layer_out = finish_out(
        *where, mixed, small, [outs_own, outs_side, outs_over], gates=(even,)
    )
    two_share = scatter_far(two_even, "two", None)
    one_shares = gather_group(sum_groups(one_share), "one", layer_out)
    ffn_shares = gather_group(sum_groups(after(ffn_share, two_share[0])), "ffn", layer_out)
    two_share = two_share[1](None)
    grad_w_in, grad_w_down = place_ffn(ffn_shares, gates=(layer_out,))
    two_shares = gather_group(sum_groups(two_share), "two")
    input_grad = finish_input(mine, [parts[0], part_side, part_over], dmixed, small)
    grad_w_qkv, grad_w_out, vector_grads = place_qkv(one_shares, two_shares, width)
    return (
        layer_out[None],
        input_grad[None],
        vector_grads[0],
        vector_grads[1],
        grad_w_qkv,
        grad_w_out,
        vector_grads[2],
        vector_grads[3],
        grad_w_in,
        vector_grads[5:9].reshape(-1),
        grad_w_down,
        vector_grads[4],
    )


def solution(mesh):
    placed = (
        P("dp", "ctx", None),
        P("dp"),
        P("dp"),
        P("dp", None),
        P("dp", None),
        P("dp"),
        P("dp"),
        P("dp", None),
        P("dp"),
        P("dp", None),
        P("dp"),
        P("dp", "ctx", None),
        P("dp"),
        P("dp", None),
    )
    return jax.shard_map(
        on_device,
        mesh=mesh,
        in_specs=placed,
        out_specs=(
            P("dp", "ctx", None),
            P("dp", "ctx", None),
            P("dp"),
            P("dp"),
            P("dp", None),
            P("dp", None),
            P("dp"),
            P("dp"),
            P("dp", None),
            P("dp"),
            P("dp", None),
            P("dp"),
        ),
        check_vma=False,
    )
```

```python
import functools
import math

import jax
import jax.numpy as jnp
from jax import lax
from jax.experimental import pallas as pl
from jax.experimental.pallas import tpu as pltpu
from jax.sharding import PartitionSpec as P

H = 12

epsilon = 1e-05
gelu_coeff = 0.7978845608
cubic_term = 0.044715
excluded = -1073741824.0
bf16 = jnp.bfloat16
f32 = jnp.float32
LANES = 128
GROUP = 4
VMEM_SMALL = 16 * 1024 * 1024
VMEM_LARGE = 52 * 1024 * 1024
VMEM_MOST = 62 * 1024 * 1024

nt_dims = (((1,), (1,)), ((), ()))
tn_dims = (((0,), (0,)), ((), ()))


def mm(left, right):
    return jnp.dot(left, right, preferred_element_type=f32)


def mm_nt(left, right):
    return lax.dot_general(left, right, nt_dims, preferred_element_type=f32)


def mm_tn(left, right):
    return lax.dot_general(left, right, tn_dims, preferred_element_type=f32)


def whole(memory_space=pltpu.VMEM):
    return pl.BlockSpec(memory_space=memory_space)


def lanes_of(shape):
    return lax.broadcasted_iota(jnp.int32, shape, 1)


def norm_parts(values):
    center = values - jnp.mean(values, axis=-1, keepdims=True)
    spread = jnp.mean(center * center, axis=-1, keepdims=True)
    inverse = lax.rsqrt(spread + epsilon)
    return center * inverse, inverse


def norm_back(scaled, unit, inverse):
    return inverse * (
        scaled
        - jnp.mean(scaled, axis=-1, keepdims=True)
        - unit * jnp.mean(scaled * unit, axis=-1, keepdims=True)
    )


def three_parts(value):
    first = value.astype(bf16).astype(f32)
    rest = value - first
    second = rest.astype(bf16).astype(f32)
    return first, second, rest - second


def with_parts(base, value):
    lane = lanes_of(base.shape)
    one, two, three = three_parts(value)
    return jnp.where(
        lane == 64, one, jnp.where(lane == 65, two, jnp.where(lane == 66, three, base))
    )


def unpack_rows(packed, rows):
    tail = jnp.concatenate([packed[rows:, :64], packed[rows:, 64:]], axis=0)
    return packed[:rows], tail


def swap(value, axis, bit, name):
    size = lax.axis_size(axis)
    with jax.named_scope(name):
        return lax.ppermute(value, axis, [(i, i ^ bit) for i in range(size)])


def launch(kernel, gates, in_specs, cost=1.0, vmem=VMEM_SMALL, **options):
    count = len(gates)
    flops = int(cost * 2e7)

    def gated(*refs):
        kernel(*refs[count:])

    call = pl.pallas_call(
        gated,
        in_specs=[whole(pl.ANY)] * count + in_specs,
        compiler_params=pltpu.CompilerParams(vmem_limit_bytes=vmem),
        cost_estimate=pl.CostEstimate(flops=flops, bytes_accessed=1024, transcendentals=0),
        **options,
    )
    return lambda *operands: call(*gates, *operands)


def hold_kernel(value_ref, out_ref):
    pass


def after(value, *gates):
    return launch(
        hold_kernel,
        gates,
        [whole(pl.ANY)],
        out_shape=jax.ShapeDtypeStruct(value.shape, value.dtype),
        out_specs=whole(pl.ANY),
        input_output_aliases={len(gates): 0},
    )(value)


def far_pieces(piece, name):
    found = [piece]
    for k in range(1, lax.axis_size("dp") // 2):
        found.append(swap(piece, "dp", 2 * k, name + "_z"))
    return found


def add(left, right):
    return (left.astype(f32) + right.astype(f32)).astype(bf16)


def scatter_far(even, name, gate):
    def step(even, gate):
        half = even.shape[0] // 2
        bit = lax.axis_size("dp") // (2 * half)
        pairs = even.reshape(half, 2, *even.shape[1:])
        received = swap(pairs[:, 1], "dp", bit, name + "_z")
        return add(pairs[:, 0], received if gate is None else after(received, gate))

    begun = step(even, gate)

    def finish(start):
        total = begun if start is None else start
        while total.shape[0] > 1:
            total = step(total, None)
        return total[0]

    return begun, finish


def sum_groups(value):
    bit = GROUP
    while bit < lax.axis_size("ctx"):
        other = swap(value, "ctx", bit, "groups")
        value = (value.astype(f32) + other.astype(f32)).astype(bf16)
        bit *= 2
    return value


def gather_group(value, name, gate=None):
    over = swap(value, "ctx", 2, name + "_x")
    if gate is not None:
        over = after(over, gate)
    side = swap(value, "ctx", 1, name + "_core")
    return [value, side, over, swap(over, "ctx", 1, name + "_pass")]


def exchange_pairs(near, far, name, gate=None):
    over = swap(far, "ctx", 2, name + "_x")
    if gate is not None:
        over = after(over, gate)
    core = swap(jnp.stack([near[1], over[1]]), "ctx", 1, name + "_core")
    return [near, core, over]


def gather_pairs(value, name, gate=None):
    over = swap(value, "ctx", 2, name + "_x")
    if gate is not None:
        over = after(over, gate)
    pair = swap(jnp.stack([value, over]), "ctx", 1, name + "_core")
    return [value, pair[0], over, pair[1]]


def position_of(order_ref, slot, rows):
    index = lax.axis_index("ctx")
    return order_ref[0, lax.bitwise_xor(index, slot)] * rows


def valid_rows(length_ref, order_ref, slot, rows):
    stored = lax.broadcasted_iota(jnp.int32, (rows, LANES), 0)[:, :1]
    position = position_of(order_ref, slot, rows) + stored
    return jnp.where(position < length_ref[0], 1.0, 0.0)


def group_index():
    return lax.rem(lax.axis_index("ctx"), GROUP)


def load_pieces(sources, target, sems, first_sem=0):
    me = lax.axis_index("dp")
    copies = []
    for source, differences in sources:
        rows = source.shape[1]
        for k, difference in enumerate(differences):
            owner = lax.bitwise_xor(me, difference)
            copies.append(
                pltpu.make_async_copy(
                    source.at[k],
                    target.at[pl.ds(pl.multiple_of(owner * rows, 16), rows)],
                    sems.at[first_sem + len(copies)],
                )
            )
    for copy in copies:
        copy.start()
    return copies


def near_and_cross(near, cross):
    halves = near.shape[0]
    return [(near, [2 * k for k in range(halves)]), (cross, [2 * k + 1 for k in range(halves)])]


def store_pieces(source, even, odd, sems):
    halves, rows, _ = even.shape
    me = lax.axis_index("dp")
    copies = []
    for parity, target in ((0, even), (1, odd)):
        for k in range(halves):
            owner = lax.bitwise_xor(me, 2 * k + parity)
            copies.append(
                pltpu.make_async_copy(
                    source.at[pl.ds(pl.multiple_of(owner * rows, 16), rows)],
                    target.at[k],
                    sems.at[2 * k + parity],
                )
            )
    for copy in copies:
        copy.start()
    for copy in copies:
        copy.wait()


def pack_kernel(w_hbm, *refs):
    w_ref, sems = refs[-2:]
    count = (len(refs) - 3) // 2
    vectors, out_ref, held = refs[:count], refs[count], refs[count + 1 : -2]
    copies = [pltpu.make_async_copy(w_hbm, w_ref, sems.at[count])]
    for i in range(count):
        copies.append(pltpu.make_async_copy(vectors[i], held[i], sems.at[i]))
    for copy in copies:
        copy.start()
    for copy in copies:
        copy.wait()
    rows = w_ref.shape[0]
    width = w_ref.shape[1] // 3
    low = group_index()
    stacked = []
    for v in held:
        flat = v[...].astype(f32).reshape(1, v.shape[0])
        stacked += [flat[:, i : i + rows] for i in range(0, v.shape[0], rows)]
    stacked.append(jnp.zeros((LANES - len(stacked), rows), f32))
    small = jnp.concatenate(stacked, axis=0).T[:, :64].astype(bf16)
    for case in range(GROUP):

        @pl.when(low == case)
        def _():
            def head(kind, h):
                at = kind * width + 192 * case + 64 * h
                return w_ref[:, at : at + 64]

            out_ref[...] = jnp.concatenate(
                [
                    head(0, 0),
                    head(1, 0),
                    head(0, 1),
                    head(1, 1),
                    head(2, 0),
                    head(2, 1),
                    head(0, 2),
                    head(1, 2),
                    head(2, 2),
                    small,
                ],
                axis=1,
            )


def pack(w_qkv, vectors, gates=()):
    rows = w_qkv.shape[0]
    return launch(
        pack_kernel,
        gates,
        vmem=VMEM_MOST,
        cost=1.0,
        out_shape=jax.ShapeDtypeStruct((rows, 640), bf16),
        in_specs=[whole(pltpu.HBM)] * (1 + len(vectors)),
        out_specs=whole(),
        scratch_shapes=[pltpu.VMEM(v.shape, bf16) for v in vectors]
        + [pltpu.VMEM(w_qkv.shape, bf16), pltpu.SemaphoreType.DMA((1 + len(vectors),))],
    )(w_qkv, *vectors)


def pack_ffn_kernel(out_ref, in_ref, down_ref, one_ref, two_ref):
    rows, ff = in_ref.shape
    width = out_ref.shape[1]
    half = width // 2
    low = group_index()
    per = 4 * rows
    for case in range(GROUP):

        @pl.when(low == case)
        def _():
            at = half * (case % 2)
            parts = [
                in_ref[:, per * i + rows * case : per * i + rows * (case + 1)]
                for i in range(ff // per)
            ]
            one_ref[:, :width] = jnp.concatenate(parts, axis=1)
            one_ref[:, width:] = out_ref[:, at : at + half]
            two_ref[...] = down_ref[rows * case : rows * (case + 1)]


def pack_ffn(w_out, w_in, w_down, gates=()):
    rows, width = w_out.shape
    return launch(
        pack_ffn_kernel,
        gates,
        cost=1.0,
        out_shape=(
            jax.ShapeDtypeStruct((rows, width + width // 2), bf16),
            jax.ShapeDtypeStruct((rows, width), bf16),
        ),
        in_specs=[whole()] * 3,
        out_specs=[whole()] * 2,
    )(w_out, w_in, w_down)


def qkv_kernel(length_ref, order_ref, *refs):
    tokens = refs[:GROUP]
    near, cross = refs[GROUP : GROUP + 2]
    q_ref, k_ref, v_ref, first_ref, small_ref, w_ref, w_two_ref, sems = refs[GROUP + 2 :]
    row_count, width = tokens[0].shape
    for copy in load_pieces(near_and_cross(near, cross), w_ref, sems):
        copy.wait()
    w_two_ref[...] = w_ref[:, 384:640]
    small = w_ref[:, 512:640].astype(f32).T
    small_ref[...] = small[64:80]
    gain, shift = small[64:65], small[65:66]
    length = length_ref[0]
    lane = lanes_of((row_count, LANES))
    ones = jnp.where((lane >= 64) & (lane < 67), 1.0, 0.0)
    bias_lane = jnp.where(lane == 67, 1.0, 0.0)
    for d in range(GROUP):
        unit, _ = norm_parts(tokens[d][...].astype(f32))
        first = (unit * gain + shift).astype(bf16)
        part = pl.ds(d * row_count, row_count)
        first_ref[part] = first
        qkv = mm(first, w_ref[...]).astype(bf16).astype(f32)

        def head(place):
            block = qkv[:, place // 2 * LANES : (place // 2 + 1) * LANES]
            if place % 2:
                block = pltpu.roll(block, 64, 1)
            return jnp.where(lane < 64, block, 0.0)

        stored = lax.broadcasted_iota(jnp.int32, (row_count, LANES), 0)
        position = position_of(order_ref, d, row_count) + stored
        bias = jnp.where(position < length, 0.0, excluded) * bias_lane
        for h, (at_q, at_k, at_v) in enumerate(((0, 1, 4), (2, 3, 5), (6, 7, 8))):
            q_ref[h, part] = (head(at_q) * 0.125 + bias_lane).astype(bf16)
            k_ref[h, part] = (head(at_k) + ones + bias).astype(bf16)
            v_ref[h, part] = (head(at_v) + ones).astype(bf16)


def project(length, order, tokens, near, cross, gates=()):
    row_count, width = tokens[0].shape
    total = GROUP * row_count
    wide = near.shape[2]
    head_out = jax.ShapeDtypeStruct((3, total, LANES), bf16)
    return launch(
        qkv_kernel,
        gates,
        cost=10.0,
        out_shape=(
            head_out,
            head_out,
            head_out,
            jax.ShapeDtypeStruct((total, width), bf16),
            jax.ShapeDtypeStruct((16, width), f32),
            jax.ShapeDtypeStruct((width, wide), bf16),
            jax.ShapeDtypeStruct((width, 256), bf16),
        ),
        in_specs=[whole(pltpu.SMEM)] * 2 + [whole()] * GROUP + [whole(pl.ANY)] * 2,
        out_specs=[whole()] * 7,
        scratch_shapes=[pltpu.SemaphoreType.DMA((2 * near.shape[0],))],
    )(length, order, *tokens, near, cross)


def attend_kernel(block_rows, q_ref, k_ref, v_ref, packed_ref, q_out_ref):
    row_count = q_ref.shape[1]
    half = row_count // 2
    lane = lanes_of((block_rows, LANES))
    for i in range(row_count // block_rows):
        part = pl.ds(i * block_rows, block_rows)
        heads = []
        for h in range(3):
            query = q_ref[h, part]
            scores = mm_nt(query, k_ref[h])
            top = jnp.max(scores, axis=1, keepdims=True)
            weights = jnp.exp(scores - top).astype(bf16)
            result = mm(weights, v_ref[h])
            denom = result[:, 64:65]
            heads.append(jnp.where(lane < 64, result / denom, 0.0))
            log_total = top + jnp.log(denom)
            q_out_ref[h, part] = with_parts(query.astype(f32), -log_total).astype(bf16)
        packed_ref[0, part] = (heads[0] + pltpu.roll(heads[1], 64, 1)).astype(bf16)
        for r in range(0, block_rows, half):
            size = min(half, block_rows)
            row = i * block_rows + r
            side, place = row // half, row % half
            packed_ref[
                0, pl.ds(row_count + place, size), 64 * side : 64 * side + 64
            ] = heads[2][r : r + size, :64].astype(bf16)


def attend(query, keys, values, first_slot, slots, row_count, gates=()):
    total = keys.shape[1]
    block_rows = min(row_count // 2, 256)
    return launch(
        functools.partial(attend_kernel, block_rows),
        gates,
        cost=5.0 * slots,
        vmem=VMEM_LARGE if total > GROUP * row_count else VMEM_SMALL,
        grid=(slots,),
        out_shape=(
            jax.ShapeDtypeStruct((slots, row_count * 3 // 2, LANES), bf16),
            jax.ShapeDtypeStruct((3, slots * row_count, LANES), bf16),
        ),
        in_specs=[
            pl.BlockSpec((3, row_count, LANES), lambda s: (0, s + first_slot, 0)),
            whole(),
            whole(),
        ],
        out_specs=(
            pl.BlockSpec((1, row_count * 3 // 2, LANES), lambda s: (s, 0, 0)),
            pl.BlockSpec((3, row_count, LANES), lambda s: (0, s, 0)),
        ),
    )(query, keys, values)


def group_attn(refs, row_count):
    near, core, over = refs
    packed = (near[0], core[0], over[0], core[1])
    return [jnp.concatenate(unpack_rows(v, row_count), axis=1) for v in packed]


def out_kernel(token_ref, *refs):
    attn_refs, pieces = refs[:3], refs[3:5]
    small_ref, mixed_ref, second_ref, w_o, sems = refs[5:]
    row_count, width = token_ref.shape
    half = width // 2
    number = pieces[0].shape[0]
    low = group_index()
    core = lax.rem(low, 2)
    differences = [2 * k for k in range(number // 2)] + [2 * k + 1 for k in range(number // 2)]
    copies = []
    for side in range(2):
        column = pl.multiple_of((core if side == 0 else 1 - core) * half, LANES)
        target = w_o.at[:, pl.ds(column, half)]
        copies += load_pieces([(pieces[side], differences)], target, sems, side * number)
    mixed = token_ref[...].astype(f32)
    attn = group_attn(attn_refs, row_count)
    for copy in copies:
        copy.wait()
    for d in range(GROUP):
        at = pl.ds(pl.multiple_of(lax.bitwise_xor(low, d) * 192, 16), 192)
        mixed = mixed + mm(attn[d], w_o[at, :])
    mixed_ref[...] = mixed
    unit, _ = norm_parts(mixed)
    second_ref[...] = (unit * small_ref[2:3] + small_ref[3:4]).astype(bf16)


def project_out(tokens, attn, pieces, small, gates=()):
    row_count, width = tokens.shape
    number = pieces[0].shape[0]
    return launch(
        out_kernel,
        gates,
        cost=4.5,
        out_shape=(
            jax.ShapeDtypeStruct((row_count, width), f32),
            jax.ShapeDtypeStruct((row_count, width), bf16),
            jax.ShapeDtypeStruct((width, width), bf16),
        ),
        in_specs=[whole()] * 4 + [whole(pl.ANY)] * 2 + [whole()],
        out_specs=[whole()] * 3,
        scratch_shapes=[pltpu.SemaphoreType.DMA((2 * number,))],
    )(tokens, *attn, *pieces, small)


def ffn_kernel(slots, gathers, length_ref, order_ref, small_ref, *refs):
    number = len(slots)
    seconds, cots = refs[:number], refs[number : 2 * number]
    refs = refs[2 * number :]
    count = 4 if gathers else 2
    sources, refs = refs[:count], refs[count:]
    outs = [refs[3 * i : 3 + 3 * i] for i in range(number)]
    refs = refs[3 * number :]
    rows, width = seconds[0].shape
    if gathers:
        w_i, w_d, sems = refs
        near, cross, near_down, cross_down = sources
        parts = near_and_cross(*(v.at[:, :, pl.ds(0, width)] for v in (near, cross)))
        in_copies = load_pieces(parts, w_i, sems)
        down_copies = load_pieces(near_and_cross(near_down, cross_down), w_d, sems, 2 * gathers)
        for copy in in_copies:
            copy.wait()
    else:
        w_i, w_d = sources
    bias = small_ref[pl.ds(5 + group_index(), 1)]
    for i, slot in enumerate(slots):
        ds_ref, active_ref, dhid_ref = outs[i]
        row_count = cots[i].shape[0]
        valid = valid_rows(length_ref, order_ref, slot, row_count)
        dlow = (cots[i][...].astype(f32) * valid).astype(bf16)
        hidden = mm(seconds[i][...], w_i[...]) + bias
        squared = hidden * hidden
        bent = jnp.tanh(hidden * (gelu_coeff + gelu_coeff * cubic_term * squared))
        plus = 0.5 + 0.5 * bent
        slope = plus + hidden * (plus * (1.0 - bent)) * (
            gelu_coeff + gelu_coeff * 3.0 * cubic_term * squared
        )
        active_ref[...] = (hidden * plus).astype(bf16)
        if gathers and i == 0:
            for copy in down_copies:
                copy.wait()
        dhid = (mm_nt(dlow, w_d[...]) * slope).astype(bf16)
        dhid_ref[...] = dhid
        ds_ref[...] = mm_nt(dhid, w_i[...]).astype(bf16)


def feed_forward(length, order, small, seconds, cots, weights, slots, gates=()):
    rows, width = seconds[0].shape
    gathers = weights[0].shape[0] if len(weights) == 4 else 0
    number = len(slots)
    block = jax.ShapeDtypeStruct((rows, width), bf16)
    square = jax.ShapeDtypeStruct((width, width), bf16)
    results = launch(
        functools.partial(ffn_kernel, slots, gathers),
        gates,
        cost=3.0 * number,
        out_shape=[block] * (3 * number) + [square] * (2 if gathers else 0),
        in_specs=[whole(pltpu.SMEM)] * 2
        + [whole()] * (1 + 2 * number)
        + [whole(pl.ANY) if gathers else whole()] * len(weights),
        out_specs=[whole()] * (3 * number + (2 if gathers else 0)),
        scratch_shapes=[pltpu.SemaphoreType.DMA((4 * gathers,))] if gathers else [],
    )(length, order, small, *seconds, *cots, *weights)
    grouped = [results[3 * i : 3 * i + 3] for i in range(number)]
    return grouped, results[3 * number :]


def out_part_kernel(*refs):
    w_d = refs[2][...]
    for i in range(2):
        refs[3 + i][...] = mm(refs[i][...], w_d).astype(bf16)


def out_parts(actives, w_down, gates=()):
    return launch(
        out_part_kernel,
        gates,
        cost=2.0,
        out_shape=[jax.ShapeDtypeStruct(v.shape, bf16) for v in actives],
        in_specs=[whole()] * 3,
        out_specs=[whole()] * 2,
    )(*actives, w_down)


def ffn_grad_kernel(length_ref, order_ref, *refs):
    cots, seconds, actives, dhids = (refs[i : i + GROUP] for i in range(0, 4 * GROUP, GROUP))
    even, odd, bias_ref, g_ref, sems = refs[4 * GROUP :]
    row_count, width = cots[0].shape
    bias = jnp.zeros((1, width), f32)
    grad_in = jnp.zeros((width, width), f32)
    for d in range(GROUP):
        dhid = dhids[d][...]
        bias = bias + jnp.sum(dhid.astype(f32), axis=0, keepdims=True)
        grad_in = grad_in + mm_tn(seconds[d][...], dhid)
    g_ref[:, :width] = grad_in.astype(bf16)
    bias_ref[...] = bias
    grad_down = jnp.zeros((width, width), f32)
    for d in range(GROUP):
        valid = valid_rows(length_ref, order_ref, d, row_count)
        dlow = (cots[d][...].astype(f32) * valid).astype(bf16)
        grad_down = grad_down + mm_tn(actives[d][...], dlow)
    g_ref[:, width:] = grad_down.astype(bf16)
    store_pieces(g_ref, even, odd, sems)


def ffn_grads(length, order, cots, seconds, actives, dhids, dp_size, gates=()):
    width = cots[0].shape[1]
    halves = dp_size // 2
    piece = jax.ShapeDtypeStruct((halves, width // dp_size, 2 * width), bf16)
    return launch(
        ffn_grad_kernel,
        gates,
        cost=7.0,
        out_shape=(piece, piece, jax.ShapeDtypeStruct((1, width), f32)),
        in_specs=[whole(pltpu.SMEM)] * 2 + [whole()] * (4 * GROUP),
        out_specs=[whole(pl.ANY)] * 2 + [whole()],
        scratch_shapes=[
            pltpu.VMEM((width, 2 * width), bf16),
            pltpu.SemaphoreType.DMA((dp_size,)),
        ],
    )(length, order, *cots, *seconds, *actives, *dhids)


def mixed_back_kernel(length_ref, order_ref, *refs):
    mixed_ref, cot_ref, small_ref, w_o = refs[:4]
    attn_refs = refs[4:7]
    ds_refs = refs[7:10]
    dmixed_ref, small_grad_ref = refs[10:12]
    own, side, over = refs[12:15]
    dattn_refs = (own, side, over.at[0], over.at[1])
    half_refs = refs[15:17]
    g_o = refs[17]
    row_count, width = mixed_ref.shape
    half = row_count // 2
    low = group_index()
    unit, inverse = norm_parts(mixed_ref[...])
    ds = sum(v[...].astype(f32) for v in ds_refs)
    valid = valid_rows(length_ref, order_ref, 0, row_count)
    dout = cot_ref[...].astype(f32) * valid
    dmixed = dout + norm_back(ds * small_ref[2:3], unit, inverse)
    dmixed_ref[...] = dmixed
    dbranch = dmixed.astype(bf16)

    def out_rows(d):
        return pl.ds(pl.multiple_of(lax.bitwise_xor(low, d) * 192, 16), 192)

    for d in range(GROUP):
        dattn = mm_nt(dbranch, w_o[out_rows(d), :])
        dattn_refs[d][pl.ds(0, row_count)] = dattn[:, :LANES].astype(bf16)
        dattn_refs[d][pl.ds(row_count, half), :64] = dattn[:half, LANES:].astype(bf16)
        dattn_refs[d][pl.ds(row_count, half), 64:] = dattn[half:, LANES:].astype(bf16)
    attn = group_attn(attn_refs, row_count)
    for d in range(GROUP):
        g_o[out_rows(d), :] = mm_tn(attn[d], dbranch).astype(bf16)
    core = lax.rem(low, 2)
    for here, half_ref in zip((core, 1 - core), half_refs):
        column = pl.multiple_of(here * (width // 2), LANES)
        half_ref[...] = g_o[:, pl.ds(column, width // 2)]
    small_grad_ref[...] = jnp.zeros_like(small_grad_ref)
    small_grad_ref[2:3] = jnp.sum(ds * unit, axis=0, keepdims=True)
    small_grad_ref[3:4] = jnp.sum(ds, axis=0, keepdims=True)
    small_grad_ref[4:5] = jnp.sum(dout, axis=0, keepdims=True)


def mixed_back(length, order, mixed, cot, small, w_o, attn, ds, gates=()):
    row_count, width = mixed.shape
    results = launch(
        mixed_back_kernel,
        gates,
        cost=7.0,
        out_shape=[
            jax.ShapeDtypeStruct((row_count, width), f32),
            jax.ShapeDtypeStruct((16, width), f32),
        ]
        + [jax.ShapeDtypeStruct((row_count * 3 // 2, LANES), bf16)] * 2
        + [jax.ShapeDtypeStruct((2, row_count * 3 // 2, LANES), bf16)]
        + [jax.ShapeDtypeStruct((width, width // 2), bf16)] * 2,
        in_specs=[whole(pltpu.SMEM)] * 2 + [whole()] * 10,
        out_specs=[whole()] * 7,
        scratch_shapes=[pltpu.VMEM((width, width), bf16)],
    )(length, order, mixed, cot, small, w_o, *attn, *ds)
    return results[0], results[1], results[2:5], results[5:7]


def layer_out_kernel(length_ref, order_ref, mixed_ref, small_ref, *refs):
    own, side, over, out_ref = refs
    row_count = mixed_ref.shape[0]
    valid = valid_rows(length_ref, order_ref, 0, row_count)
    total = mixed_ref[...] + own[...].astype(f32) + side[...].astype(f32) + over[...].astype(f32)
    out_ref[...] = ((total + small_ref[4:5]) * valid).astype(bf16)


def finish_out(length, order, mixed, small, parts, gates=()):
    return launch(
        layer_out_kernel,
        gates,
        cost=3.0,
        out_shape=jax.ShapeDtypeStruct(mixed.shape, bf16),
        in_specs=[whole(pltpu.SMEM)] * 2 + [whole()] * 5,
        out_specs=whole(),
    )(length, order, mixed, small, *parts)


def attend_back_kernel(mode, heads, slots, row_count, starts, *refs):
    number = len(slots)
    pairs = number // 2
    q_refs, (k_ref, v_ref) = refs[:pairs], refs[pairs : pairs + 2]
    refs = refs[pairs + 2 :]
    attn_refs, dattn_refs = refs[:pairs], refs[pairs : pairs + number]
    refs = refs[pairs + number :]
    if starts:
        dk_in, dv_in, dq_in = refs[:3]
        refs = refs[3:]
    outs = refs[:-5]
    grad_ref, k_turned, dq_ref, dk_ref, dv_ref = refs[-5:]
    head, step = pl.program_id(0), pl.program_id(1)
    total = k_ref.shape[1]
    chunk = row_count
    first_slot = slots[0] if mode == "final" else 0

    @pl.when((head == 0) & (step == 0))
    def _():
        lane = lanes_of((row_count, LANES))
        for d in range(number):
            top, tail = unpack_rows(dattn_refs[d][...].astype(f32), row_count)
            top_a, tail_a = unpack_rows(attn_refs[d // 2][d % 2].astype(f32), row_count)
            product = top * top_a
            for i, h in enumerate(heads):
                if h == 0:
                    block = top
                    delta = jnp.sum(jnp.where(lane < 64, product, 0.0), axis=1, keepdims=True)
                elif h == 1:
                    block = pltpu.roll(top, 64, 1)
                    delta = jnp.sum(jnp.where(lane >= 64, product, 0.0), axis=1, keepdims=True)
                else:
                    block = jnp.concatenate([tail, tail], axis=1)
                    delta = jnp.sum(tail * tail_a, axis=1, keepdims=True)
                base = jnp.where(lane < 64, block, 0.0)
                grad_ref[i, pl.ds(d * row_count, row_count)] = with_parts(base, -delta).astype(bf16)

    @pl.when(step == 0)
    def _():
        k_turned[...] = k_ref[0].astype(f32).T.astype(bf16)
        if starts:
            dk_ref[...] = dk_in[0]
            dv_ref[...] = dv_in[0]
            dq_ref[: first_slot * row_count] = dq_in[0]
        else:
            dk_ref[...] = jnp.zeros_like(dk_ref)
            dv_ref[...] = jnp.zeros_like(dv_ref)

    query = q_refs[0][0]
    if pairs > 1:
        query = jnp.where(step < 2, query, q_refs[1][0])
    grad = grad_ref[head, pl.ds(pl.multiple_of(step * row_count, row_count), row_count)]
    turned = jnp.zeros((LANES, row_count), f32)
    for c in range(total // chunk):
        at = pl.ds(c * chunk, chunk)
        probs = jnp.exp(mm_nt(k_ref[0, at], query))
        dscores = (probs * mm_nt(v_ref[0, at], grad)).astype(bf16)
        dv_ref[at] += mm(probs.astype(bf16), grad)
        dk_ref[at] += mm(dscores, query)
        turned = turned + mm(k_turned[:, at], dscores)
    place = pl.multiple_of((first_slot + step) * row_count, row_count)
    dq_ref[pl.ds(place, row_count)] = turned.T * 0.125

    @pl.when(step == number - 1)
    def _():
        if mode != "final":
            outs[0][0] = dk_ref[...]
            outs[1][0] = dv_ref[...]
            outs[2][0] = dq_ref[...]
            return
        lane = lanes_of((row_count, LANES))
        last_at = LANES * len(heads)
        for i in range(len(heads)):

            @pl.when(head == i)
            def _():
                for d in range(GROUP):
                    at = pl.ds(d * row_count, row_count)
                    pair = jnp.where(lane < 64, dq_ref[at], pltpu.roll(dk_ref[at], 64, 1))
                    out = outs[d // 2].at[d % 2]
                    out[:, i * LANES : (i + 1) * LANES] = pair.astype(bf16)
                    value = dv_ref[at]
                    if i == 0:
                        value = jnp.where(lane < 64, value, 0.0)
                        out[:, last_at : last_at + LANES] = value.astype(bf16)
                    else:
                        out[:, last_at + 64 : last_at + LANES] = value[:, :64].astype(bf16)


def attend_back(queries, keys, values, attn, dattn, heads, slots, mode, begun, gates=()):
    row_count = dattn[0].shape[0] * 2 // 3
    total = keys.shape[1]
    number = len(slots)
    kept = GROUP if mode == "final" else number
    first_head = heads[0]
    if number == 2:
        places = [lambda h, s: (h + first_head, s, 0)]
    else:
        places = [
            lambda h, s: (h + first_head, jnp.minimum(s, 1), 0),
            lambda h, s: (h + first_head, jnp.maximum(s - 2, 0), 0),
        ]

    def per_head(size):
        return (
            jax.ShapeDtypeStruct((len(heads), size, LANES), f32),
            pl.BlockSpec((1, size, LANES), lambda h, s: (h, 0, 0)),
        )

    if mode == "final":
        wide = LANES * (len(heads) + 1)
        outs = [
            (
                jax.ShapeDtypeStruct((2, row_count, wide), bf16),
                pl.BlockSpec((2, row_count, wide), lambda h, s: (0, 0, 0)),
            )
        ] * 2
    else:
        outs = [per_head(total), per_head(total), per_head(number * row_count)]
    begun_specs = []
    if begun:
        begun_specs = [
            pl.BlockSpec((1, v.shape[1], LANES), lambda h, s: (h, 0, 0)) for v in begun
        ]
    return launch(
        functools.partial(attend_back_kernel, mode, heads, slots, row_count, bool(begun)),
        gates,
        cost=3.2 * number * len(heads),
        vmem=VMEM_LARGE if total > GROUP * row_count else VMEM_SMALL,
        grid=(len(heads), number),
        out_shape=[shape for shape, _ in outs],
        out_specs=[spec for _, spec in outs],
        in_specs=[
            pl.BlockSpec((1, row_count, LANES), place) for place in places
        ]
        + [pl.BlockSpec((1, total, LANES), lambda h, s: (h + first_head, 0, 0))] * 2
        + [whole()] * (len(attn) + number)
        + begun_specs,
        scratch_shapes=[
            pltpu.VMEM((len(heads), number * row_count, LANES), bf16),
            pltpu.VMEM((LANES, total), bf16),
            pltpu.VMEM((kept * row_count, LANES), f32),
            pltpu.VMEM((total, LANES), f32),
            pltpu.VMEM((total, LANES), f32),
        ],
    )(*queries, keys, values, *attn, *dattn, *begun)


def first_grad_kernel(*refs):
    parts, first_ref, w_ref, block_refs = refs[:2], refs[2], refs[3], refs[4:6]
    even, odd, side_ref, d_ref, g_ref, sems = refs[6:]
    _, row_count, wide = parts[0].shape
    for d in range(GROUP):
        d_ref[d * row_count : (d + 1) * row_count] = parts[d // 2][d % 2]
    weights = w_ref[...].astype(f32)
    grad = mm_tn(first_ref[...], d_ref[...])
    g_ref[:, :wide] = grad.astype(bf16)
    columns = jnp.sum(d_ref[...].astype(f32), axis=0, keepdims=True)
    shift = weights[:, 577:578]
    used = weights[:, :wide]
    gain_part = jnp.sum(used * (grad - shift * columns), axis=1, keepdims=True)
    shift_part = jnp.sum(used * columns, axis=1, keepdims=True)
    lane = lanes_of(side_ref.shape)
    side_ref[...] = jnp.where(lane == 64, gain_part, jnp.where(lane == 65, shift_part, 0.0))
    block = block_refs[0][...].astype(f32) + block_refs[1][...].astype(f32)
    g_ref[:, wide:] = block.astype(bf16)
    store_pieces(g_ref, even, odd, sems)


def first_grad(parts, first, weights, blocks, dp_size, gates=()):
    total, width = first.shape
    wide = parts[0].shape[2]
    piece = jax.ShapeDtypeStruct((dp_size // 2, width // dp_size, wide + width // 2), bf16)
    return launch(
        first_grad_kernel,
        gates,
        cost=5.0,
        out_shape=(piece, piece, jax.ShapeDtypeStruct((width, LANES), f32)),
        in_specs=[whole()] * 6,
        out_specs=[whole(pl.ANY)] * 2 + [whole()],
        scratch_shapes=[
            pltpu.VMEM((total, wide), bf16),
            pltpu.VMEM((width, wide + width // 2), bf16),
            pltpu.SemaphoreType.DMA((dp_size,)),
        ],
    )(*parts, first, weights, *blocks)


def second_grad_kernel(*refs):
    parts = refs[:2]
    first_ref, w_ref, side_ref, small_grad_ref, bias_grad_ref = refs[2:7]
    even, odd, d_ref, g_ref, turn_ref, sems = refs[7:]
    _, row_count, wide = parts[0].shape
    width = first_ref.shape[1]
    for d in range(GROUP):
        d_ref[d * row_count : (d + 1) * row_count] = parts[d // 2][d % 2]
    weights = w_ref[...].astype(f32)
    grad = mm_tn(first_ref[...], d_ref[...])
    columns = jnp.sum(d_ref[...].astype(f32), axis=0, keepdims=True)
    gain, shift = weights[:, 576:577], weights[:, 577:578]
    used = weights[:, 640 - wide :]
    gain_part = jnp.sum(used * (grad - shift * columns), axis=1, keepdims=True)
    shift_part = jnp.sum(used * columns, axis=1, keepdims=True)
    gain_part = (gain_part + side_ref[:, 64:65]) / gain
    shift_part = shift_part + side_ref[:, 65:66]
    turn_ref[...] = jnp.zeros_like(turn_ref)
    turn_ref[64:80] = small_grad_ref[...]
    turn_ref[pl.ds(69 + group_index(), 1)] = bias_grad_ref[...]
    lane = lanes_of((width, LANES))
    last = jnp.where(lane < 64, grad[:, wide - LANES :], turn_ref[...].T)
    last = jnp.where(lane == 64, gain_part, jnp.where(lane == 65, shift_part, last))
    g_ref[:, : wide - LANES] = grad[:, : wide - LANES].astype(bf16)
    g_ref[:, wide - LANES :] = last.astype(bf16)
    store_pieces(g_ref, even, odd, sems)


def second_grad(parts, first, weights, side, small_grad, bias_grad, dp_size, gates=()):
    total, width = first.shape
    wide = parts[0].shape[2]
    piece = jax.ShapeDtypeStruct((dp_size // 2, width // dp_size, wide), bf16)
    return launch(
        second_grad_kernel,
        gates,
        cost=5.0,
        out_shape=(piece, piece),
        in_specs=[whole()] * 7,
        out_specs=[whole(pl.ANY)] * 2,
        scratch_shapes=[
            pltpu.VMEM((total, wide), bf16),
            pltpu.VMEM((width, wide), bf16),
            pltpu.VMEM((LANES, width), f32),
            pltpu.SemaphoreType.DMA((dp_size,)),
        ],
    )(*parts, first, weights, side, small_grad, bias_grad)


def part_kernel(near, far, w_ref, *outs):
    cut = near.shape[2]
    weights = w_ref[:, :cut]
    for d in range(GROUP):
        outs[d][...] = mm_nt((near, far)[d // 2][d % 2], weights).astype(bf16)


def input_parts(ones, weight, gates=()):
    row_count, width = ones[0].shape[1], weight.shape[0]
    return launch(
        part_kernel,
        gates,
        cost=2.5,
        out_shape=[jax.ShapeDtypeStruct((row_count, width), bf16)] * GROUP,
        in_specs=[whole()] * 3,
        out_specs=[whole()] * GROUP,
    )(*ones, weight)


def last_kernel(token_ref, dmixed_ref, small_ref, *refs):
    begun, (near, core, over), weights = refs[:3], refs[3:6], refs[6 : 6 + GROUP]
    out_ref = refs[6 + GROUP]
    unit, inverse = norm_parts(token_ref[...].astype(f32))
    df = sum(v[...].astype(f32) for v in begun)
    for d, two in enumerate((near.at[0], core.at[0], over.at[0], core.at[1])):
        df = df + mm_nt(two[...], weights[d][...])
    back = norm_back(df * small_ref[0:1], unit, inverse)
    out_ref[...] = (dmixed_ref[...] + back).astype(bf16)


def finish_input(tokens, dmixed, small, begun, twos, weights, gates=()):
    return launch(
        last_kernel,
        gates,
        cost=3.0,
        out_shape=jax.ShapeDtypeStruct(tokens.shape, bf16),
        in_specs=[whole()] * (9 + GROUP),
        out_specs=whole(),
    )(tokens, dmixed, small, *begun, *twos, *weights)


def place_ffn_kernel(*refs):
    shares, in_ref, down_ref = refs[:4], refs[4], refs[5]
    rows, ff = in_ref.shape
    width = down_ref.shape[1]
    low = group_index()
    for case in range(GROUP):

        @pl.when(low == case)
        def _():
            for d in range(GROUP):
                whose = case ^ d
                down_ref[rows * whose : rows * (whose + 1)] = shares[d][:, width:].astype(f32)
                part = shares[d][:, :width].astype(f32)
                for i in range(width // rows):
                    at = 4 * rows * i + rows * whose
                    in_ref[:, at : at + rows] = part[:, rows * i : rows * (i + 1)]


def place_ffn(shares, gates=()):
    rows, wide = shares[0].shape
    width = wide // 2
    return launch(
        place_ffn_kernel,
        gates,
        cost=3.0,
        out_shape=(
            jax.ShapeDtypeStruct((rows, 4 * width), f32),
            jax.ShapeDtypeStruct((4 * rows, width), f32),
        ),
        in_specs=[whole()] * 4,
        out_specs=[whole()] * 2,
    )(*shares)


def place_qkv_kernel(*refs):
    ones, twos, qkv_ref, out_ref = refs[:4], refs[4:8], refs[8], refs[9]
    rows, width = out_ref.shape
    low = group_index()
    vectors = twos[0][:, 128:].astype(f32)
    for d in range(1, GROUP):
        vectors = vectors + twos[d][:, 128:].astype(f32)
    vectors = vectors.T
    for i, vector_ref in enumerate(refs[10:]):
        for part in range(vector_ref.shape[0] // rows):
            at = 64 + i + part
            vector_ref[part * rows : (part + 1) * rows] = vectors[at : at + 1].reshape(rows)
    cut = width // 2
    halves = [
        ones[i][:, 3 * LANES :].astype(f32) + ones[i + 2][:, 3 * LANES :].astype(f32)
        for i in range(2)
    ]
    for case in range(GROUP):

        @pl.when(low == case)
        def _():
            for i in range(2):
                at = cut * ((case % 2) ^ i)
                out_ref[:, at : at + cut] = halves[i]
            for d in range(GROUP):
                whose = case ^ d
                one, two = ones[d][...].astype(f32), twos[d][...].astype(f32)

                def put(kind, h, part):
                    at = kind * width + 192 * whose + 64 * h
                    qkv_ref[:, at : at + 64] = part

                for h in range(2):
                    put(0, h, one[:, LANES * h : LANES * h + 64])
                    put(1, h, one[:, LANES * h + 64 : LANES * h + LANES])
                    put(2, h, one[:, 2 * LANES + 64 * h : 2 * LANES + 64 * h + 64])
                for kind in range(3):
                    put(kind, 2, two[:, 64 * kind : 64 * kind + 64])


def place_qkv(ones, twos, width, gates=()):
    rows = ones[0].shape[0]
    return launch(
        place_qkv_kernel,
        gates,
        cost=2.0,
        out_shape=(
            jax.ShapeDtypeStruct((rows, 3 * width), f32),
            jax.ShapeDtypeStruct((rows, width), f32),
            *[jax.ShapeDtypeStruct((rows,), f32)] * 5,
            jax.ShapeDtypeStruct((4 * rows,), f32),
        ),
        in_specs=[whole()] * 8,
        out_specs=[whole()] * 8,
    )(*ones, *twos)


def on_device(
    tokens,
    attn_gain,
    attn_shift,
    w_qkv,
    w_out,
    ffn_gain,
    ffn_shift,
    w_in,
    b_in,
    w_down,
    b_down,
    cotangent,
    lengths,
    block_order,
):
    mine = tokens[0]
    row_count, width = mine.shape
    ctx_size = lax.axis_size("ctx")
    dp_size = lax.axis_size("dp")
    far = ctx_size // GROUP
    rows = w_qkv.shape[0]
    half = row_count // 2
    assert math.gcd(H, ctx_size) == GROUP and w_down.shape[0] == GROUP * rows
    where = (lengths, block_order)

    vectors = [attn_gain, attn_shift, ffn_gain, ffn_shift, b_down, b_in]
    piece = pack(w_qkv, vectors)
    far_qkv = far_pieces(piece, "qkv")
    tok_side = swap(mine, "ctx", 1, "tokens_core")
    tok_over = swap(mine, "ctx", 2, "tokens_x")
    piece_in, piece_down = pack_ffn(w_out, w_in, w_down, gates=(piece, tok_side))
    near_qkv = jnp.stack(far_qkv)
    cross_qkv = swap(near_qkv, "dp", 1, "qkv_y")
    tok_over = after(tok_over, near_qkv)
    blocks = [mine, tok_side, tok_over, swap(tok_over, "ctx", 1, "tokens_pass")]
    cot = cotangent[0]

    query, keys, values, first, small, qkv_weight, weight_two = project(
        *where, blocks, near_qkv, cross_qkv
    )
    far_in = far_pieces(after(piece_in, near_qkv, blocks[3]), "in")
    cot_over = swap(after(cot, near_qkv), "ctx", 2, "cot_x")
    near_in = jnp.stack(far_in[:-1] + [after(far_in[-1], query)])
    if far > 1:
        groups = [[g * GROUP + i for g in range(far)] for i in range(GROUP)]
        keys = lax.all_gather(keys, "ctx", axis=1, tiled=True, axis_index_groups=groups)
        values = lax.all_gather(values, "ctx", axis=1, tiled=True, axis_index_groups=groups)

    far_attn, far_query = attend(
        query, keys, values, 2, 2, row_count, gates=(near_in, cot_over)
    )
    cross_in = swap(near_in, "dp", 1, "in_y")
    weight_over = swap(weight_two, "ctx", 2, "weight_x")
    cot_side = swap(after(cot, far_attn), "ctx", 1, "cot_core")
    far_down = far_pieces(after(piece_down, near_in), "down")
    near_down = jnp.stack(far_down[:-1] + [after(far_down[-1], far_attn)])
    near_attn, near_query = attend(
        query, keys, values, 0, 2, row_count, gates=(far_attn, near_down, weight_over)
    )
    over_attn = swap(far_attn, "ctx", 2, "attn_x")
    cross_down = swap(near_down, "dp", 1, "down_y")
    held_in = after(cross_in, near_attn)
    out_piece = jnp.concatenate([near_in[:, :, width:], held_in[:, :, width:]])
    out_pieces = [out_piece, swap(out_piece, "ctx", 1, "out_core")]
    core_attn = swap(jnp.stack([near_attn[1], over_attn[1]]), "ctx", 1, "attn_core")
    attn = [near_attn, core_attn, over_attn]

    mixed, second, w_o = project_out(
        mine, attn, out_pieces, small, gates=(cross_down, cot_side)
    )
    side = swap(second, "ctx", 1, "second_core")
    cot_pass = swap(after(cot_over, mixed), "ctx", 1, "cot_pass")
    cots = [cot, cot_side, cot_over, cot_pass]
    (own_part, side_part), weights = feed_forward(
        *where,
        small,
        [second, side],
        cots[:2],
        [near_in, held_in, near_down, cross_down],
        (0, 1),
    )
    outs_near = out_parts([own_part[1], side_part[1]], weights[1])
    over = after(swap(second, "ctx", 2, "second_x"), outs_near[0])
    ds_side = swap(side_part[0], "ctx", 1, "ds_core")
    weight_over = after(weight_over, outs_near[0])
    weight_pair = swap(jnp.stack([weight_two, weight_over]), "ctx", 1, "weight_core")
    two_weights = [weight_two, weight_pair[0], weight_over, weight_pair[1]]
    (over_part,), _ = feed_forward(
        *where, small, [over], cots[2:3], weights, (2,), gates=(outs_near[0], ds_side, cot_pass, weight_pair)
    )
    cross = after(swap(over, "ctx", 1, "second_pass"), over_part[0])
    (cross_part,), _ = feed_forward(*where, small, [cross], cots[3:], weights, (3,))
    parts = [own_part, side_part, over_part, cross_part]
    ds_sum = add(over_part[0], swap(cross_part[0], "ctx", 1, "ds_side"))
    even_ff, odd_ff, bias_grad = ffn_grads(
        *where,
        cots,
        [second, side, over, cross],
        [part[1] for part in parts],
        [part[2] for part in parts],
        dp_size,
        gates=(ds_sum,),
    )
    outs_far = out_parts([over_part[1], cross_part[1]], weights[1], gates=(even_ff,))
    ds_over = swap(ds_sum, "ctx", 2, "ds_x")
    outs_own, outs_one = outs_near
    outs_two, outs_three = outs_far
    dmixed, small_grad, dattn, out_halves = mixed_back(
        *where,
        mixed,
        cot,
        small,
        w_o,
        attn,
        [own_part[0], ds_side, ds_over],
        gates=(outs_two,),
    )
    dattn_side = swap(dattn[1], "ctx", 1, "dattn_core")
    odd_sent = swap(odd_ff, "dp", 1, "ffn_y")
    outs_side = swap(after(outs_one, dattn_side), "ctx", 1, "outs_core")
    outs_back = swap(after(outs_three, dattn_side), "ctx", 1, "outs_side")

    out_sent = swap(after(out_halves[1], dattn_side), "ctx", 1, "dw_out_core")

    if far > 1:
        over = swap(dattn[2], "ctx", 2, "dattn_x")
        dattn = [dattn[0], dattn_side, over[0], swap(over[1], "ctx", 1, "dattn_pass")]
        ffn_even = add(even_ff, odd_sent)
        dk, dv, dq = attend_back(
            [near_query, far_query],
            keys,
            values,
            [near_attn, far_attn],
            dattn,
            (0, 1, 2),
            (0, 1, 2, 3),
            "raw",
            (),
        )
        dk, dv = (
            lax.psum_scatter(v, "ctx", scatter_dimension=1, tiled=True, axis_index_groups=groups)
            for v in (dk, dv)
        )
        dq, dk, dv = (v[..., :64].astype(bf16) for v in (dq, dk, dv))
        one = jnp.concatenate([dq[0], dk[0], dq[1], dk[1], dv[0], dv[1]], axis=1)
        two = jnp.concatenate([dq[2], dk[2], dv[2], jnp.zeros_like(dv[2])], axis=1)
        ones, twos = (v.reshape(2, 2, row_count, v.shape[1]) for v in (one, two))
        begun = (dq, dk, dv)
        outs_sum = add(outs_two, outs_back)
    else:
        begun = attend_back(
            [near_query],
            keys,
            values,
            [near_attn],
            [dattn[0], dattn_side],
            (0, 1),
            (0, 1),
            "begin",
            (),
        )
        over = after(swap(dattn[2], "ctx", 2, "dattn_x"), begun[0])
        dattn = [dattn[0], dattn_side, over[0], swap(over[1], "ctx", 1, "dattn_pass")]
        ffn_even = add(even_ff, after(odd_sent, begun[0], outs_side, outs_back, out_sent))
        outs_sum = add(outs_two, outs_back)
        ones = attend_back(
            [far_query],
            keys,
            values,
            [far_attn],
            dattn[2:],
            (0, 1),
            (2, 3),
            "final",
            begun,
            gates=(ffn_even, outs_sum),
        )
    outs_over = after(swap(outs_sum, "ctx", 2, "outs_x"), ones[0])
    parts = input_parts(ones, qkv_weight)
    ffn_share = scatter_far(ffn_even, "ffn", ones[0])

    even, odd, part_sums = first_grad(
        ones,
        first,
        qkv_weight,
        (out_halves[0], out_sent),
        dp_size,
        gates=(ffn_share[0], parts[0]),
    )
    part_side = swap(parts[1], "ctx", 1, "df_core")
    part_sum = add(parts[2], swap(parts[3], "ctx", 1, "df_side"))
    if far == 1:
        twos = attend_back(
            [near_query, far_query],
            keys,
            values,
            [near_attn, far_attn],
            dattn,
            (2,),
            (0, 1, 2, 3),
            "final",
            (),
            gates=(even, part_sum, outs_over, part_side),
        )
    part_over = swap(part_sum, "ctx", 2, "df_x")
    ffn_share = ffn_share[1](None)
    one_even = add(even, after(swap(odd, "dp", 1, "one_y"), twos[0]))
    ffn_share = sum_groups(ffn_share)
    ffn_over = swap(ffn_share, "ctx", 2, "ffn_x")
    even, odd = second_grad(
        twos,
        first,
        qkv_weight,
        part_sums,
        small_grad,
        bias_grad,
        dp_size,
        gates=(one_even, ffn_share),
    )
    one_share = scatter_far(one_even, "one", even)
    part_over = after(part_over, even)
    two_even = add(even, swap(odd, "dp", 1, "two_y"))
    two_even = after(two_even, one_share[0], part_over)
    two_share = scatter_far(two_even, "two", None)
    one_share = sum_groups(one_share[1](None))
    layer_out = finish_out(
        *where, mixed, small, [outs_own, outs_side, outs_over], gates=(two_even,)
    )
    two_begun = after(two_share[0], one_share)
    two_share = sum_groups(two_share[1](two_begun))
    two_shares = gather_group(two_share, "two")
    ffn_over = after(ffn_over, two_share)
    dtwos = exchange_pairs(*twos, "dtwos", two_share)
    ffn_pair = swap(jnp.stack([ffn_share, ffn_over]), "ctx", 1, "ffn_core")
    ffn_shares = [ffn_share, ffn_pair[0], ffn_over, ffn_pair[1]]
    input_grad = finish_input(
        mine,
        dmixed,
        small,
        [parts[0], part_side, part_over],
        dtwos,
        two_weights,
    )
    grad_w_in, grad_w_down = place_ffn(ffn_shares, gates=(two_share, input_grad))
    one_shares = gather_pairs(one_share, "one", two_share)
    grad_w_qkv, grad_w_out, *vector_grads, grad_b_in = place_qkv(one_shares, two_shares, width)
    return (
        layer_out[None],
        input_grad[None],
        vector_grads[0],
        vector_grads[1],
        grad_w_qkv,
        grad_w_out,
        vector_grads[2],
        vector_grads[3],
        grad_w_in,
        grad_b_in,
        grad_w_down,
        vector_grads[4],
    )


def solution(mesh):
    placed = (
        P("dp", "ctx", None),
        P("dp"),
        P("dp"),
        P("dp", None),
        P("dp", None),
        P("dp"),
        P("dp"),
        P("dp", None),
        P("dp"),
        P("dp", None),
        P("dp"),
        P("dp", "ctx", None),
        P("dp"),
        P("dp", None),
    )
    return jax.shard_map(
        on_device,
        mesh=mesh,
        in_specs=placed,
        out_specs=(
            P("dp", "ctx", None),
            P("dp", "ctx", None),
            P("dp"),
            P("dp"),
            P("dp", None),
            P("dp", None),
            P("dp"),
            P("dp"),
            P("dp", None),
            P("dp"),
            P("dp", None),
            P("dp"),
        ),
        check_vma=False,
    )
```

```python
import functools
import math

import jax
import jax.numpy as jnp
from jax import lax
from jax.experimental import pallas as pl
from jax.experimental.pallas import tpu as pltpu
from jax.sharding import PartitionSpec as P

H = 12

epsilon = 1e-05
gelu_coeff = 0.7978845608
cubic_term = 0.044715
excluded = -1073741824.0
bf16 = jnp.bfloat16
f32 = jnp.float32
LANES = 128
GROUP = 4
VMEM_SMALL = 16 * 1024 * 1024
VMEM_LARGE = 52 * 1024 * 1024
VMEM_MOST = 62 * 1024 * 1024

nt_dims = (((1,), (1,)), ((), ()))
tn_dims = (((0,), (0,)), ((), ()))


def mm(left, right):
    return jnp.dot(left, right, preferred_element_type=f32)


def mm_nt(left, right):
    return lax.dot_general(left, right, nt_dims, preferred_element_type=f32)


def mm_tn(left, right):
    return lax.dot_general(left, right, tn_dims, preferred_element_type=f32)


def whole(memory_space=pltpu.VMEM):
    return pl.BlockSpec(memory_space=memory_space)


def lanes_of(shape):
    return lax.broadcasted_iota(jnp.int32, shape, 1)


def norm_parts(values):
    center = values - jnp.mean(values, axis=-1, keepdims=True)
    spread = jnp.mean(center * center, axis=-1, keepdims=True)
    inverse = lax.rsqrt(spread + epsilon)
    return center * inverse, inverse


def norm_back(scaled, unit, inverse):
    return inverse * (
        scaled
        - jnp.mean(scaled, axis=-1, keepdims=True)
        - unit * jnp.mean(scaled * unit, axis=-1, keepdims=True)
    )


def three_parts(value):
    first = value.astype(bf16).astype(f32)
    rest = value - first
    second = rest.astype(bf16).astype(f32)
    return first, second, rest - second


def with_parts(base, value):
    lane = lanes_of(base.shape)
    one, two, three = three_parts(value)
    return jnp.where(
        lane == 64, one, jnp.where(lane == 65, two, jnp.where(lane == 66, three, base))
    )


def unpack_rows(packed, rows):
    tail = jnp.concatenate([packed[rows:, :64], packed[rows:, 64:]], axis=0)
    return packed[:rows], tail


def swap(value, axis, bit, name):
    size = lax.axis_size(axis)
    with jax.named_scope(name):
        return lax.ppermute(value, axis, [(i, i ^ bit) for i in range(size)])


def launch(kernel, gates, in_specs, cost=1.0, vmem=VMEM_SMALL, mark=False, **options):
    count = len(gates)
    place = None
    if mark:
        shapes, specs = options["out_shape"], options["out_specs"]
        if not isinstance(shapes, (list, tuple)):
            shapes, specs = [shapes], [specs]
        place = count + len(in_specs) + len(shapes)
        options["out_shape"] = [*shapes, jax.ShapeDtypeStruct((8, LANES), f32)]
        options["out_specs"] = [*specs, whole()]

    def gated(*refs):
        refs = list(refs)
        if mark:
            refs.pop(place)[...] = jnp.zeros((8, LANES), f32)
        kernel(*refs[count:])

    call = pl.pallas_call(
        gated,
        in_specs=[whole(pl.ANY)] * count + in_specs,
        compiler_params=pltpu.CompilerParams(vmem_limit_bytes=vmem),
        cost_estimate=pl.CostEstimate(
            flops=int(cost * 2e7), bytes_accessed=1024, transcendentals=0
        ),
        **options,
    )
    return lambda *operands: call(*gates, *operands)


def hold_kernel(value_ref, out_ref):
    pass


def after(value, *gates):
    return launch(
        hold_kernel,
        gates,
        [whole(pl.ANY)],
        out_shape=jax.ShapeDtypeStruct(value.shape, value.dtype),
        out_specs=whole(pl.ANY),
        input_output_aliases={len(gates): 0},
    )(value)


def far_pieces(piece, name):
    found = [piece]
    for k in range(1, lax.axis_size("dp") // 2):
        found.append(swap(piece, "dp", 2 * k, name + "_z"))
    return found


def add(left, right):
    return (left.astype(f32) + right.astype(f32)).astype(bf16)


def scatter_far(even, name, gate):
    def step(even, gate):
        half = even.shape[0] // 2
        bit = lax.axis_size("dp") // (2 * half)
        pairs = even.reshape(half, 2, *even.shape[1:])
        received = swap(pairs[:, 1], "dp", bit, name + "_z")
        return add(pairs[:, 0], received if gate is None else after(received, gate))

    begun = step(even, gate)

    def finish(gate):
        total = begun
        while total.shape[0] > 1:
            total = step(total, gate)
        return total[0]

    return begun, finish


def sum_groups(value):
    bit = GROUP
    while bit < lax.axis_size("ctx"):
        other = swap(value, "ctx", bit, "groups")
        value = (value.astype(f32) + other.astype(f32)).astype(bf16)
        bit *= 2
    return value


def gather_group(value, name, gate=None):
    over = swap(value, "ctx", 2, name + "_x")
    if gate is not None:
        over = after(over, gate)
    side = swap(value, "ctx", 1, name + "_core")
    return [value, side, over, swap(over, "ctx", 1, name + "_pass")]


def exchange_pairs(near, far, name, gate=None):
    over = swap(far, "ctx", 2, name + "_x")
    if gate is not None:
        over = after(over, gate)
    core = swap(jnp.stack([near[1], over[1]]), "ctx", 1, name + "_core")
    return [near, core, over]


def gather_pairs(value, name, gate=None):
    over = swap(value, "ctx", 2, name + "_x")
    if gate is not None:
        over = after(over, gate)
    pair = swap(jnp.stack([value, over]), "ctx", 1, name + "_core")
    return [value, pair[0], over, pair[1]]


def position_of(order_ref, slot, rows):
    index = lax.axis_index("ctx")
    return order_ref[0, lax.bitwise_xor(index, slot)] * rows


def valid_rows(length_ref, order_ref, slot, rows):
    stored = lax.broadcasted_iota(jnp.int32, (rows, LANES), 0)[:, :1]
    position = position_of(order_ref, slot, rows) + stored
    return jnp.where(position < length_ref[0], 1.0, 0.0)


def group_index():
    return lax.rem(lax.axis_index("ctx"), GROUP)


def load_pieces(sources, target, sems, first_sem=0):
    me = lax.axis_index("dp")
    copies = []
    for source, differences in sources:
        rows = source.shape[1]
        for k, difference in enumerate(differences):
            owner = lax.bitwise_xor(me, difference)
            copies.append(
                pltpu.make_async_copy(
                    source.at[k],
                    target.at[pl.ds(pl.multiple_of(owner * rows, 16), rows)],
                    sems.at[first_sem + len(copies)],
                )
            )
    for copy in copies:
        copy.start()
    return copies


def near_and_cross(near, cross):
    halves = near.shape[0]
    return [(near, [2 * k for k in range(halves)]), (cross, [2 * k + 1 for k in range(halves)])]


def store_pieces(source, even, odd, sems):
    halves, rows, _ = even.shape
    me = lax.axis_index("dp")
    copies = []
    for parity, target in ((0, even), (1, odd)):
        for k in range(halves):
            owner = lax.bitwise_xor(me, 2 * k + parity)
            copies.append(
                pltpu.make_async_copy(
                    source.at[pl.ds(pl.multiple_of(owner * rows, 16), rows)],
                    target.at[k],
                    sems.at[2 * k + parity],
                )
            )
    for copy in copies:
        copy.start()
    for copy in copies:
        copy.wait()


def pack_kernel(w_hbm, *refs):
    w_ref, sems = refs[-2:]
    count = (len(refs) - 3) // 2
    vectors, out_ref, held = refs[:count], refs[count], refs[count + 1 : -2]
    copies = [pltpu.make_async_copy(w_hbm, w_ref, sems.at[count])]
    for i in range(count):
        copies.append(pltpu.make_async_copy(vectors[i], held[i], sems.at[i]))
    for copy in copies:
        copy.start()
    for copy in copies:
        copy.wait()
    rows = w_ref.shape[0]
    width = w_ref.shape[1] // 3
    low = group_index()
    stacked = []
    for v in held:
        flat = v[...].astype(f32).reshape(1, v.shape[0])
        stacked += [flat[:, i : i + rows] for i in range(0, v.shape[0], rows)]
    stacked.append(jnp.zeros((LANES - len(stacked), rows), f32))
    small = jnp.concatenate(stacked, axis=0).T[:, :64].astype(bf16)
    for case in range(GROUP):

        @pl.when(low == case)
        def _():
            def head(kind, h):
                at = kind * width + 192 * case + 64 * h
                return w_ref[:, at : at + 64]

            out_ref[...] = jnp.concatenate(
                [
                    head(0, 0),
                    head(1, 0),
                    head(0, 1),
                    head(1, 1),
                    head(2, 0),
                    head(2, 1),
                    head(0, 2),
                    head(1, 2),
                    head(2, 2),
                    small,
                ],
                axis=1,
            )


def pack(w_qkv, vectors, gates=()):
    rows = w_qkv.shape[0]
    return launch(
        pack_kernel,
        gates,
        vmem=VMEM_MOST,
        cost=1.0,
        out_shape=jax.ShapeDtypeStruct((rows, 640), bf16),
        in_specs=[whole(pltpu.HBM)] * (1 + len(vectors)),
        out_specs=whole(),
        scratch_shapes=[pltpu.VMEM(v.shape, bf16) for v in vectors]
        + [pltpu.VMEM(w_qkv.shape, bf16), pltpu.SemaphoreType.DMA((1 + len(vectors),))],
    )(w_qkv, *vectors)


def pack_ffn_kernel(out_ref, in_ref, down_ref, one_ref, two_ref):
    rows, ff = in_ref.shape
    width = out_ref.shape[1]
    half = width // 2
    low = group_index()
    per = 4 * rows
    for case in range(GROUP):

        @pl.when(low == case)
        def _():
            at = half * (case % 2)
            parts = [
                in_ref[:, per * i + rows * case : per * i + rows * (case + 1)]
                for i in range(ff // per)
            ]
            one_ref[:, :width] = jnp.concatenate(parts, axis=1)
            one_ref[:, width:] = out_ref[:, at : at + half]
            two_ref[...] = down_ref[rows * case : rows * (case + 1)]


def pack_ffn(w_out, w_in, w_down, gates=()):
    rows, width = w_out.shape
    return launch(
        pack_ffn_kernel,
        gates,
        cost=1.0,
        out_shape=(
            jax.ShapeDtypeStruct((rows, width + width // 2), bf16),
            jax.ShapeDtypeStruct((rows, width), bf16),
        ),
        in_specs=[whole()] * 3,
        out_specs=[whole()] * 2,
    )(w_out, w_in, w_down)


def qkv_kernel(length_ref, order_ref, *refs):
    tokens = refs[:GROUP]
    near, cross = refs[GROUP : GROUP + 2]
    q_ref, k_ref, v_ref, first_ref, small_ref, w_ref, w_two_ref, sems = refs[GROUP + 2 :]
    row_count, width = tokens[0].shape
    for copy in load_pieces(near_and_cross(near, cross), w_ref, sems):
        copy.wait()
    w_two_ref[...] = w_ref[:, 384:640]
    small = w_ref[:, 512:640].astype(f32).T
    small_ref[...] = small[64:80]
    gain, shift = small[64:65], small[65:66]
    length = length_ref[0]
    lane = lanes_of((row_count, LANES))
    ones = jnp.where((lane >= 64) & (lane < 67), 1.0, 0.0)
    bias_lane = jnp.where(lane == 67, 1.0, 0.0)
    for d in range(GROUP):
        unit, _ = norm_parts(tokens[d][...].astype(f32))
        first = (unit * gain + shift).astype(bf16)
        part = pl.ds(d * row_count, row_count)
        first_ref[part] = first
        qkv = mm(first, w_ref[...]).astype(bf16).astype(f32)

        def head(place):
            block = qkv[:, place // 2 * LANES : (place // 2 + 1) * LANES]
            if place % 2:
                block = pltpu.roll(block, 64, 1)
            return jnp.where(lane < 64, block, 0.0)

        stored = lax.broadcasted_iota(jnp.int32, (row_count, LANES), 0)
        position = position_of(order_ref, d, row_count) + stored
        bias = jnp.where(position < length, 0.0, excluded) * bias_lane
        for h, (at_q, at_k, at_v) in enumerate(((0, 1, 4), (2, 3, 5), (6, 7, 8))):
            q_ref[h, part] = (head(at_q) * 0.125 + bias_lane).astype(bf16)
            k_ref[h, part] = (head(at_k) + ones + bias).astype(bf16)
            v_ref[h, part] = (head(at_v) + ones).astype(bf16)


def project(length, order, tokens, near, cross, gates=()):
    row_count, width = tokens[0].shape
    total = GROUP * row_count
    wide = near.shape[2]
    head_out = jax.ShapeDtypeStruct((3, total, LANES), bf16)
    return launch(
        qkv_kernel,
        gates,
        cost=10.0,
        out_shape=(
            head_out,
            head_out,
            head_out,
            jax.ShapeDtypeStruct((total, width), bf16),
            jax.ShapeDtypeStruct((16, width), f32),
            jax.ShapeDtypeStruct((width, wide), bf16),
            jax.ShapeDtypeStruct((width, 256), bf16),
        ),
        in_specs=[whole(pltpu.SMEM)] * 2 + [whole()] * GROUP + [whole(pl.ANY)] * 2,
        out_specs=[whole()] * 7,
        scratch_shapes=[pltpu.SemaphoreType.DMA((2 * near.shape[0],))],
    )(length, order, *tokens, near, cross)


def attend_kernel(block_rows, q_ref, k_ref, v_ref, packed_ref, q_out_ref):
    row_count = q_ref.shape[1]
    half = row_count // 2
    lane = lanes_of((block_rows, LANES))
    for i in range(row_count // block_rows):
        part = pl.ds(i * block_rows, block_rows)
        heads = []
        for h in range(3):
            query = q_ref[h, part]
            scores = mm_nt(query, k_ref[h])
            top = jnp.max(scores, axis=1, keepdims=True)
            weights = jnp.exp(scores - top).astype(bf16)
            result = mm(weights, v_ref[h])
            denom = result[:, 64:65]
            heads.append(jnp.where(lane < 64, result / denom, 0.0))
            log_total = top + jnp.log(denom)
            q_out_ref[h, part] = with_parts(query.astype(f32), -log_total).astype(bf16)
        packed_ref[0, part] = (heads[0] + pltpu.roll(heads[1], 64, 1)).astype(bf16)
        for r in range(0, block_rows, half):
            size = min(half, block_rows)
            row = i * block_rows + r
            side, place = row // half, row % half
            packed_ref[
                0, pl.ds(row_count + place, size), 64 * side : 64 * side + 64
            ] = heads[2][r : r + size, :64].astype(bf16)


def attend(query, keys, values, first_slot, slots, row_count, gates=()):
    total = keys.shape[1]
    block_rows = min(row_count // 2, 256)
    return launch(
        functools.partial(attend_kernel, block_rows),
        gates,
        mark=True,
        cost=5.0 * slots,
        vmem=VMEM_LARGE if total > GROUP * row_count else VMEM_SMALL,
        grid=(slots,),
        out_shape=(
            jax.ShapeDtypeStruct((slots, row_count * 3 // 2, LANES), bf16),
            jax.ShapeDtypeStruct((3, slots * row_count, LANES), bf16),
        ),
        in_specs=[
            pl.BlockSpec((3, row_count, LANES), lambda s: (0, s + first_slot, 0)),
            whole(),
            whole(),
        ],
        out_specs=(
            pl.BlockSpec((1, row_count * 3 // 2, LANES), lambda s: (s, 0, 0)),
            pl.BlockSpec((3, row_count, LANES), lambda s: (0, s, 0)),
        ),
    )(query, keys, values)


def weights_kernel(near_ref, far_ref, k_ref, out_ref):
    query = jnp.where(pl.program_id(1) < 2, near_ref[0], far_ref[0])
    rows = query.shape[0]
    for c in range(k_ref.shape[1] // rows):
        at = pl.ds(c * rows, rows)
        out_ref[0, 0, at] = jnp.exp(mm_nt(k_ref[0, at], query)).astype(bf16)


def attend_weights(near_query, far_query, keys, heads, gates=()):
    row_count = near_query.shape[1] // 2
    total = keys.shape[1]
    first = heads[0]
    return launch(
        weights_kernel,
        gates,
        mark=True,
        cost=3.0 * len(heads),
        grid=(len(heads), GROUP),
        out_shape=jax.ShapeDtypeStruct((len(heads), GROUP, total, row_count), bf16),
        in_specs=[
            pl.BlockSpec((1, row_count, LANES), lambda h, s: (h + first, jnp.minimum(s, 1), 0)),
            pl.BlockSpec((1, row_count, LANES), lambda h, s: (h + first, jnp.maximum(s - 2, 0), 0)),
            pl.BlockSpec((1, total, LANES), lambda h, s: (h + first, 0, 0)),
        ],
        out_specs=pl.BlockSpec((1, 1, total, row_count), lambda h, s: (h, s, 0, 0)),
    )(near_query, far_query, keys)


def group_attn(refs, row_count):
    near, core, over = refs
    packed = (near[0], core[0], over[0], core[1])
    return [jnp.concatenate(unpack_rows(v, row_count), axis=1) for v in packed]


def out_kernel(token_ref, *refs):
    attn_refs, pieces = refs[:3], refs[3:5]
    small_ref, mixed_ref, second_ref, w_o, sems = refs[5:]
    row_count, width = token_ref.shape
    half = width // 2
    number = pieces[0].shape[0]
    low = group_index()
    core = lax.rem(low, 2)
    differences = [2 * k for k in range(number // 2)] + [2 * k + 1 for k in range(number // 2)]
    copies = []
    for side in range(2):
        column = pl.multiple_of((core if side == 0 else 1 - core) * half, LANES)
        target = w_o.at[:, pl.ds(column, half)]
        copies += load_pieces([(pieces[side], differences)], target, sems, side * number)
    mixed = token_ref[...].astype(f32)
    attn = group_attn(attn_refs, row_count)
    for copy in copies:
        copy.wait()
    for d in range(GROUP):
        at = pl.ds(pl.multiple_of(lax.bitwise_xor(low, d) * 192, 16), 192)
        mixed = mixed + mm(attn[d], w_o[at, :])
    mixed_ref[...] = mixed
    unit, _ = norm_parts(mixed)
    second_ref[...] = (unit * small_ref[2:3] + small_ref[3:4]).astype(bf16)


def project_out(tokens, attn, pieces, small, gates=()):
    row_count, width = tokens.shape
    number = pieces[0].shape[0]
    return launch(
        out_kernel,
        gates,
        mark=True,
        cost=4.5,
        out_shape=(
            jax.ShapeDtypeStruct((row_count, width), f32),
            jax.ShapeDtypeStruct((row_count, width), bf16),
            jax.ShapeDtypeStruct((width, width), bf16),
        ),
        in_specs=[whole()] * 4 + [whole(pl.ANY)] * 2 + [whole()],
        out_specs=[whole()] * 3,
        scratch_shapes=[pltpu.SemaphoreType.DMA((2 * number,))],
    )(tokens, *attn, *pieces, small)


def ffn_kernel(slots, gathers, length_ref, order_ref, small_ref, *refs):
    number = len(slots)
    seconds, cots = refs[:number], refs[number : 2 * number]
    refs = refs[2 * number :]
    count = 4 if gathers else 2
    sources, refs = refs[:count], refs[count:]
    outs = [refs[3 * i : 3 + 3 * i] for i in range(number)]
    refs = refs[3 * number :]
    rows, width = seconds[0].shape
    if gathers:
        w_i, w_d, sems = refs
        near, cross, near_down, cross_down = sources
        parts = near_and_cross(*(v.at[:, :, pl.ds(0, width)] for v in (near, cross)))
        in_copies = load_pieces(parts, w_i, sems)
        down_copies = load_pieces(near_and_cross(near_down, cross_down), w_d, sems, 2 * gathers)
        for copy in in_copies:
            copy.wait()
    else:
        w_i, w_d = sources
    bias = small_ref[pl.ds(5 + group_index(), 1)]
    for i, slot in enumerate(slots):
        ds_ref, active_ref, dhid_ref = outs[i]
        row_count = cots[i].shape[0]
        valid = valid_rows(length_ref, order_ref, slot, row_count)
        dlow = (cots[i][...].astype(f32) * valid).astype(bf16)
        hidden = mm(seconds[i][...], w_i[...]) + bias
        squared = hidden * hidden
        bent = jnp.tanh(hidden * (gelu_coeff + gelu_coeff * cubic_term * squared))
        plus = 0.5 + 0.5 * bent
        slope = plus + hidden * (plus * (1.0 - bent)) * (
            gelu_coeff + gelu_coeff * 3.0 * cubic_term * squared
        )
        active_ref[...] = (hidden * plus).astype(bf16)
        if gathers and i == 0:
            for copy in down_copies:
                copy.wait()
        dhid = (mm_nt(dlow, w_d[...]) * slope).astype(bf16)
        dhid_ref[...] = dhid
        ds_ref[...] = mm_nt(dhid, w_i[...]).astype(bf16)


def feed_forward(length, order, small, seconds, cots, weights, slots, gates=()):
    rows, width = seconds[0].shape
    gathers = weights[0].shape[0] if len(weights) == 4 else 0
    number = len(slots)
    block = jax.ShapeDtypeStruct((rows, width), bf16)
    square = jax.ShapeDtypeStruct((width, width), bf16)
    results = launch(
        functools.partial(ffn_kernel, slots, gathers),
        gates,
        cost=3.0 * number,
        out_shape=[block] * (3 * number) + [square] * (2 if gathers else 0),
        in_specs=[whole(pltpu.SMEM)] * 2
        + [whole()] * (1 + 2 * number)
        + [whole(pl.ANY) if gathers else whole()] * len(weights),
        out_specs=[whole()] * (3 * number + (2 if gathers else 0)),
        scratch_shapes=[pltpu.SemaphoreType.DMA((4 * gathers,))] if gathers else [],
    )(length, order, small, *seconds, *cots, *weights)
    grouped = [results[3 * i : 3 * i + 3] for i in range(number)]
    return grouped, results[3 * number :]


def out_part_kernel(*refs):
    w_d = refs[2][...]
    for i in range(2):
        refs[3 + i][...] = mm(refs[i][...], w_d).astype(bf16)


def out_parts(actives, w_down, gates=()):
    return launch(
        out_part_kernel,
        gates,
        mark=True,
        cost=2.0,
        out_shape=[jax.ShapeDtypeStruct(v.shape, bf16) for v in actives],
        in_specs=[whole()] * 3,
        out_specs=[whole()] * 2,
    )(*actives, w_down)


def ffn_grad_kernel(length_ref, order_ref, *refs):
    cots, seconds, actives, dhids = (refs[i : i + GROUP] for i in range(0, 4 * GROUP, GROUP))
    even, odd, bias_ref, g_ref, sems = refs[4 * GROUP :]
    row_count, width = cots[0].shape
    bias = jnp.zeros((1, width), f32)
    grad_in = jnp.zeros((width, width), f32)
    for d in range(GROUP):
        dhid = dhids[d][...]
        bias = bias + jnp.sum(dhid.astype(f32), axis=0, keepdims=True)
        grad_in = grad_in + mm_tn(seconds[d][...], dhid)
    g_ref[:, :width] = grad_in.astype(bf16)
    bias_ref[...] = bias
    grad_down = jnp.zeros((width, width), f32)
    for d in range(GROUP):
        valid = valid_rows(length_ref, order_ref, d, row_count)
        dlow = (cots[d][...].astype(f32) * valid).astype(bf16)
        grad_down = grad_down + mm_tn(actives[d][...], dlow)
    g_ref[:, width:] = grad_down.astype(bf16)
    store_pieces(g_ref, even, odd, sems)


def ffn_grads(length, order, cots, seconds, actives, dhids, dp_size, gates=()):
    width = cots[0].shape[1]
    halves = dp_size // 2
    piece = jax.ShapeDtypeStruct((halves, width // dp_size, 2 * width), bf16)
    return launch(
        ffn_grad_kernel,
        gates,
        mark=True,
        cost=7.0,
        out_shape=(piece, piece, jax.ShapeDtypeStruct((1, width), f32)),
        in_specs=[whole(pltpu.SMEM)] * 2 + [whole()] * (4 * GROUP),
        out_specs=[whole(pl.ANY)] * 2 + [whole()],
        scratch_shapes=[
            pltpu.VMEM((width, 2 * width), bf16),
            pltpu.SemaphoreType.DMA((dp_size,)),
        ],
    )(length, order, *cots, *seconds, *actives, *dhids)


def mixed_back_kernel(length_ref, order_ref, *refs):
    mixed_ref, cot_ref, small_ref, w_o = refs[:4]
    attn_refs = refs[4:7]
    ds_refs = refs[7:10]
    dmixed_ref, small_grad_ref = refs[10:12]
    own, side, over = refs[12:15]
    dattn_refs = (own, side, over.at[0], over.at[1])
    half_refs = refs[15:17]
    g_o = refs[17]
    row_count, width = mixed_ref.shape
    half = row_count // 2
    low = group_index()
    unit, inverse = norm_parts(mixed_ref[...])
    ds = sum(v[...].astype(f32) for v in ds_refs)
    valid = valid_rows(length_ref, order_ref, 0, row_count)
    dout = cot_ref[...].astype(f32) * valid
    dmixed = dout + norm_back(ds * small_ref[2:3], unit, inverse)
    dmixed_ref[...] = dmixed
    dbranch = dmixed.astype(bf16)

    def out_rows(d):
        return pl.ds(pl.multiple_of(lax.bitwise_xor(low, d) * 192, 16), 192)

    for d in range(GROUP):
        dattn = mm_nt(dbranch, w_o[out_rows(d), :])
        dattn_refs[d][pl.ds(0, row_count)] = dattn[:, :LANES].astype(bf16)
        dattn_refs[d][pl.ds(row_count, half), :64] = dattn[:half, LANES:].astype(bf16)
        dattn_refs[d][pl.ds(row_count, half), 64:] = dattn[half:, LANES:].astype(bf16)
    attn = group_attn(attn_refs, row_count)
    for d in range(GROUP):
        g_o[out_rows(d), :] = mm_tn(attn[d], dbranch).astype(bf16)
    core = lax.rem(low, 2)
    for here, half_ref in zip((core, 1 - core), half_refs):
        column = pl.multiple_of(here * (width // 2), LANES)
        half_ref[...] = g_o[:, pl.ds(column, width // 2)]
    small_grad_ref[...] = jnp.zeros_like(small_grad_ref)
    small_grad_ref[2:3] = jnp.sum(ds * unit, axis=0, keepdims=True)
    small_grad_ref[3:4] = jnp.sum(ds, axis=0, keepdims=True)
    small_grad_ref[4:5] = jnp.sum(dout, axis=0, keepdims=True)


def mixed_back(length, order, mixed, cot, small, w_o, attn, ds, gates=()):
    row_count, width = mixed.shape
    results = launch(
        mixed_back_kernel,
        gates,
        cost=7.0,
        out_shape=[
            jax.ShapeDtypeStruct((row_count, width), f32),
            jax.ShapeDtypeStruct((16, width), f32),
        ]
        + [jax.ShapeDtypeStruct((row_count * 3 // 2, LANES), bf16)] * 2
        + [jax.ShapeDtypeStruct((2, row_count * 3 // 2, LANES), bf16)]
        + [jax.ShapeDtypeStruct((width, width // 2), bf16)] * 2,
        in_specs=[whole(pltpu.SMEM)] * 2 + [whole()] * 10,
        out_specs=[whole()] * 7,
        scratch_shapes=[pltpu.VMEM((width, width), bf16)],
    )(length, order, mixed, cot, small, w_o, *attn, *ds)
    return results[0], results[1], results[2:5], results[5:7]


def layer_out_kernel(length_ref, order_ref, mixed_ref, small_ref, *refs):
    own, side, over, out_ref = refs
    row_count = mixed_ref.shape[0]
    valid = valid_rows(length_ref, order_ref, 0, row_count)
    total = mixed_ref[...] + own[...].astype(f32) + side[...].astype(f32) + over[...].astype(f32)
    out_ref[...] = ((total + small_ref[4:5]) * valid).astype(bf16)


def finish_out(length, order, mixed, small, parts, gates=()):
    return launch(
        layer_out_kernel,
        gates,
        mark=True,
        cost=3.0,
        out_shape=jax.ShapeDtypeStruct(mixed.shape, bf16),
        in_specs=[whole(pltpu.SMEM)] * 2 + [whole()] * 5,
        out_specs=whole(),
    )(length, order, mixed, small, *parts)


def attend_back_kernel(mode, heads, slots, row_count, starts, *refs):
    number = len(slots)
    pairs = number // 2
    q_refs, (k_ref, v_ref) = refs[:pairs], refs[pairs : pairs + 2]
    refs = refs[pairs + 2 :]
    if mode != "raw":
        prob_ref, refs = refs[0], refs[1:]
    attn_refs, dattn_refs = refs[:pairs], refs[pairs : pairs + number]
    refs = refs[pairs + number :]
    if starts:
        dk_in, dv_in, dq_in = refs[:3]
        refs = refs[3:]
    outs = refs[:-5]
    grad_ref, k_turned, dq_ref, dk_ref, dv_ref = refs[-5:]
    head, step = pl.program_id(0), pl.program_id(1)
    total = k_ref.shape[1]
    chunk = row_count
    first_slot = slots[0] if mode == "final" else 0

    @pl.when((head == 0) & (step == 0))
    def _():
        lane = lanes_of((row_count, LANES))
        for d in range(number):
            top, tail = unpack_rows(dattn_refs[d][...].astype(f32), row_count)
            top_a, tail_a = unpack_rows(attn_refs[d // 2][d % 2].astype(f32), row_count)
            product = top * top_a
            for i, h in enumerate(heads):
                if h == 0:
                    block = top
                    delta = jnp.sum(jnp.where(lane < 64, product, 0.0), axis=1, keepdims=True)
                elif h == 1:
                    block = pltpu.roll(top, 64, 1)
                    delta = jnp.sum(jnp.where(lane >= 64, product, 0.0), axis=1, keepdims=True)
                else:
                    block = jnp.concatenate([tail, tail], axis=1)
                    delta = jnp.sum(tail * tail_a, axis=1, keepdims=True)
                base = jnp.where(lane < 64, block, 0.0)
                grad_ref[i, pl.ds(d * row_count, row_count)] = with_parts(base, -delta).astype(bf16)

    @pl.when(step == 0)
    def _():
        k_turned[...] = k_ref[0].astype(f32).T.astype(bf16)
        if starts:
            dk_ref[...] = dk_in[0]
            dv_ref[...] = dv_in[0]
            dq_ref[: first_slot * row_count] = dq_in[0]
        else:
            dk_ref[...] = jnp.zeros_like(dk_ref)
            dv_ref[...] = jnp.zeros_like(dv_ref)

    query = q_refs[0][0]
    if pairs > 1:
        query = jnp.where(step < 2, query, q_refs[1][0])
    grad = grad_ref[head, pl.ds(pl.multiple_of(step * row_count, row_count), row_count)]
    turned = jnp.zeros((LANES, row_count), f32)
    for c in range(total // chunk):
        at = pl.ds(c * chunk, chunk)
        if mode == "raw":
            probs = jnp.exp(mm_nt(k_ref[0, at], query)).astype(bf16)
        else:
            probs = prob_ref[0, 0, at]
        dscores = (probs.astype(f32) * mm_nt(v_ref[0, at], grad)).astype(bf16)
        dv_ref[at] += mm(probs, grad)
        dk_ref[at] += mm(dscores, query)
        turned = turned + mm(k_turned[:, at], dscores)
    place = pl.multiple_of((first_slot + step) * row_count, row_count)
    dq_ref[pl.ds(place, row_count)] = turned.T * 0.125

    @pl.when(step == number - 1)
    def _():
        if mode != "final":
            outs[0][0] = dk_ref[...]
            outs[1][0] = dv_ref[...]
            outs[2][0] = dq_ref[...]
            return
        lane = lanes_of((row_count, LANES))
        last_at = LANES * len(heads)
        for i in range(len(heads)):

            @pl.when(head == i)
            def _():
                for d in range(GROUP):
                    at = pl.ds(d * row_count, row_count)
                    pair = jnp.where(lane < 64, dq_ref[at], pltpu.roll(dk_ref[at], 64, 1))
                    out = outs[d // 2].at[d % 2]
                    out[:, i * LANES : (i + 1) * LANES] = pair.astype(bf16)
                    value = dv_ref[at]
                    if i == 0:
                        value = jnp.where(lane < 64, value, 0.0)
                        out[:, last_at : last_at + LANES] = value.astype(bf16)
                    else:
                        out[:, last_at + 64 : last_at + LANES] = value[:, :64].astype(bf16)


def attend_back(queries, keys, values, probs, attn, dattn, heads, slots, mode, begun, gates=()):
    row_count = dattn[0].shape[0] * 2 // 3
    total = keys.shape[1]
    number = len(slots)
    kept = GROUP if mode == "final" else number
    first_head = heads[0]
    if number == 2:
        places = [lambda h, s: (h + first_head, s, 0)]
    else:
        places = [
            lambda h, s: (h + first_head, jnp.minimum(s, 1), 0),
            lambda h, s: (h + first_head, jnp.maximum(s - 2, 0), 0),
        ]

    def per_head(size):
        return (
            jax.ShapeDtypeStruct((len(heads), size, LANES), f32),
            pl.BlockSpec((1, size, LANES), lambda h, s: (h, 0, 0)),
        )

    if mode == "final":
        wide = LANES * (len(heads) + 1)
        outs = [
            (
                jax.ShapeDtypeStruct((2, row_count, wide), bf16),
                pl.BlockSpec((2, row_count, wide), lambda h, s: (0, 0, 0)),
            )
        ] * 2
    else:
        outs = [per_head(total), per_head(total), per_head(number * row_count)]
    begun_specs = []
    if begun:
        begun_specs = [
            pl.BlockSpec((1, v.shape[1], LANES), lambda h, s: (h, 0, 0)) for v in begun
        ]
    return launch(
        functools.partial(attend_back_kernel, mode, heads, slots, row_count, bool(begun)),
        gates,
        mark=True,
        cost=3.2 * number * len(heads),
        vmem=VMEM_LARGE if total > GROUP * row_count else VMEM_SMALL,
        grid=(len(heads), number),
        out_shape=[shape for shape, _ in outs],
        out_specs=[spec for _, spec in outs],
        in_specs=[
            pl.BlockSpec((1, row_count, LANES), place) for place in places
        ]
        + [pl.BlockSpec((1, total, LANES), lambda h, s: (h + first_head, 0, 0))] * 2
        + [
            pl.BlockSpec((1, 1, total, row_count), lambda h, s: (h, s + slots[0], 0, 0))
            for _ in probs
        ]
        + [whole()] * (len(attn) + number)
        + begun_specs,
        scratch_shapes=[
            pltpu.VMEM((len(heads), number * row_count, LANES), bf16),
            pltpu.VMEM((LANES, total), bf16),
            pltpu.VMEM((kept * row_count, LANES), f32),
            pltpu.VMEM((total, LANES), f32),
            pltpu.VMEM((total, LANES), f32),
        ],
    )(*queries, keys, values, *probs, *attn, *dattn, *begun)


def first_grad_kernel(*refs):
    parts, first_ref, w_ref, block_refs = refs[:2], refs[2], refs[3], refs[4:6]
    even, odd, side_ref, d_ref, g_ref, sems = refs[6:]
    _, row_count, wide = parts[0].shape
    for d in range(GROUP):
        d_ref[d * row_count : (d + 1) * row_count] = parts[d // 2][d % 2]
    weights = w_ref[...].astype(f32)
    grad = mm_tn(first_ref[...], d_ref[...])
    g_ref[:, :wide] = grad.astype(bf16)
    columns = jnp.sum(d_ref[...].astype(f32), axis=0, keepdims=True)
    shift = weights[:, 577:578]
    used = weights[:, :wide]
    gain_part = jnp.sum(used * (grad - shift * columns), axis=1, keepdims=True)
    shift_part = jnp.sum(used * columns, axis=1, keepdims=True)
    lane = lanes_of(side_ref.shape)
    side_ref[...] = jnp.where(lane == 64, gain_part, jnp.where(lane == 65, shift_part, 0.0))
    block = block_refs[0][...].astype(f32) + block_refs[1][...].astype(f32)
    g_ref[:, wide:] = block.astype(bf16)
    store_pieces(g_ref, even, odd, sems)


def first_grad(parts, first, weights, blocks, dp_size, gates=()):
    total, width = first.shape
    wide = parts[0].shape[2]
    piece = jax.ShapeDtypeStruct((dp_size // 2, width // dp_size, wide + width // 2), bf16)
    return launch(
        first_grad_kernel,
        gates,
        mark=True,
        cost=5.0,
        out_shape=(piece, piece, jax.ShapeDtypeStruct((width, LANES), f32)),
        in_specs=[whole()] * 6,
        out_specs=[whole(pl.ANY)] * 2 + [whole()],
        scratch_shapes=[
            pltpu.VMEM((total, wide), bf16),
            pltpu.VMEM((width, wide + width // 2), bf16),
            pltpu.SemaphoreType.DMA((dp_size,)),
        ],
    )(*parts, first, weights, *blocks)


def second_grad_kernel(*refs):
    parts = refs[:2]
    first_ref, w_ref, side_ref, small_grad_ref, bias_grad_ref = refs[2:7]
    even, odd, d_ref, g_ref, turn_ref, sems = refs[7:]
    _, row_count, wide = parts[0].shape
    width = first_ref.shape[1]
    for d in range(GROUP):
        d_ref[d * row_count : (d + 1) * row_count] = parts[d // 2][d % 2]
    weights = w_ref[...].astype(f32)
    grad = mm_tn(first_ref[...], d_ref[...])
    columns = jnp.sum(d_ref[...].astype(f32), axis=0, keepdims=True)
    gain, shift = weights[:, 576:577], weights[:, 577:578]
    used = weights[:, 640 - wide :]
    gain_part = jnp.sum(used * (grad - shift * columns), axis=1, keepdims=True)
    shift_part = jnp.sum(used * columns, axis=1, keepdims=True)
    gain_part = (gain_part + side_ref[:, 64:65]) / gain
    shift_part = shift_part + side_ref[:, 65:66]
    turn_ref[...] = jnp.zeros_like(turn_ref)
    turn_ref[64:80] = small_grad_ref[...]
    turn_ref[pl.ds(69 + group_index(), 1)] = bias_grad_ref[...]
    lane = lanes_of((width, LANES))
    last = jnp.where(lane < 64, grad[:, wide - LANES :], turn_ref[...].T)
    last = jnp.where(lane == 64, gain_part, jnp.where(lane == 65, shift_part, last))
    g_ref[:, : wide - LANES] = grad[:, : wide - LANES].astype(bf16)
    g_ref[:, wide - LANES :] = last.astype(bf16)
    store_pieces(g_ref, even, odd, sems)


def second_grad(parts, first, weights, side, small_grad, bias_grad, dp_size, gates=()):
    total, width = first.shape
    wide = parts[0].shape[2]
    piece = jax.ShapeDtypeStruct((dp_size // 2, width // dp_size, wide), bf16)
    return launch(
        second_grad_kernel,
        gates,
        mark=True,
        cost=0.01,
        out_shape=(piece, piece),
        in_specs=[whole()] * 7,
        out_specs=[whole(pl.ANY)] * 2,
        scratch_shapes=[
            pltpu.VMEM((total, wide), bf16),
            pltpu.VMEM((width, wide), bf16),
            pltpu.VMEM((LANES, width), f32),
            pltpu.SemaphoreType.DMA((dp_size,)),
        ],
    )(*parts, first, weights, side, small_grad, bias_grad)


def part_kernel(near, far, w_ref, *outs):
    cut = near.shape[2]
    weights = w_ref[:, :cut]
    for d in range(GROUP):
        outs[d][...] = mm_nt((near, far)[d // 2][d % 2], weights).astype(bf16)


def input_parts(ones, weight, gates=()):
    row_count, width = ones[0].shape[1], weight.shape[0]
    return launch(
        part_kernel,
        gates,
        mark=True,
        cost=2.5,
        out_shape=[jax.ShapeDtypeStruct((row_count, width), bf16)] * GROUP,
        in_specs=[whole()] * 3,
        out_specs=[whole()] * GROUP,
    )(*ones, weight)


def last_kernel(token_ref, dmixed_ref, small_ref, *refs):
    begun, (near, core, over), weights = refs[:3], refs[3:6], refs[6 : 6 + GROUP]
    out_ref = refs[6 + GROUP]
    unit, inverse = norm_parts(token_ref[...].astype(f32))
    df = sum(v[...].astype(f32) for v in begun)
    for d, two in enumerate((near.at[0], core.at[0], over.at[0], core.at[1])):
        df = df + mm_nt(two[...], weights[d][...])
    back = norm_back(df * small_ref[0:1], unit, inverse)
    out_ref[...] = (dmixed_ref[...] + back).astype(bf16)


def finish_input(tokens, dmixed, small, begun, twos, weights, gates=()):
    return launch(
        last_kernel,
        gates,
        mark=True,
        cost=3.0,
        out_shape=jax.ShapeDtypeStruct(tokens.shape, bf16),
        in_specs=[whole()] * (9 + GROUP),
        out_specs=whole(),
    )(tokens, dmixed, small, *begun, *twos, *weights)


def place_ffn_kernel(*refs):
    shares, in_ref, down_ref = refs[:4], refs[4], refs[5]
    rows, ff = in_ref.shape
    width = down_ref.shape[1]
    low = group_index()
    for case in range(GROUP):

        @pl.when(low == case)
        def _():
            for d in range(GROUP):
                whose = case ^ d
                down_ref[rows * whose : rows * (whose + 1)] = shares[d][:, width:].astype(f32)
                part = shares[d][:, :width].astype(f32)
                for i in range(width // rows):
                    at = 4 * rows * i + rows * whose
                    in_ref[:, at : at + rows] = part[:, rows * i : rows * (i + 1)]


def place_ffn(shares, gates=()):
    rows, wide = shares[0].shape
    width = wide // 2
    return launch(
        place_ffn_kernel,
        gates,
        mark=True,
        cost=3.0,
        out_shape=(
            jax.ShapeDtypeStruct((rows, 4 * width), f32),
            jax.ShapeDtypeStruct((4 * rows, width), f32),
        ),
        in_specs=[whole()] * 4,
        out_specs=[whole()] * 2,
    )(*shares)


def place_qkv_kernel(*refs):
    ones, twos, qkv_ref, out_ref = refs[:4], refs[4:8], refs[8], refs[9]
    rows, width = out_ref.shape
    low = group_index()
    vectors = twos[0][:, 128:].astype(f32)
    for d in range(1, GROUP):
        vectors = vectors + twos[d][:, 128:].astype(f32)
    vectors = vectors.T
    for i, vector_ref in enumerate(refs[10:]):
        for part in range(vector_ref.shape[0] // rows):
            at = 64 + i + part
            vector_ref[part * rows : (part + 1) * rows] = vectors[at : at + 1].reshape(rows)
    cut = width // 2
    halves = [
        ones[i][:, 3 * LANES :].astype(f32) + ones[i + 2][:, 3 * LANES :].astype(f32)
        for i in range(2)
    ]
    for case in range(GROUP):

        @pl.when(low == case)
        def _():
            for i in range(2):
                at = cut * ((case % 2) ^ i)
                out_ref[:, at : at + cut] = halves[i]
            for d in range(GROUP):
                whose = case ^ d
                one, two = ones[d][...].astype(f32), twos[d][...].astype(f32)

                def put(kind, h, part):
                    at = kind * width + 192 * whose + 64 * h
                    qkv_ref[:, at : at + 64] = part

                for h in range(2):
                    put(0, h, one[:, LANES * h : LANES * h + 64])
                    put(1, h, one[:, LANES * h + 64 : LANES * h + LANES])
                    put(2, h, one[:, 2 * LANES + 64 * h : 2 * LANES + 64 * h + 64])
                for kind in range(3):
                    put(kind, 2, two[:, 64 * kind : 64 * kind + 64])


def place_qkv(ones, twos, width, gates=()):
    rows = ones[0].shape[0]
    return launch(
        place_qkv_kernel,
        gates,
        cost=2.0,
        out_shape=(
            jax.ShapeDtypeStruct((rows, 3 * width), f32),
            jax.ShapeDtypeStruct((rows, width), f32),
            *[jax.ShapeDtypeStruct((rows,), f32)] * 5,
            jax.ShapeDtypeStruct((4 * rows,), f32),
        ),
        in_specs=[whole()] * 8,
        out_specs=[whole()] * 8,
    )(*ones, *twos)


def on_device(
    tokens,
    attn_gain,
    attn_shift,
    w_qkv,
    w_out,
    ffn_gain,
    ffn_shift,
    w_in,
    b_in,
    w_down,
    b_down,
    cotangent,
    lengths,
    block_order,
):
    mine = tokens[0]
    row_count, width = mine.shape
    ctx_size = lax.axis_size("ctx")
    dp_size = lax.axis_size("dp")
    far = ctx_size // GROUP
    rows = w_qkv.shape[0]
    half = row_count // 2
    assert math.gcd(H, ctx_size) == GROUP and w_down.shape[0] == GROUP * rows
    where = (lengths, block_order)

    vectors = [attn_gain, attn_shift, ffn_gain, ffn_shift, b_down, b_in]
    piece = pack(w_qkv, vectors)
    far_qkv = far_pieces(piece, "qkv")
    tok_side = swap(mine, "ctx", 1, "tokens_core")
    tok_over = swap(mine, "ctx", 2, "tokens_x")
    piece_in, piece_down = pack_ffn(w_out, w_in, w_down, gates=(piece, tok_side))
    near_qkv = jnp.stack(far_qkv)
    cross_qkv = swap(near_qkv, "dp", 1, "qkv_y")
    tok_over = after(tok_over, near_qkv)
    blocks = [mine, tok_side, tok_over, swap(tok_over, "ctx", 1, "tokens_pass")]
    cot = cotangent[0]

    query, keys, values, first, small, qkv_weight, weight_two = project(
        *where, blocks, near_qkv, cross_qkv
    )
    far_in = far_pieces(after(piece_in, near_qkv, blocks[3]), "in")
    cot_over = swap(after(cot, near_qkv), "ctx", 2, "cot_x")
    near_in = jnp.stack(far_in[:-1] + [after(far_in[-1], small)])
    if far > 1:
        groups = [[g * GROUP + i for g in range(far)] for i in range(GROUP)]
        keys = lax.all_gather(keys, "ctx", axis=1, tiled=True, axis_index_groups=groups)
        values = lax.all_gather(values, "ctx", axis=1, tiled=True, axis_index_groups=groups)

    far_attn, far_query, far_mark = attend(
        query, keys, values, 2, 2, row_count, gates=(near_in, cot_over)
    )
    cross_in = swap(near_in, "dp", 1, "in_y")
    weight_over = swap(weight_two, "ctx", 2, "weight_x")
    cot_side = swap(after(cot, far_mark), "ctx", 1, "cot_core")
    far_down = far_pieces(after(piece_down, near_in), "down")
    near_down = jnp.stack(far_down[:-1] + [after(far_down[-1], far_mark)])
    near_attn, near_query, near_mark = attend(
        query, keys, values, 0, 2, row_count, gates=(far_mark, near_down, weight_over)
    )
    over_attn = swap(far_attn, "ctx", 2, "attn_x")
    cross_down = swap(near_down, "dp", 1, "down_y")
    held_in = after(cross_in, near_mark)
    out_piece = jnp.concatenate([near_in[:, :, width:], held_in[:, :, width:]])
    out_pieces = [out_piece, swap(out_piece, "ctx", 1, "out_core")]
    core_attn = swap(jnp.stack([near_attn[1], over_attn[1]]), "ctx", 1, "attn_core")
    attn = [near_attn, core_attn, over_attn]

    mixed, second, w_o, mixed_mark = project_out(
        mine, attn, out_pieces, small, gates=(cross_down, cot_side)
    )
    side = swap(second, "ctx", 1, "second_core")
    cot_pass = swap(after(cot_over, mixed_mark), "ctx", 1, "cot_pass")
    cots = [cot, cot_side, cot_over, cot_pass]
    (own_part, side_part), weights = feed_forward(
        *where,
        small,
        [second, side],
        cots[:2],
        [near_in, held_in, near_down, cross_down],
        (0, 1),
    )
    *outs_near, out_mark = out_parts([own_part[1], side_part[1]], weights[1])
    if far == 1:
        probs_one, out_mark = attend_weights(
            near_query, far_query, keys, (0, 1), gates=(out_mark,)
        )
    over = after(swap(second, "ctx", 2, "second_x"), out_mark)
    ds_side = swap(side_part[0], "ctx", 1, "ds_core")
    weight_over = after(weight_over, out_mark)
    weight_pair = swap(jnp.stack([weight_two, weight_over]), "ctx", 1, "weight_core")
    two_weights = [weight_two, weight_pair[0], weight_over, weight_pair[1]]
    (over_part,), _ = feed_forward(
        *where, small, [over], cots[2:3], weights, (2,), gates=(out_mark, ds_side, cot_pass, weight_pair)
    )
    cross = after(swap(over, "ctx", 1, "second_pass"), over_part[0])
    (cross_part,), _ = feed_forward(*where, small, [cross], cots[3:], weights, (3,))
    parts = [own_part, side_part, over_part, cross_part]
    ds_sum = add(over_part[0], swap(cross_part[0], "ctx", 1, "ds_side"))
    even_ff, odd_ff, bias_grad, far_mark = ffn_grads(
        *where,
        cots,
        [second, side, over, cross],
        [part[1] for part in parts],
        [part[2] for part in parts],
        dp_size,
        gates=(ds_sum,),
    )
    *outs_far, far_mark = out_parts(
        [over_part[1], cross_part[1]], weights[1], gates=(far_mark,)
    )
    if far == 1:
        probs_two, far_mark = attend_weights(
            near_query, far_query, keys, (2,), gates=(far_mark,)
        )
    ds_over = swap(ds_sum, "ctx", 2, "ds_x")
    outs_own, outs_one = outs_near
    outs_two, outs_three = outs_far
    dmixed, small_grad, dattn, out_halves = mixed_back(
        *where,
        mixed,
        cot,
        small,
        w_o,
        attn,
        [own_part[0], ds_side, ds_over],
        gates=(far_mark,),
    )
    dattn_side = swap(dattn[1], "ctx", 1, "dattn_core")
    odd_sent = swap(odd_ff, "dp", 1, "ffn_y")
    outs_side = swap(after(outs_one, dattn_side), "ctx", 1, "outs_core")
    outs_back = swap(after(outs_three, dattn_side), "ctx", 1, "outs_side")

    out_sent = swap(after(out_halves[1], dattn_side), "ctx", 1, "dw_out_core")

    if far > 1:
        over = swap(dattn[2], "ctx", 2, "dattn_x")
        dattn = [dattn[0], dattn_side, over[0], swap(over[1], "ctx", 1, "dattn_pass")]
        ffn_even = add(even_ff, odd_sent)
        dk, dv, dq, _ = attend_back(
            [near_query, far_query],
            keys,
            values,
            [],
            [near_attn, far_attn],
            dattn,
            (0, 1, 2),
            (0, 1, 2, 3),
            "raw",
            (),
        )
        dk, dv = (
            lax.psum_scatter(v, "ctx", scatter_dimension=1, tiled=True, axis_index_groups=groups)
            for v in (dk, dv)
        )
        dq, dk, dv = (v[..., :64].astype(bf16) for v in (dq, dk, dv))
        one = jnp.concatenate([dq[0], dk[0], dq[1], dk[1], dv[0], dv[1]], axis=1)
        two = jnp.concatenate([dq[2], dk[2], dv[2], jnp.zeros_like(dv[2])], axis=1)
        ones, twos = (v.reshape(2, 2, row_count, v.shape[1]) for v in (one, two))
        ones_mark = ones[0]
        outs_sum = add(outs_two, outs_back)
    else:
        *begun, begun_mark = attend_back(
            [near_query],
            keys,
            values,
            [probs_one],
            [near_attn],
            [dattn[0], dattn_side],
            (0, 1),
            (0, 1),
            "begin",
            (),
        )
        over = after(swap(dattn[2], "ctx", 2, "dattn_x"), begun_mark)
        dattn = [dattn[0], dattn_side, over[0], swap(over[1], "ctx", 1, "dattn_pass")]
        ffn_even = add(even_ff, after(odd_sent, begun_mark, outs_side, outs_back, out_sent))
        outs_sum = add(outs_two, outs_back)
        *ones, ones_mark = attend_back(
            [far_query],
            keys,
            values,
            [probs_one],
            [far_attn],
            dattn[2:],
            (0, 1),
            (2, 3),
            "final",
            begun,
            gates=(ffn_even, outs_sum),
        )
    outs_over = after(swap(outs_sum, "ctx", 2, "outs_x"), ones_mark)
    ffn_share = scatter_far(ffn_even, "ffn", ones_mark)

    even, odd, part_sums, first_mark = first_grad(
        ones,
        first,
        qkv_weight,
        (out_halves[0], out_sent),
        dp_size,
    )
    *parts, _ = input_parts(ones, qkv_weight, gates=(first_mark, ffn_share[0]))
    part_side = swap(parts[1], "ctx", 1, "df_core")
    part_sum = add(parts[2], swap(parts[3], "ctx", 1, "df_side"))
    if far == 1:
        *twos, twos_mark = attend_back(
            [near_query, far_query],
            keys,
            values,
            [probs_two],
            [near_attn, far_attn],
            dattn,
            (2,),
            (0, 1, 2, 3),
            "final",
            (),
            gates=(first_mark, part_sum, outs_over, part_side),
        )
    else:
        twos_mark = twos[0]
    part_over = swap(part_sum, "ctx", 2, "df_x")
    ffn_share = ffn_share[1](twos_mark)
    one_even = add(even, after(swap(odd, "dp", 1, "one_y"), twos_mark))
    ffn_share = sum_groups(ffn_share)
    even, odd, second_mark = second_grad(
        twos,
        first,
        qkv_weight,
        part_sums,
        small_grad,
        bias_grad,
        dp_size,
        gates=(ffn_share,),
    )
    one_share = scatter_far(one_even, "one", second_mark)
    two_even = add(even, swap(odd, "dp", 1, "two_y"))
    part_over = after(part_over, second_mark)
    two_even = after(two_even, one_share[0], part_over)
    ffn_over = swap(ffn_share, "ctx", 2, "ffn_x")
    layer_out, out_mark = finish_out(
        *where, mixed, small, [outs_own, outs_side, outs_over], gates=(two_even,)
    )
    two_share = scatter_far(two_even, "two", out_mark)
    one_share = sum_groups(one_share[1](None))
    two_share = sum_groups(two_share[1](None))
    two_shares = gather_group(two_share, "two")
    ffn_over = after(ffn_over, two_shares[2])
    dtwos = exchange_pairs(*twos, "dtwos", two_shares[2])
    ffn_pair = swap(jnp.stack([ffn_share, ffn_over]), "ctx", 1, "ffn_core")
    ffn_shares = [ffn_share, ffn_pair[0], ffn_over, ffn_pair[1]]
    input_grad, input_mark = finish_input(
        mine,
        dmixed,
        small,
        [parts[0], part_side, part_over],
        dtwos,
        two_weights,
    )
    grad_w_in, grad_w_down, ffn_mark = place_ffn(ffn_shares, gates=(input_mark,))
    one_shares = gather_pairs(one_share, "one", two_share)
    grad_w_qkv, grad_w_out, *vector_grads, grad_b_in = place_qkv(
        one_shares, two_shares, width, gates=(ffn_mark,)
    )
    return (
        layer_out[None],
        input_grad[None],
        vector_grads[0],
        vector_grads[1],
        grad_w_qkv,
        grad_w_out,
        vector_grads[2],
        vector_grads[3],
        grad_w_in,
        grad_b_in,
        grad_w_down,
        vector_grads[4],
    )


def solution(mesh):
    placed = (
        P("dp", "ctx", None),
        P("dp"),
        P("dp"),
        P("dp", None),
        P("dp", None),
        P("dp"),
        P("dp"),
        P("dp", None),
        P("dp"),
        P("dp", None),
        P("dp"),
        P("dp", "ctx", None),
        P("dp"),
        P("dp", None),
    )
    return jax.shard_map(
        on_device,
        mesh=mesh,
        in_specs=placed,
        out_specs=(
            P("dp", "ctx", None),
            P("dp", "ctx", None),
            P("dp"),
            P("dp"),
            P("dp", None),
            P("dp", None),
            P("dp"),
            P("dp"),
            P("dp", None),
            P("dp"),
            P("dp", None),
            P("dp"),
        ),
        check_vma=False,
    )
```

```python
import functools
import math

import jax
import jax.numpy as jnp
from jax import lax
from jax.experimental import pallas as pl
from jax.experimental.pallas import tpu as pltpu
from jax.sharding import PartitionSpec as P

H = 12

epsilon = 1e-05
gelu_coeff = 0.7978845608
cubic_term = 0.044715
excluded = -1073741824.0
bf16 = jnp.bfloat16
f32 = jnp.float32
LANES = 128
GROUP = 4
VMEM_SMALL = 14 * 1024 * 1024
VMEM_LARGE = 52 * 1024 * 1024
VMEM_MOST = 62 * 1024 * 1024

nt_dims = (((1,), (1,)), ((), ()))
tn_dims = (((0,), (0,)), ((), ()))


def mm(left, right):
    return jnp.dot(left, right, preferred_element_type=f32)


def mm_nt(left, right):
    return lax.dot_general(left, right, nt_dims, preferred_element_type=f32)


def mm_tn(left, right):
    return lax.dot_general(left, right, tn_dims, preferred_element_type=f32)


def whole(memory_space=pltpu.VMEM):
    return pl.BlockSpec(memory_space=memory_space)


def lanes_of(shape):
    return lax.broadcasted_iota(jnp.int32, shape, 1)


def norm_parts(values):
    center = values - jnp.mean(values, axis=-1, keepdims=True)
    spread = jnp.mean(center * center, axis=-1, keepdims=True)
    inverse = lax.rsqrt(spread + epsilon)
    return center * inverse, inverse


def norm_back(scaled, unit, inverse):
    return inverse * (
        scaled
        - jnp.mean(scaled, axis=-1, keepdims=True)
        - unit * jnp.mean(scaled * unit, axis=-1, keepdims=True)
    )


def three_parts(value):
    first = value.astype(bf16).astype(f32)
    rest = value - first
    second = rest.astype(bf16).astype(f32)
    return first, second, rest - second


def with_parts(base, value):
    lane = lanes_of(base.shape)
    one, two, three = three_parts(value)
    return jnp.where(
        lane == 64, one, jnp.where(lane == 65, two, jnp.where(lane == 66, three, base))
    )


def unpack_rows(packed, rows):
    tail = jnp.concatenate([packed[rows:, :64], packed[rows:, 64:]], axis=0)
    return packed[:rows], tail


def swap(value, axis, bit, name):
    size = lax.axis_size(axis)
    with jax.named_scope(name):
        return lax.ppermute(value, axis, [(i, i ^ bit) for i in range(size)])


def launch(kernel, gates, in_specs, cost=1.0, vmem=VMEM_SMALL, mark=False, **options):
    count = len(gates)
    place = None
    if mark:
        shapes, specs = options["out_shape"], options["out_specs"]
        if not isinstance(shapes, (list, tuple)):
            shapes, specs = [shapes], [specs]
        place = count + len(in_specs) + len(shapes)
        options["out_shape"] = [*shapes, jax.ShapeDtypeStruct((8, LANES), f32)]
        options["out_specs"] = [*specs, whole()]

    def gated(*refs):
        refs = list(refs)
        if mark:
            refs.pop(place)[...] = jnp.zeros((8, LANES), f32)
        kernel(*refs[count:])

    call = pl.pallas_call(
        gated,
        in_specs=[whole(pl.ANY)] * count + in_specs,
        compiler_params=pltpu.CompilerParams(vmem_limit_bytes=vmem),
        cost_estimate=pl.CostEstimate(
            flops=int(cost * 2e7), bytes_accessed=1024, transcendentals=0
        ),
        **options,
    )
    return lambda *operands: call(*gates, *operands)


def hold_kernel(value_ref, out_ref):
    pass


def after(value, *gates):
    return launch(
        hold_kernel,
        gates,
        [whole(pl.ANY)],
        out_shape=jax.ShapeDtypeStruct(value.shape, value.dtype),
        out_specs=whole(pl.ANY),
        input_output_aliases={len(gates): 0},
    )(value)


def far_pieces(piece, name):
    found = [piece]
    for k in range(1, lax.axis_size("dp") // 2):
        found.append(swap(piece, "dp", 2 * k, name + "_z"))
    return found


def add(left, right):
    return (left.astype(f32) + right.astype(f32)).astype(bf16)


def scatter_far(even, name, gate):
    def step(even, gate):
        half = even.shape[0] // 2
        bit = lax.axis_size("dp") // (2 * half)
        pairs = even.reshape(half, 2, *even.shape[1:])
        received = swap(pairs[:, 1], "dp", bit, name + "_z")
        return add(pairs[:, 0], received if gate is None else after(received, gate))

    begun = step(even, gate)

    def finish(gate):
        total = begun
        while total.shape[0] > 1:
            total = step(total, gate)
        return total[0]

    return begun, finish


def sum_groups(value):
    bit = GROUP
    while bit < lax.axis_size("ctx"):
        other = swap(value, "ctx", bit, "groups")
        value = (value.astype(f32) + other.astype(f32)).astype(bf16)
        bit *= 2
    return value


def gather_group(value, name, gate=None):
    over = swap(value, "ctx", 2, name + "_x")
    if gate is not None:
        over = after(over, gate)
    side = swap(value, "ctx", 1, name + "_core")
    return [value, side, over, swap(over, "ctx", 1, name + "_pass")]


def exchange_pairs(near, far, name, gate=None):
    over = swap(far, "ctx", 2, name + "_x")
    if gate is not None:
        over = after(over, gate)
    core = swap(jnp.stack([near[1], over[1]]), "ctx", 1, name + "_core")
    return [near, core, over]


def gather_pairs(value, name, gate=None):
    over = swap(value, "ctx", 2, name + "_x")
    if gate is not None:
        over = after(over, gate)
    pair = swap(jnp.stack([value, over]), "ctx", 1, name + "_core")
    return [value, pair[0], over, pair[1]]


def position_of(order_ref, slot, rows):
    index = lax.axis_index("ctx")
    return order_ref[0, lax.bitwise_xor(index, slot)] * rows


def valid_rows(length_ref, order_ref, slot, rows):
    stored = lax.broadcasted_iota(jnp.int32, (rows, LANES), 0)[:, :1]
    position = position_of(order_ref, slot, rows) + stored
    return jnp.where(position < length_ref[0], 1.0, 0.0)


def group_index():
    return lax.rem(lax.axis_index("ctx"), GROUP)


def load_pieces(sources, target, sems, first_sem=0):
    me = lax.axis_index("dp")
    copies = []
    for source, differences in sources:
        rows = source.shape[1]
        for k, difference in enumerate(differences):
            owner = lax.bitwise_xor(me, difference)
            copies.append(
                pltpu.make_async_copy(
                    source.at[k],
                    target.at[pl.ds(pl.multiple_of(owner * rows, 16), rows)],
                    sems.at[first_sem + len(copies)],
                )
            )
    for copy in copies:
        copy.start()
    return copies


def near_and_cross(near, cross):
    halves = near.shape[0]
    return [(near, [2 * k for k in range(halves)]), (cross, [2 * k + 1 for k in range(halves)])]


def store_pieces(source, even, odd, sems):
    halves, rows, _ = even.shape
    me = lax.axis_index("dp")
    copies = []
    for parity, target in ((0, even), (1, odd)):
        for k in range(halves):
            owner = lax.bitwise_xor(me, 2 * k + parity)
            copies.append(
                pltpu.make_async_copy(
                    source.at[pl.ds(pl.multiple_of(owner * rows, 16), rows)],
                    target.at[k],
                    sems.at[2 * k + parity],
                )
            )
    for copy in copies:
        copy.start()
    for copy in copies:
        copy.wait()


def pack_kernel(w_hbm, *refs):
    w_ref, sems = refs[-2:]
    count = (len(refs) - 3) // 2
    vectors, out_ref, held = refs[:count], refs[count], refs[count + 1 : -2]
    copies = [pltpu.make_async_copy(w_hbm, w_ref, sems.at[count])]
    for i in range(count):
        copies.append(pltpu.make_async_copy(vectors[i], held[i], sems.at[i]))
    for copy in copies:
        copy.start()
    for copy in copies:
        copy.wait()
    rows = w_ref.shape[0]
    width = w_ref.shape[1] // 3
    low = group_index()
    stacked = []
    for v in held:
        flat = v[...].astype(f32).reshape(1, v.shape[0])
        stacked += [flat[:, i : i + rows] for i in range(0, v.shape[0], rows)]
    stacked.append(jnp.zeros((LANES - len(stacked), rows), f32))
    small = jnp.concatenate(stacked, axis=0).T[:, :64].astype(bf16)
    for case in range(GROUP):

        @pl.when(low == case)
        def _():
            def head(kind, h):
                at = kind * width + 192 * case + 64 * h
                return w_ref[:, at : at + 64]

            out_ref[...] = jnp.concatenate(
                [
                    head(0, 0),
                    head(1, 0),
                    head(0, 1),
                    head(1, 1),
                    head(2, 0),
                    head(2, 1),
                    head(0, 2),
                    head(1, 2),
                    head(2, 2),
                    small,
                ],
                axis=1,
            )


def pack(w_qkv, vectors, gates=()):
    rows = w_qkv.shape[0]
    return launch(
        pack_kernel,
        gates,
        vmem=VMEM_MOST,
        cost=1.0,
        out_shape=jax.ShapeDtypeStruct((rows, 640), bf16),
        in_specs=[whole(pltpu.HBM)] * (1 + len(vectors)),
        out_specs=whole(),
        scratch_shapes=[pltpu.VMEM(v.shape, bf16) for v in vectors]
        + [pltpu.VMEM(w_qkv.shape, bf16), pltpu.SemaphoreType.DMA((1 + len(vectors),))],
    )(w_qkv, *vectors)


def pack_ffn_kernel(out_ref, in_ref, down_ref, one_ref, two_ref):
    rows, ff = in_ref.shape
    width = out_ref.shape[1]
    half = width // 2
    low = group_index()
    per = 4 * rows
    for case in range(GROUP):

        @pl.when(low == case)
        def _():
            at = half * (case % 2)
            parts = [
                in_ref[:, per * i + rows * case : per * i + rows * (case + 1)]
                for i in range(ff // per)
            ]
            one_ref[:, :width] = jnp.concatenate(parts, axis=1)
            one_ref[:, width:] = out_ref[:, at : at + half]
            two_ref[...] = down_ref[rows * case : rows * (case + 1)]


def pack_ffn(w_out, w_in, w_down, gates=()):
    rows, width = w_out.shape
    return launch(
        pack_ffn_kernel,
        gates,
        cost=1.0,
        out_shape=(
            jax.ShapeDtypeStruct((rows, width + width // 2), bf16),
            jax.ShapeDtypeStruct((rows, width), bf16),
        ),
        in_specs=[whole()] * 3,
        out_specs=[whole()] * 2,
    )(w_out, w_in, w_down)


def qkv_kernel(length_ref, order_ref, *refs):
    tokens = refs[:GROUP]
    near, cross = refs[GROUP : GROUP + 2]
    q_ref, k_ref, v_ref, first_ref, small_ref, w_ref, w_two_ref, sems = refs[GROUP + 2 :]
    row_count, width = tokens[0].shape
    for copy in load_pieces(near_and_cross(near, cross), w_ref, sems):
        copy.wait()
    w_two_ref[...] = w_ref[:, 384:640]
    small = w_ref[:, 512:640].astype(f32).T
    small_ref[...] = small[64:80]
    gain, shift = small[64:65], small[65:66]
    length = length_ref[0]
    lane = lanes_of((row_count, LANES))
    ones = jnp.where((lane >= 64) & (lane < 67), 1.0, 0.0)
    bias_lane = jnp.where(lane == 67, 1.0, 0.0)
    for d in range(GROUP):
        unit, _ = norm_parts(tokens[d][...].astype(f32))
        first = (unit * gain + shift).astype(bf16)
        part = pl.ds(d * row_count, row_count)
        first_ref[part] = first
        qkv = mm(first, w_ref[...]).astype(bf16).astype(f32)

        def head(place):
            block = qkv[:, place // 2 * LANES : (place // 2 + 1) * LANES]
            if place % 2:
                block = pltpu.roll(block, 64, 1)
            return jnp.where(lane < 64, block, 0.0)

        stored = lax.broadcasted_iota(jnp.int32, (row_count, LANES), 0)
        position = position_of(order_ref, d, row_count) + stored
        bias = jnp.where(position < length, 0.0, excluded) * bias_lane
        for h, (at_q, at_k, at_v) in enumerate(((0, 1, 4), (2, 3, 5), (6, 7, 8))):
            q_ref[h, part] = (head(at_q) * 0.125 + bias_lane).astype(bf16)
            k_ref[h, part] = (head(at_k) + ones + bias).astype(bf16)
            v_ref[h, part] = (head(at_v) + ones).astype(bf16)


def project(length, order, tokens, near, cross, gates=()):
    row_count, width = tokens[0].shape
    total = GROUP * row_count
    wide = near.shape[2]
    head_out = jax.ShapeDtypeStruct((3, total, LANES), bf16)
    return launch(
        qkv_kernel,
        gates,
        cost=10.0,
        out_shape=(
            head_out,
            head_out,
            head_out,
            jax.ShapeDtypeStruct((total, width), bf16),
            jax.ShapeDtypeStruct((16, width), f32),
            jax.ShapeDtypeStruct((width, wide), bf16),
            jax.ShapeDtypeStruct((width, 256), bf16),
        ),
        in_specs=[whole(pltpu.SMEM)] * 2 + [whole()] * GROUP + [whole(pl.ANY)] * 2,
        out_specs=[whole()] * 7,
        scratch_shapes=[pltpu.SemaphoreType.DMA((2 * near.shape[0],))],
    )(length, order, *tokens, near, cross)


def attend_kernel(block_rows, q_ref, k_ref, v_ref, packed_ref, q_out_ref):
    row_count = q_ref.shape[1]
    half = row_count // 2
    lane = lanes_of((block_rows, LANES))
    for i in range(row_count // block_rows):
        part = pl.ds(i * block_rows, block_rows)
        heads = []
        for h in range(3):
            query = q_ref[h, part]
            scores = mm_nt(query, k_ref[h])
            top = jnp.max(scores, axis=1, keepdims=True)
            weights = jnp.exp(scores - top).astype(bf16)
            result = mm(weights, v_ref[h])
            denom = result[:, 64:65]
            heads.append(jnp.where(lane < 64, result / denom, 0.0))
            log_total = top + jnp.log(denom)
            q_out_ref[h, part] = with_parts(query.astype(f32), -log_total).astype(bf16)
        packed_ref[0, part] = (heads[0] + pltpu.roll(heads[1], 64, 1)).astype(bf16)
        for r in range(0, block_rows, half):
            size = min(half, block_rows)
            row = i * block_rows + r
            side, place = row // half, row % half
            packed_ref[
                0, pl.ds(row_count + place, size), 64 * side : 64 * side + 64
            ] = heads[2][r : r + size, :64].astype(bf16)


def attend(query, keys, values, first_slot, slots, row_count, gates=()):
    total = keys.shape[1]
    block_rows = min(row_count // 2, 256)
    return launch(
        functools.partial(attend_kernel, block_rows),
        gates,
        mark=True,
        cost=5.0 * slots,
        vmem=VMEM_LARGE if total > GROUP * row_count else VMEM_SMALL,
        grid=(slots,),
        out_shape=(
            jax.ShapeDtypeStruct((slots, row_count * 3 // 2, LANES), bf16),
            jax.ShapeDtypeStruct((3, slots * row_count, LANES), bf16),
        ),
        in_specs=[
            pl.BlockSpec((3, row_count, LANES), lambda s: (0, s + first_slot, 0)),
            whole(),
            whole(),
        ],
        out_specs=(
            pl.BlockSpec((1, row_count * 3 // 2, LANES), lambda s: (s, 0, 0)),
            pl.BlockSpec((3, row_count, LANES), lambda s: (0, s, 0)),
        ),
    )(query, keys, values)


def weights_kernel(near_ref, far_ref, k_ref, out_ref):
    query = jnp.where(pl.program_id(1) < 2, near_ref[0], far_ref[0])
    rows = query.shape[0]
    for c in range(k_ref.shape[1] // rows):
        at = pl.ds(c * rows, rows)
        out_ref[0, 0, at] = jnp.exp(mm_nt(k_ref[0, at], query)).astype(bf16)


def attend_weights(near_query, far_query, keys, heads, gates=()):
    row_count = near_query.shape[1] // 2
    total = keys.shape[1]
    first = heads[0]
    return launch(
        weights_kernel,
        gates,
        mark=True,
        cost=3.0 * len(heads),
        grid=(len(heads), GROUP),
        out_shape=jax.ShapeDtypeStruct((len(heads), GROUP, total, row_count), bf16),
        in_specs=[
            pl.BlockSpec((1, row_count, LANES), lambda h, s: (h + first, jnp.minimum(s, 1), 0)),
            pl.BlockSpec((1, row_count, LANES), lambda h, s: (h + first, jnp.maximum(s - 2, 0), 0)),
            pl.BlockSpec((1, total, LANES), lambda h, s: (h + first, 0, 0)),
        ],
        out_specs=pl.BlockSpec((1, 1, total, row_count), lambda h, s: (h, s, 0, 0)),
    )(near_query, far_query, keys)


def group_attn(refs, row_count):
    near, core, over = refs
    packed = (near[0], core[0], over[0], core[1])
    return [jnp.concatenate(unpack_rows(v, row_count), axis=1) for v in packed]


def out_kernel(token_ref, *refs):
    attn_refs, pieces = refs[:3], refs[3:5]
    small_ref, mixed_ref, second_ref, w_o, sems = refs[5:]
    row_count, width = token_ref.shape
    half = width // 2
    number = pieces[0].shape[0]
    low = group_index()
    core = lax.rem(low, 2)
    differences = [2 * k for k in range(number // 2)] + [2 * k + 1 for k in range(number // 2)]
    copies = []
    for side in range(2):
        column = pl.multiple_of((core if side == 0 else 1 - core) * half, LANES)
        target = w_o.at[:, pl.ds(column, half)]
        copies += load_pieces([(pieces[side], differences)], target, sems, side * number)
    mixed = token_ref[...].astype(f32)
    attn = group_attn(attn_refs, row_count)
    for copy in copies:
        copy.wait()
    for d in range(GROUP):
        at = pl.ds(pl.multiple_of(lax.bitwise_xor(low, d) * 192, 16), 192)
        mixed = mixed + mm(attn[d], w_o[at, :])
    mixed_ref[...] = mixed
    unit, _ = norm_parts(mixed)
    second_ref[...] = (unit * small_ref[2:3] + small_ref[3:4]).astype(bf16)


def project_out(tokens, attn, pieces, small, gates=()):
    row_count, width = tokens.shape
    number = pieces[0].shape[0]
    return launch(
        out_kernel,
        gates,
        mark=True,
        cost=4.5,
        out_shape=(
            jax.ShapeDtypeStruct((row_count, width), f32),
            jax.ShapeDtypeStruct((row_count, width), bf16),
            jax.ShapeDtypeStruct((width, width), bf16),
        ),
        in_specs=[whole()] * 4 + [whole(pl.ANY)] * 2 + [whole()],
        out_specs=[whole()] * 3,
        scratch_shapes=[pltpu.SemaphoreType.DMA((2 * number,))],
    )(tokens, *attn, *pieces, small)


def ffn_kernel(slots, gathers, length_ref, order_ref, small_ref, *refs):
    number = len(slots)
    seconds, cots = refs[:number], refs[number : 2 * number]
    refs = refs[2 * number :]
    count = 4 if gathers else 2
    sources, refs = refs[:count], refs[count:]
    outs = [refs[3 * i : 3 + 3 * i] for i in range(number)]
    refs = refs[3 * number :]
    rows, width = seconds[0].shape
    if gathers:
        w_i, w_d, sems = refs
        near, cross, near_down, cross_down = sources
        parts = near_and_cross(*(v.at[:, :, pl.ds(0, width)] for v in (near, cross)))
        in_copies = load_pieces(parts, w_i, sems)
        down_copies = load_pieces(near_and_cross(near_down, cross_down), w_d, sems, 2 * gathers)
        for copy in in_copies:
            copy.wait()
    else:
        w_i, w_d = sources
    bias = small_ref[pl.ds(5 + group_index(), 1)]
    for i, slot in enumerate(slots):
        ds_ref, active_ref, dhid_ref = outs[i]
        row_count = cots[i].shape[0]
        valid = valid_rows(length_ref, order_ref, slot, row_count)
        dlow = (cots[i][...].astype(f32) * valid).astype(bf16)
        hidden = mm(seconds[i][...], w_i[...]) + bias
        squared = hidden * hidden
        bent = jnp.tanh(hidden * (gelu_coeff + gelu_coeff * cubic_term * squared))
        plus = 0.5 + 0.5 * bent
        slope = plus + hidden * (plus * (1.0 - bent)) * (
            gelu_coeff + gelu_coeff * 3.0 * cubic_term * squared
        )
        active_ref[...] = (hidden * plus).astype(bf16)
        if gathers and i == 0:
            for copy in down_copies:
                copy.wait()
        dhid = (mm_nt(dlow, w_d[...]) * slope).astype(bf16)
        dhid_ref[...] = dhid
        ds_ref[...] = mm_nt(dhid, w_i[...]).astype(bf16)


def feed_forward(length, order, small, seconds, cots, weights, slots, gates=()):
    rows, width = seconds[0].shape
    gathers = weights[0].shape[0] if len(weights) == 4 else 0
    number = len(slots)
    block = jax.ShapeDtypeStruct((rows, width), bf16)
    square = jax.ShapeDtypeStruct((width, width), bf16)
    results = launch(
        functools.partial(ffn_kernel, slots, gathers),
        gates,
        cost=3.0 * number,
        out_shape=[block] * (3 * number) + [square] * (2 if gathers else 0),
        in_specs=[whole(pltpu.SMEM)] * 2
        + [whole()] * (1 + 2 * number)
        + [whole(pl.ANY) if gathers else whole()] * len(weights),
        out_specs=[whole()] * (3 * number + (2 if gathers else 0)),
        scratch_shapes=[pltpu.SemaphoreType.DMA((4 * gathers,))] if gathers else [],
    )(length, order, small, *seconds, *cots, *weights)
    grouped = [results[3 * i : 3 * i + 3] for i in range(number)]
    return grouped, results[3 * number :]


def out_part_kernel(*refs):
    w_d = refs[2][...]
    for i in range(2):
        refs[3 + i][...] = mm(refs[i][...], w_d).astype(bf16)


def out_parts(actives, w_down, gates=()):
    return launch(
        out_part_kernel,
        gates,
        mark=True,
        cost=2.0,
        out_shape=[jax.ShapeDtypeStruct(v.shape, bf16) for v in actives],
        in_specs=[whole()] * 3,
        out_specs=[whole()] * 2,
    )(*actives, w_down)


def ffn_grad_kernel(length_ref, order_ref, *refs):
    cots, seconds, actives, dhids = (refs[i : i + GROUP] for i in range(0, 4 * GROUP, GROUP))
    even, odd, bias_ref, g_ref, sems = refs[4 * GROUP :]
    row_count, width = cots[0].shape
    bias = jnp.zeros((1, width), f32)
    grad_in = jnp.zeros((width, width), f32)
    for d in range(GROUP):
        dhid = dhids[d][...]
        bias = bias + jnp.sum(dhid.astype(f32), axis=0, keepdims=True)
        grad_in = grad_in + mm_tn(seconds[d][...], dhid)
    g_ref[:, :width] = grad_in.astype(bf16)
    bias_ref[...] = bias
    grad_down = jnp.zeros((width, width), f32)
    for d in range(GROUP):
        valid = valid_rows(length_ref, order_ref, d, row_count)
        dlow = (cots[d][...].astype(f32) * valid).astype(bf16)
        grad_down = grad_down + mm_tn(actives[d][...], dlow)
    g_ref[:, width:] = grad_down.astype(bf16)
    store_pieces(g_ref, even, odd, sems)


def ffn_grads(length, order, cots, seconds, actives, dhids, dp_size, gates=()):
    width = cots[0].shape[1]
    halves = dp_size // 2
    piece = jax.ShapeDtypeStruct((halves, width // dp_size, 2 * width), bf16)
    return launch(
        ffn_grad_kernel,
        gates,
        mark=True,
        cost=7.0,
        out_shape=(piece, piece, jax.ShapeDtypeStruct((1, width), f32)),
        in_specs=[whole(pltpu.SMEM)] * 2 + [whole()] * (4 * GROUP),
        out_specs=[whole(pl.ANY)] * 2 + [whole()],
        scratch_shapes=[
            pltpu.VMEM((width, 2 * width), bf16),
            pltpu.SemaphoreType.DMA((dp_size,)),
        ],
    )(length, order, *cots, *seconds, *actives, *dhids)


def mixed_back_kernel(length_ref, order_ref, *refs):
    mixed_ref, cot_ref, small_ref, w_o = refs[:4]
    attn_refs = refs[4:7]
    ds_refs = refs[7:10]
    dmixed_ref, small_grad_ref = refs[10:12]
    own, side, over = refs[12:15]
    dattn_refs = (own, side, over.at[0], over.at[1])
    half_refs = refs[15:17]
    g_o = refs[17]
    row_count, width = mixed_ref.shape
    half = row_count // 2
    low = group_index()
    unit, inverse = norm_parts(mixed_ref[...])
    ds = sum(v[...].astype(f32) for v in ds_refs)
    valid = valid_rows(length_ref, order_ref, 0, row_count)
    dout = cot_ref[...].astype(f32) * valid
    dmixed = dout + norm_back(ds * small_ref[2:3], unit, inverse)
    dmixed_ref[...] = dmixed
    dbranch = dmixed.astype(bf16)

    def out_rows(d):
        return pl.ds(pl.multiple_of(lax.bitwise_xor(low, d) * 192, 16), 192)

    for d in range(GROUP):
        dattn = mm_nt(dbranch, w_o[out_rows(d), :])
        dattn_refs[d][pl.ds(0, row_count)] = dattn[:, :LANES].astype(bf16)
        dattn_refs[d][pl.ds(row_count, half), :64] = dattn[:half, LANES:].astype(bf16)
        dattn_refs[d][pl.ds(row_count, half), 64:] = dattn[half:, LANES:].astype(bf16)
    attn = group_attn(attn_refs, row_count)
    for d in range(GROUP):
        g_o[out_rows(d), :] = mm_tn(attn[d], dbranch).astype(bf16)
    core = lax.rem(low, 2)
    for here, half_ref in zip((core, 1 - core), half_refs):
        column = pl.multiple_of(here * (width // 2), LANES)
        half_ref[...] = g_o[:, pl.ds(column, width // 2)]
    small_grad_ref[...] = jnp.zeros_like(small_grad_ref)
    small_grad_ref[2:3] = jnp.sum(ds * unit, axis=0, keepdims=True)
    small_grad_ref[3:4] = jnp.sum(ds, axis=0, keepdims=True)
    small_grad_ref[4:5] = jnp.sum(dout, axis=0, keepdims=True)


def mixed_back(length, order, mixed, cot, small, w_o, attn, ds, gates=()):
    row_count, width = mixed.shape
    results = launch(
        mixed_back_kernel,
        gates,
        cost=7.0,
        out_shape=[
            jax.ShapeDtypeStruct((row_count, width), f32),
            jax.ShapeDtypeStruct((16, width), f32),
        ]
        + [jax.ShapeDtypeStruct((row_count * 3 // 2, LANES), bf16)] * 2
        + [jax.ShapeDtypeStruct((2, row_count * 3 // 2, LANES), bf16)]
        + [jax.ShapeDtypeStruct((width, width // 2), bf16)] * 2,
        in_specs=[whole(pltpu.SMEM)] * 2 + [whole()] * 10,
        out_specs=[whole()] * 7,
        scratch_shapes=[pltpu.VMEM((width, width), bf16)],
    )(length, order, mixed, cot, small, w_o, *attn, *ds)
    return results[0], results[1], results[2:5], results[5:7]


def layer_out_kernel(length_ref, order_ref, mixed_ref, small_ref, *refs):
    own, side, over, out_ref = refs
    row_count = mixed_ref.shape[0]
    valid = valid_rows(length_ref, order_ref, 0, row_count)
    total = mixed_ref[...] + own[...].astype(f32) + side[...].astype(f32) + over[...].astype(f32)
    out_ref[...] = ((total + small_ref[4:5]) * valid).astype(bf16)


def finish_out(length, order, mixed, small, parts, gates=()):
    return launch(
        layer_out_kernel,
        gates,
        mark=True,
        cost=3.0,
        out_shape=jax.ShapeDtypeStruct(mixed.shape, bf16),
        in_specs=[whole(pltpu.SMEM)] * 2 + [whole()] * 5,
        out_specs=whole(),
    )(length, order, mixed, small, *parts)


def attend_back_kernel(mode, heads, slots, row_count, starts, *refs):
    number = len(slots)
    pairs = number // 2
    q_refs, (k_ref, v_ref) = refs[:pairs], refs[pairs : pairs + 2]
    refs = refs[pairs + 2 :]
    if mode != "raw":
        prob_ref, refs = refs[0], refs[1:]
    attn_refs, dattn_refs = refs[:pairs], refs[pairs : pairs + number]
    refs = refs[pairs + number :]
    if starts:
        dk_in, dv_in, dq_in = refs[:3]
        refs = refs[3:]
    outs = refs[:-5]
    grad_ref, k_turned, dq_ref, dk_ref, dv_ref = refs[-5:]
    head, step = pl.program_id(0), pl.program_id(1)
    total = k_ref.shape[1]
    chunk = row_count
    first_slot = slots[0] if mode == "final" else 0

    @pl.when((head == 0) & (step == 0))
    def _():
        lane = lanes_of((row_count, LANES))
        for d in range(number):
            top, tail = unpack_rows(dattn_refs[d][...].astype(f32), row_count)
            top_a, tail_a = unpack_rows(attn_refs[d // 2][d % 2].astype(f32), row_count)
            product = top * top_a
            for i, h in enumerate(heads):
                if h == 0:
                    block = top
                    delta = jnp.sum(jnp.where(lane < 64, product, 0.0), axis=1, keepdims=True)
                elif h == 1:
                    block = pltpu.roll(top, 64, 1)
                    delta = jnp.sum(jnp.where(lane >= 64, product, 0.0), axis=1, keepdims=True)
                else:
                    block = jnp.concatenate([tail, tail], axis=1)
                    delta = jnp.sum(tail * tail_a, axis=1, keepdims=True)
                base = jnp.where(lane < 64, block, 0.0)
                grad_ref[i, pl.ds(d * row_count, row_count)] = with_parts(base, -delta).astype(bf16)

    @pl.when(step == 0)
    def _():
        k_turned[...] = k_ref[0].astype(f32).T.astype(bf16)
        if starts:
            dk_ref[...] = dk_in[0]
            dv_ref[...] = dv_in[0]
            dq_ref[: first_slot * row_count] = dq_in[0]
        else:
            dk_ref[...] = jnp.zeros_like(dk_ref)
            dv_ref[...] = jnp.zeros_like(dv_ref)

    query = q_refs[0][0]
    if pairs > 1:
        query = jnp.where(step < 2, query, q_refs[1][0])
    grad = grad_ref[head, pl.ds(pl.multiple_of(step * row_count, row_count), row_count)]
    turned = jnp.zeros((LANES, row_count), f32)
    for c in range(total // chunk):
        at = pl.ds(c * chunk, chunk)
        if mode == "raw":
            probs = jnp.exp(mm_nt(k_ref[0, at], query)).astype(bf16)
        else:
            probs = prob_ref[0, 0, at]
        dscores = (probs.astype(f32) * mm_nt(v_ref[0, at], grad)).astype(bf16)
        dv_ref[at] += mm(probs, grad)
        dk_ref[at] += mm(dscores, query)
        turned = turned + mm(k_turned[:, at], dscores)
    place = pl.multiple_of((first_slot + step) * row_count, row_count)
    dq_ref[pl.ds(place, row_count)] = turned.T * 0.125

    @pl.when(step == number - 1)
    def _():
        if mode != "final":
            outs[0][0] = dk_ref[...]
            outs[1][0] = dv_ref[...]
            outs[2][0] = dq_ref[...]
            return
        lane = lanes_of((row_count, LANES))
        last_at = LANES * len(heads)
        for i in range(len(heads)):

            @pl.when(head == i)
            def _():
                for d in range(GROUP):
                    at = pl.ds(d * row_count, row_count)
                    pair = jnp.where(lane < 64, dq_ref[at], pltpu.roll(dk_ref[at], 64, 1))
                    out = outs[d // 2].at[d % 2]
                    out[:, i * LANES : (i + 1) * LANES] = pair.astype(bf16)
                    value = dv_ref[at]
                    if i == 0:
                        value = jnp.where(lane < 64, value, 0.0)
                        out[:, last_at : last_at + LANES] = value.astype(bf16)
                    else:
                        out[:, last_at + 64 : last_at + LANES] = value[:, :64].astype(bf16)


def attend_back(queries, keys, values, probs, attn, dattn, heads, slots, mode, begun, gates=()):
    row_count = dattn[0].shape[0] * 2 // 3
    total = keys.shape[1]
    number = len(slots)
    kept = GROUP if mode == "final" else number
    first_head = heads[0]
    if number == 2:
        places = [lambda h, s: (h + first_head, s, 0)]
    else:
        places = [
            lambda h, s: (h + first_head, jnp.minimum(s, 1), 0),
            lambda h, s: (h + first_head, jnp.maximum(s - 2, 0), 0),
        ]

    def per_head(size):
        return (
            jax.ShapeDtypeStruct((len(heads), size, LANES), f32),
            pl.BlockSpec((1, size, LANES), lambda h, s: (h, 0, 0)),
        )

    if mode == "final":
        wide = LANES * (len(heads) + 1)
        outs = [
            (
                jax.ShapeDtypeStruct((2, row_count, wide), bf16),
                pl.BlockSpec((2, row_count, wide), lambda h, s: (0, 0, 0)),
            )
        ] * 2
    else:
        outs = [per_head(total), per_head(total), per_head(number * row_count)]
    begun_specs = []
    if begun:
        begun_specs = [
            pl.BlockSpec((1, v.shape[1], LANES), lambda h, s: (h, 0, 0)) for v in begun
        ]
    return launch(
        functools.partial(attend_back_kernel, mode, heads, slots, row_count, bool(begun)),
        gates,
        mark=True,
        cost=3.2 * number * len(heads),
        vmem=VMEM_LARGE if total > GROUP * row_count else VMEM_SMALL,
        grid=(len(heads), number),
        out_shape=[shape for shape, _ in outs],
        out_specs=[spec for _, spec in outs],
        in_specs=[
            pl.BlockSpec((1, row_count, LANES), place) for place in places
        ]
        + [pl.BlockSpec((1, total, LANES), lambda h, s: (h + first_head, 0, 0))] * 2
        + [
            pl.BlockSpec((1, 1, total, row_count), lambda h, s: (h, s + slots[0], 0, 0))
            for _ in probs
        ]
        + [whole()] * (len(attn) + number)
        + begun_specs,
        scratch_shapes=[
            pltpu.VMEM((len(heads), number * row_count, LANES), bf16),
            pltpu.VMEM((LANES, total), bf16),
            pltpu.VMEM((kept * row_count, LANES), f32),
            pltpu.VMEM((total, LANES), f32),
            pltpu.VMEM((total, LANES), f32),
        ],
    )(*queries, keys, values, *probs, *attn, *dattn, *begun)


def first_grad_kernel(*refs):
    parts, first_ref, w_ref, block_refs = refs[:2], refs[2], refs[3], refs[4:6]
    even, odd, side_ref, d_ref, g_ref, sems = refs[6:]
    _, row_count, wide = parts[0].shape
    for d in range(GROUP):
        d_ref[d * row_count : (d + 1) * row_count] = parts[d // 2][d % 2]
    weights = w_ref[...].astype(f32)
    grad = mm_tn(first_ref[...], d_ref[...])
    g_ref[:, :wide] = grad.astype(bf16)
    columns = jnp.sum(d_ref[...].astype(f32), axis=0, keepdims=True)
    shift = weights[:, 577:578]
    used = weights[:, :wide]
    gain_part = jnp.sum(used * (grad - shift * columns), axis=1, keepdims=True)
    shift_part = jnp.sum(used * columns, axis=1, keepdims=True)
    lane = lanes_of(side_ref.shape)
    side_ref[...] = jnp.where(lane == 64, gain_part, jnp.where(lane == 65, shift_part, 0.0))
    block = block_refs[0][...].astype(f32) + block_refs[1][...].astype(f32)
    g_ref[:, wide:] = block.astype(bf16)
    store_pieces(g_ref, even, odd, sems)


def first_grad(parts, first, weights, blocks, dp_size, gates=()):
    total, width = first.shape
    wide = parts[0].shape[2]
    piece = jax.ShapeDtypeStruct((dp_size // 2, width // dp_size, wide + width // 2), bf16)
    return launch(
        first_grad_kernel,
        gates,
        mark=True,
        cost=5.0,
        out_shape=(piece, piece, jax.ShapeDtypeStruct((width, LANES), f32)),
        in_specs=[whole()] * 6,
        out_specs=[whole(pl.ANY)] * 2 + [whole()],
        scratch_shapes=[
            pltpu.VMEM((total, wide), bf16),
            pltpu.VMEM((width, wide + width // 2), bf16),
            pltpu.SemaphoreType.DMA((dp_size,)),
        ],
    )(*parts, first, weights, *blocks)


def second_grad_kernel(*refs):
    parts = refs[:2]
    first_ref, w_ref, side_ref, small_grad_ref, bias_grad_ref = refs[2:7]
    even, odd, d_ref, g_ref, turn_ref, sems = refs[7:]
    _, row_count, wide = parts[0].shape
    width = first_ref.shape[1]
    for d in range(GROUP):
        d_ref[d * row_count : (d + 1) * row_count] = parts[d // 2][d % 2]
    weights = w_ref[...].astype(f32)
    grad = mm_tn(first_ref[...], d_ref[...])
    columns = jnp.sum(d_ref[...].astype(f32), axis=0, keepdims=True)
    gain, shift = weights[:, 576:577], weights[:, 577:578]
    used = weights[:, 640 - wide :]
    gain_part = jnp.sum(used * (grad - shift * columns), axis=1, keepdims=True)
    shift_part = jnp.sum(used * columns, axis=1, keepdims=True)
    gain_part = (gain_part + side_ref[:, 64:65]) / gain
    shift_part = shift_part + side_ref[:, 65:66]
    turn_ref[...] = jnp.zeros_like(turn_ref)
    turn_ref[64:80] = small_grad_ref[...]
    turn_ref[pl.ds(69 + group_index(), 1)] = bias_grad_ref[...]
    lane = lanes_of((width, LANES))
    last = jnp.where(lane < 64, grad[:, wide - LANES :], turn_ref[...].T)
    last = jnp.where(lane == 64, gain_part, jnp.where(lane == 65, shift_part, last))
    g_ref[:, : wide - LANES] = grad[:, : wide - LANES].astype(bf16)
    g_ref[:, wide - LANES :] = last.astype(bf16)
    store_pieces(g_ref, even, odd, sems)


def second_grad(parts, first, weights, side, small_grad, bias_grad, dp_size, gates=()):
    total, width = first.shape
    wide = parts[0].shape[2]
    piece = jax.ShapeDtypeStruct((dp_size // 2, width // dp_size, wide), bf16)
    return launch(
        second_grad_kernel,
        gates,
        mark=True,
        cost=0.01,
        out_shape=(piece, piece),
        in_specs=[whole()] * 7,
        out_specs=[whole(pl.ANY)] * 2,
        scratch_shapes=[
            pltpu.VMEM((total, wide), bf16),
            pltpu.VMEM((width, wide), bf16),
            pltpu.VMEM((LANES, width), f32),
            pltpu.SemaphoreType.DMA((dp_size,)),
        ],
    )(*parts, first, weights, side, small_grad, bias_grad)


def part_kernel(near, far, w_ref, *outs):
    cut = near.shape[2]
    weights = w_ref[:, :cut]
    for d in range(GROUP):
        outs[d][...] = mm_nt((near, far)[d // 2][d % 2], weights).astype(bf16)


def input_parts(ones, weight, gates=()):
    row_count, width = ones[0].shape[1], weight.shape[0]
    return launch(
        part_kernel,
        gates,
        mark=True,
        cost=2.5,
        out_shape=[jax.ShapeDtypeStruct((row_count, width), bf16)] * GROUP,
        in_specs=[whole()] * 3,
        out_specs=[whole()] * GROUP,
    )(*ones, weight)


def last_kernel(token_ref, dmixed_ref, small_ref, *refs):
    begun, (near, core, over), weights = refs[:3], refs[3:6], refs[6 : 6 + GROUP]
    out_ref = refs[6 + GROUP]
    unit, inverse = norm_parts(token_ref[...].astype(f32))
    df = sum(v[...].astype(f32) for v in begun)
    for d, two in enumerate((near.at[0], core.at[0], over.at[0], core.at[1])):
        df = df + mm_nt(two[...], weights[d][...])
    back = norm_back(df * small_ref[0:1], unit, inverse)
    out_ref[...] = (dmixed_ref[...] + back).astype(bf16)


def finish_input(tokens, dmixed, small, begun, twos, weights, gates=()):
    return launch(
        last_kernel,
        gates,
        mark=True,
        cost=3.0,
        out_shape=jax.ShapeDtypeStruct(tokens.shape, bf16),
        in_specs=[whole()] * (9 + GROUP),
        out_specs=whole(),
    )(tokens, dmixed, small, *begun, *twos, *weights)


def place_ffn_kernel(*refs):
    shares, in_ref, down_ref = refs[:4], refs[4], refs[5]
    rows, ff = in_ref.shape
    width = down_ref.shape[1]
    low = group_index()
    for case in range(GROUP):

        @pl.when(low == case)
        def _():
            for d in range(GROUP):
                whose = case ^ d
                down_ref[rows * whose : rows * (whose + 1)] = shares[d][:, width:].astype(f32)
                part = shares[d][:, :width].astype(f32)
                for i in range(width // rows):
                    at = 4 * rows * i + rows * whose
                    in_ref[:, at : at + rows] = part[:, rows * i : rows * (i + 1)]


def place_ffn(shares, gates=()):
    rows, wide = shares[0].shape
    width = wide // 2
    return launch(
        place_ffn_kernel,
        gates,
        mark=True,
        cost=3.0,
        out_shape=(
            jax.ShapeDtypeStruct((rows, 4 * width), f32),
            jax.ShapeDtypeStruct((4 * rows, width), f32),
        ),
        in_specs=[whole()] * 4,
        out_specs=[whole()] * 2,
    )(*shares)


def place_qkv_kernel(*refs):
    ones, twos, qkv_ref, out_ref = refs[:4], refs[4:8], refs[8], refs[9]
    rows, width = out_ref.shape
    low = group_index()
    vectors = twos[0][:, 128:].astype(f32)
    for d in range(1, GROUP):
        vectors = vectors + twos[d][:, 128:].astype(f32)
    vectors = vectors.T
    for i, vector_ref in enumerate(refs[10:]):
        for part in range(vector_ref.shape[0] // rows):
            at = 64 + i + part
            vector_ref[part * rows : (part + 1) * rows] = vectors[at : at + 1].reshape(rows)
    cut = width // 2
    halves = [
        ones[i][:, 3 * LANES :].astype(f32) + ones[i + 2][:, 3 * LANES :].astype(f32)
        for i in range(2)
    ]
    for case in range(GROUP):

        @pl.when(low == case)
        def _():
            for i in range(2):
                at = cut * ((case % 2) ^ i)
                out_ref[:, at : at + cut] = halves[i]
            for d in range(GROUP):
                whose = case ^ d
                one, two = ones[d][...].astype(f32), twos[d][...].astype(f32)

                def put(kind, h, part):
                    at = kind * width + 192 * whose + 64 * h
                    qkv_ref[:, at : at + 64] = part

                for h in range(2):
                    put(0, h, one[:, LANES * h : LANES * h + 64])
                    put(1, h, one[:, LANES * h + 64 : LANES * h + LANES])
                    put(2, h, one[:, 2 * LANES + 64 * h : 2 * LANES + 64 * h + 64])
                for kind in range(3):
                    put(kind, 2, two[:, 64 * kind : 64 * kind + 64])


def place_qkv(ones, twos, width, gates=()):
    rows = ones[0].shape[0]
    return launch(
        place_qkv_kernel,
        gates,
        cost=2.0,
        out_shape=(
            jax.ShapeDtypeStruct((rows, 3 * width), f32),
            jax.ShapeDtypeStruct((rows, width), f32),
            *[jax.ShapeDtypeStruct((rows,), f32)] * 5,
            jax.ShapeDtypeStruct((4 * rows,), f32),
        ),
        in_specs=[whole()] * 8,
        out_specs=[whole()] * 8,
    )(*ones, *twos)


def on_device(
    tokens,
    attn_gain,
    attn_shift,
    w_qkv,
    w_out,
    ffn_gain,
    ffn_shift,
    w_in,
    b_in,
    w_down,
    b_down,
    cotangent,
    lengths,
    block_order,
):
    mine = tokens[0]
    row_count, width = mine.shape
    ctx_size = lax.axis_size("ctx")
    dp_size = lax.axis_size("dp")
    far = ctx_size // GROUP
    rows = w_qkv.shape[0]
    half = row_count // 2
    assert math.gcd(H, ctx_size) == GROUP and w_down.shape[0] == GROUP * rows
    where = (lengths, block_order)

    vectors = [attn_gain, attn_shift, ffn_gain, ffn_shift, b_down, b_in]
    piece = pack(w_qkv, vectors)
    far_qkv = far_pieces(piece, "qkv")
    tok_side = swap(mine, "ctx", 1, "tokens_core")
    tok_over = swap(mine, "ctx", 2, "tokens_x")
    piece_in, piece_down = pack_ffn(w_out, w_in, w_down, gates=(piece, tok_side))
    near_qkv = jnp.stack(far_qkv)
    cross_qkv = swap(near_qkv, "dp", 1, "qkv_y")
    tok_over = after(tok_over, near_qkv)
    blocks = [mine, tok_side, tok_over, swap(tok_over, "ctx", 1, "tokens_pass")]
    cot = cotangent[0]

    query, keys, values, first, small, qkv_weight, weight_two = project(
        *where, blocks, near_qkv, cross_qkv
    )
    far_in = far_pieces(after(piece_in, near_qkv, blocks[3]), "in")
    cot_over = swap(after(cot, near_qkv), "ctx", 2, "cot_x")
    near_in = jnp.stack(far_in[:-1] + [after(far_in[-1], small)])
    if far > 1:
        groups = [[g * GROUP + i for g in range(far)] for i in range(GROUP)]
        keys = lax.all_gather(keys, "ctx", axis=1, tiled=True, axis_index_groups=groups)
        values = lax.all_gather(values, "ctx", axis=1, tiled=True, axis_index_groups=groups)

    far_attn, far_query, far_mark = attend(
        query, keys, values, 2, 2, row_count, gates=(near_in, cot_over)
    )
    cross_in = swap(near_in, "dp", 1, "in_y")
    weight_over = swap(weight_two, "ctx", 2, "weight_x")
    cot_side = swap(after(cot, far_mark), "ctx", 1, "cot_core")
    far_down = far_pieces(after(piece_down, near_in), "down")
    near_down = jnp.stack(far_down[:-1] + [after(far_down[-1], far_mark)])
    near_attn, near_query, near_mark = attend(
        query, keys, values, 0, 2, row_count, gates=(far_mark, near_down, weight_over)
    )
    over_attn = swap(far_attn, "ctx", 2, "attn_x")
    cross_down = swap(near_down, "dp", 1, "down_y")
    held_in = after(cross_in, near_mark)
    out_piece = jnp.concatenate([near_in[:, :, width:], held_in[:, :, width:]])
    out_pieces = [out_piece, swap(out_piece, "ctx", 1, "out_core")]
    core_attn = swap(jnp.stack([near_attn[1], over_attn[1]]), "ctx", 1, "attn_core")
    attn = [near_attn, core_attn, over_attn]

    mixed, second, w_o, mixed_mark = project_out(
        mine, attn, out_pieces, small, gates=(cross_down, cot_side)
    )
    side = swap(second, "ctx", 1, "second_core")
    cot_pass = swap(after(cot_over, mixed_mark), "ctx", 1, "cot_pass")
    cots = [cot, cot_side, cot_over, cot_pass]
    if far == 1:
        probs_one, mixed_mark = attend_weights(
            near_query, far_query, keys, (0, 1), gates=(mixed_mark,)
        )
    (own_part, side_part), weights = feed_forward(
        *where,
        small,
        [second, side],
        cots[:2],
        [near_in, held_in, near_down, cross_down],
        (0, 1),
        gates=(mixed_mark,),
    )
    *outs_near, out_mark = out_parts([own_part[1], side_part[1]], weights[1])
    over = after(swap(second, "ctx", 2, "second_x"), out_mark)
    ds_side = swap(side_part[0], "ctx", 1, "ds_core")
    weight_over = after(weight_over, out_mark)
    weight_pair = swap(jnp.stack([weight_two, weight_over]), "ctx", 1, "weight_core")
    two_weights = [weight_two, weight_pair[0], weight_over, weight_pair[1]]
    (over_part,), _ = feed_forward(
        *where, small, [over], cots[2:3], weights, (2,), gates=(out_mark, cot_pass, weight_pair)
    )
    cross = after(swap(over, "ctx", 1, "second_pass"), over_part[0])
    (cross_part,), _ = feed_forward(*where, small, [cross], cots[3:], weights, (3,))
    parts = [own_part, side_part, over_part, cross_part]
    ds_sum = add(over_part[0], swap(cross_part[0], "ctx", 1, "ds_side"))
    even_ff, odd_ff, bias_grad, far_mark = ffn_grads(
        *where,
        cots,
        [second, side, over, cross],
        [part[1] for part in parts],
        [part[2] for part in parts],
        dp_size,
        gates=(ds_sum, ds_side),
    )
    *outs_far, far_mark = out_parts(
        [over_part[1], cross_part[1]], weights[1], gates=(far_mark,)
    )
    if far == 1:
        probs_two, far_mark = attend_weights(
            near_query, far_query, keys, (2,), gates=(far_mark,)
        )
    ds_over = swap(ds_sum, "ctx", 2, "ds_x")
    outs_own, outs_one = outs_near
    outs_two, outs_three = outs_far
    dmixed, small_grad, dattn, out_halves = mixed_back(
        *where,
        mixed,
        cot,
        small,
        w_o,
        attn,
        [own_part[0], ds_side, ds_over],
        gates=(far_mark,),
    )
    dattn_side = swap(dattn[1], "ctx", 1, "dattn_core")
    odd_sent = swap(odd_ff, "dp", 1, "ffn_y")
    outs_side = swap(after(outs_one, dattn_side), "ctx", 1, "outs_core")
    outs_back = swap(after(outs_three, dattn_side), "ctx", 1, "outs_side")

    out_sent = swap(after(out_halves[1], dattn_side), "ctx", 1, "dw_out_core")

    if far > 1:
        over = swap(dattn[2], "ctx", 2, "dattn_x")
        dattn = [dattn[0], dattn_side, over[0], swap(over[1], "ctx", 1, "dattn_pass")]
        ffn_even = add(even_ff, odd_sent)
        dk, dv, dq, _ = attend_back(
            [near_query, far_query],
            keys,
            values,
            [],
            [near_attn, far_attn],
            dattn,
            (0, 1, 2),
            (0, 1, 2, 3),
            "raw",
            (),
        )
        dk, dv = (
            lax.psum_scatter(v, "ctx", scatter_dimension=1, tiled=True, axis_index_groups=groups)
            for v in (dk, dv)
        )
        dq, dk, dv = (v[..., :64].astype(bf16) for v in (dq, dk, dv))
        one = jnp.concatenate([dq[0], dk[0], dq[1], dk[1], dv[0], dv[1]], axis=1)
        two = jnp.concatenate([dq[2], dk[2], dv[2], jnp.zeros_like(dv[2])], axis=1)
        ones, twos = (v.reshape(2, 2, row_count, v.shape[1]) for v in (one, two))
        ones_mark = ones[0]
        outs_sum = add(outs_two, outs_back)
    else:
        *begun, begun_mark = attend_back(
            [near_query],
            keys,
            values,
            [probs_one],
            [near_attn],
            [dattn[0], dattn_side],
            (0, 1),
            (0, 1),
            "begin",
            (),
        )
        over = after(swap(dattn[2], "ctx", 2, "dattn_x"), begun_mark)
        dattn = [dattn[0], dattn_side, over[0], swap(over[1], "ctx", 1, "dattn_pass")]
        ffn_even = add(even_ff, after(odd_sent, begun_mark, outs_side, outs_back, out_sent))
        outs_sum = add(outs_two, outs_back)
        *ones, ones_mark = attend_back(
            [far_query],
            keys,
            values,
            [probs_one],
            [far_attn],
            dattn[2:],
            (0, 1),
            (2, 3),
            "final",
            begun,
            gates=(ffn_even, outs_sum),
        )
    outs_over = after(swap(outs_sum, "ctx", 2, "outs_x"), ones_mark)
    ffn_share = scatter_far(ffn_even, "ffn", ones_mark)

    even, odd, part_sums, first_mark = first_grad(
        ones,
        first,
        qkv_weight,
        (out_halves[0], out_sent),
        dp_size,
    )
    *parts, _ = input_parts(ones, qkv_weight, gates=(first_mark, ffn_share[0]))
    part_side = swap(parts[1], "ctx", 1, "df_core")
    part_sum = add(parts[2], swap(parts[3], "ctx", 1, "df_side"))
    if far == 1:
        *twos, twos_mark = attend_back(
            [near_query, far_query],
            keys,
            values,
            [probs_two],
            [near_attn, far_attn],
            dattn,
            (2,),
            (0, 1, 2, 3),
            "final",
            (),
            gates=(first_mark, part_sum, outs_over, part_side),
        )
    else:
        twos_mark = twos[0]
    part_over = swap(part_sum, "ctx", 2, "df_x")
    ffn_share = ffn_share[1](twos_mark)
    one_even = add(even, after(swap(odd, "dp", 1, "one_y"), twos_mark))
    ffn_share = sum_groups(ffn_share)
    even, odd, second_mark = second_grad(
        twos,
        first,
        qkv_weight,
        part_sums,
        small_grad,
        bias_grad,
        dp_size,
        gates=(ffn_share,),
    )
    one_share = scatter_far(one_even, "one", second_mark)
    two_even = add(even, swap(odd, "dp", 1, "two_y"))
    part_over = after(part_over, second_mark)
    two_even = after(two_even, one_share[0], part_over)
    ffn_over = swap(ffn_share, "ctx", 2, "ffn_x")
    layer_out, out_mark = finish_out(
        *where, mixed, small, [outs_own, outs_side, outs_over], gates=(two_even,)
    )
    two_share = scatter_far(two_even, "two", out_mark)
    one_share = sum_groups(one_share[1](None))
    two_share = sum_groups(two_share[1](None))
    two_shares = gather_group(two_share, "two")
    ffn_over = after(ffn_over, two_shares[2])
    dtwos = exchange_pairs(*twos, "dtwos", two_shares[2])
    ffn_pair = swap(jnp.stack([ffn_share, ffn_over]), "ctx", 1, "ffn_core")
    ffn_shares = [ffn_share, ffn_pair[0], ffn_over, ffn_pair[1]]
    input_grad, input_mark = finish_input(
        mine,
        dmixed,
        small,
        [parts[0], part_side, part_over],
        dtwos,
        two_weights,
    )
    grad_w_in, grad_w_down, ffn_mark = place_ffn(ffn_shares, gates=(input_mark,))
    one_shares = gather_pairs(one_share, "one", two_share)
    grad_w_qkv, grad_w_out, *vector_grads, grad_b_in = place_qkv(
        one_shares, two_shares, width, gates=(ffn_mark,)
    )
    return (
        layer_out[None],
        input_grad[None],
        vector_grads[0],
        vector_grads[1],
        grad_w_qkv,
        grad_w_out,
        vector_grads[2],
        vector_grads[3],
        grad_w_in,
        grad_b_in,
        grad_w_down,
        vector_grads[4],
    )


def solution(mesh):
    placed = (
        P("dp", "ctx", None),
        P("dp"),
        P("dp"),
        P("dp", None),
        P("dp", None),
        P("dp"),
        P("dp"),
        P("dp", None),
        P("dp"),
        P("dp", None),
        P("dp"),
        P("dp", "ctx", None),
        P("dp"),
        P("dp", None),
    )
    return jax.shard_map(
        on_device,
        mesh=mesh,
        in_specs=placed,
        out_specs=(
            P("dp", "ctx", None),
            P("dp", "ctx", None),
            P("dp"),
            P("dp"),
            P("dp", None),
            P("dp", None),
            P("dp"),
            P("dp"),
            P("dp", None),
            P("dp"),
            P("dp", None),
            P("dp"),
        ),
        check_vma=False,
    )
```

```python
import functools
import math

import jax
import jax.numpy as jnp
from jax import lax
from jax.experimental import pallas as pl
from jax.experimental.pallas import tpu as pltpu
from jax.sharding import PartitionSpec as P

H = 12

epsilon = 1e-05
gelu_coeff = 0.7978845608
cubic_term = 0.044715
excluded = -1073741824.0
bf16 = jnp.bfloat16
f32 = jnp.float32
LANES = 128
GROUP = 4
VMEM_SMALL = 14 * 1024 * 1024
VMEM_LARGE = 52 * 1024 * 1024
VMEM_MOST = 62 * 1024 * 1024

nt_dims = (((1,), (1,)), ((), ()))
tn_dims = (((0,), (0,)), ((), ()))


def mm(left, right):
    return jnp.dot(left, right, preferred_element_type=f32)


def mm_nt(left, right):
    return lax.dot_general(left, right, nt_dims, preferred_element_type=f32)


def mm_tn(left, right):
    return lax.dot_general(left, right, tn_dims, preferred_element_type=f32)


def whole(memory_space=pltpu.VMEM):
    return pl.BlockSpec(memory_space=memory_space)


def lanes_of(shape):
    return lax.broadcasted_iota(jnp.int32, shape, 1)


def norm_parts(values):
    center = values - jnp.mean(values, axis=-1, keepdims=True)
    spread = jnp.mean(center * center, axis=-1, keepdims=True)
    inverse = lax.rsqrt(spread + epsilon)
    return center * inverse, inverse


def norm_back(scaled, unit, inverse):
    return inverse * (
        scaled
        - jnp.mean(scaled, axis=-1, keepdims=True)
        - unit * jnp.mean(scaled * unit, axis=-1, keepdims=True)
    )


def three_parts(value):
    first = value.astype(bf16).astype(f32)
    rest = value - first
    second = rest.astype(bf16).astype(f32)
    return first, second, rest - second


def with_parts(base, value):
    lane = lanes_of(base.shape)
    one, two, three = three_parts(value)
    return jnp.where(
        lane == 64, one, jnp.where(lane == 65, two, jnp.where(lane == 66, three, base))
    )


def unpack_rows(packed, rows):
    tail = jnp.concatenate([packed[rows:, :64], packed[rows:, 64:]], axis=0)
    return packed[:rows], tail


def swap(value, axis, bit, name):
    size = lax.axis_size(axis)
    with jax.named_scope(name):
        return lax.ppermute(value, axis, [(i, i ^ bit) for i in range(size)])


def launch(kernel, gates, in_specs, cost=1.0, vmem=VMEM_SMALL, mark=False, **options):
    count = len(gates)
    place = None
    if mark:
        shapes, specs = options["out_shape"], options["out_specs"]
        if not isinstance(shapes, (list, tuple)):
            shapes, specs = [shapes], [specs]
        place = count + len(in_specs) + len(shapes)
        options["out_shape"] = [*shapes, jax.ShapeDtypeStruct((8, LANES), f32)]
        options["out_specs"] = [*specs, whole()]

    def gated(*refs):
        refs = list(refs)
        if mark:
            refs.pop(place)[...] = jnp.zeros((8, LANES), f32)
        kernel(*refs[count:])

    call = pl.pallas_call(
        gated,
        in_specs=[whole(pl.ANY)] * count + in_specs,
        compiler_params=pltpu.CompilerParams(vmem_limit_bytes=vmem),
        cost_estimate=pl.CostEstimate(
            flops=int(cost * 2e7), bytes_accessed=1024, transcendentals=0
        ),
        **options,
    )
    return lambda *operands: call(*gates, *operands)


def hold_kernel(value_ref, out_ref):
    pass


def after(value, *gates):
    return launch(
        hold_kernel,
        gates,
        [whole(pl.ANY)],
        out_shape=jax.ShapeDtypeStruct(value.shape, value.dtype),
        out_specs=whole(pl.ANY),
        input_output_aliases={len(gates): 0},
    )(value)


def far_pieces(piece, name):
    found = [piece]
    for k in range(1, lax.axis_size("dp") // 2):
        found.append(swap(piece, "dp", 2 * k, name + "_z"))
    return found


def add(left, right):
    return (left.astype(f32) + right.astype(f32)).astype(bf16)


def scatter_far(even, name, gate):
    def step(even, gate):
        half = even.shape[0] // 2
        bit = lax.axis_size("dp") // (2 * half)
        pairs = even.reshape(half, 2, *even.shape[1:])
        received = swap(pairs[:, 1], "dp", bit, name + "_z")
        return add(pairs[:, 0], received if gate is None else after(received, gate))

    begun = step(even, gate)

    def finish(gate):
        total = begun
        while total.shape[0] > 1:
            total = step(total, gate)
        return total[0]

    return begun, finish


def sum_groups(value):
    bit = GROUP
    while bit < lax.axis_size("ctx"):
        other = swap(value, "ctx", bit, "groups")
        value = (value.astype(f32) + other.astype(f32)).astype(bf16)
        bit *= 2
    return value


def gather_group(value, name, gate=None):
    over = swap(value, "ctx", 2, name + "_x")
    if gate is not None:
        over = after(over, gate)
    side = swap(value, "ctx", 1, name + "_core")
    return [value, side, over, swap(over, "ctx", 1, name + "_pass")]


def exchange_pairs(near, far, name, gate=None):
    over = swap(far, "ctx", 2, name + "_x")
    if gate is not None:
        over = after(over, gate)
    core = swap(jnp.stack([near[1], over[1]]), "ctx", 1, name + "_core")
    return [near, core, over]


def gather_pairs(value, name, gate=None):
    over = swap(value, "ctx", 2, name + "_x")
    if gate is not None:
        over = after(over, gate)
    pair = swap(jnp.stack([value, over]), "ctx", 1, name + "_core")
    return [value, pair[0], over, pair[1]]


def position_of(order_ref, slot, rows):
    index = lax.axis_index("ctx")
    return order_ref[0, lax.bitwise_xor(index, slot)] * rows


def valid_rows(length_ref, order_ref, slot, rows):
    stored = lax.broadcasted_iota(jnp.int32, (rows, LANES), 0)[:, :1]
    position = position_of(order_ref, slot, rows) + stored
    return jnp.where(position < length_ref[0], 1.0, 0.0)


def group_index():
    return lax.rem(lax.axis_index("ctx"), GROUP)


def load_pieces(sources, target, sems, first_sem=0):
    me = lax.axis_index("dp")
    copies = []
    for source, differences in sources:
        rows = source.shape[1]
        for k, difference in enumerate(differences):
            owner = lax.bitwise_xor(me, difference)
            copies.append(
                pltpu.make_async_copy(
                    source.at[k],
                    target.at[pl.ds(pl.multiple_of(owner * rows, 16), rows)],
                    sems.at[first_sem + len(copies)],
                )
            )
    for copy in copies:
        copy.start()
    return copies


def near_and_cross(near, cross):
    halves = near.shape[0]
    return [(near, [2 * k for k in range(halves)]), (cross, [2 * k + 1 for k in range(halves)])]


def store_pieces(source, even, odd, sems):
    halves, rows, _ = even.shape
    me = lax.axis_index("dp")
    copies = []
    for parity, target in ((0, even), (1, odd)):
        for k in range(halves):
            owner = lax.bitwise_xor(me, 2 * k + parity)
            copies.append(
                pltpu.make_async_copy(
                    source.at[pl.ds(pl.multiple_of(owner * rows, 16), rows)],
                    target.at[k],
                    sems.at[2 * k + parity],
                )
            )
    for copy in copies:
        copy.start()
    for copy in copies:
        copy.wait()


def pack_kernel(w_hbm, *refs):
    w_ref, sems = refs[-2:]
    count = (len(refs) - 3) // 2
    vectors, out_ref, held = refs[:count], refs[count], refs[count + 1 : -2]
    copies = [pltpu.make_async_copy(w_hbm, w_ref, sems.at[count])]
    for i in range(count):
        copies.append(pltpu.make_async_copy(vectors[i], held[i], sems.at[i]))
    for copy in copies:
        copy.start()
    for copy in copies:
        copy.wait()
    rows = w_ref.shape[0]
    width = w_ref.shape[1] // 3
    low = group_index()
    stacked = []
    for v in held:
        flat = v[...].astype(f32).reshape(1, v.shape[0])
        stacked += [flat[:, i : i + rows] for i in range(0, v.shape[0], rows)]
    stacked.append(jnp.zeros((LANES - len(stacked), rows), f32))
    small = jnp.concatenate(stacked, axis=0).T[:, :64].astype(bf16)
    for case in range(GROUP):

        @pl.when(low == case)
        def _():
            def head(kind, h):
                at = kind * width + 192 * case + 64 * h
                return w_ref[:, at : at + 64]

            out_ref[...] = jnp.concatenate(
                [
                    head(0, 0),
                    head(1, 0),
                    head(0, 1),
                    head(1, 1),
                    head(2, 0),
                    head(2, 1),
                    head(0, 2),
                    head(1, 2),
                    head(2, 2),
                    small,
                ],
                axis=1,
            )


def pack(w_qkv, vectors, gates=()):
    rows = w_qkv.shape[0]
    return launch(
        pack_kernel,
        gates,
        vmem=VMEM_MOST,
        cost=1.0,
        out_shape=jax.ShapeDtypeStruct((rows, 640), bf16),
        in_specs=[whole(pltpu.HBM)] * (1 + len(vectors)),
        out_specs=whole(),
        scratch_shapes=[pltpu.VMEM(v.shape, bf16) for v in vectors]
        + [pltpu.VMEM(w_qkv.shape, bf16), pltpu.SemaphoreType.DMA((1 + len(vectors),))],
    )(w_qkv, *vectors)


def pack_ffn_kernel(out_ref, in_ref, down_ref, one_ref, two_ref):
    rows, ff = in_ref.shape
    width = out_ref.shape[1]
    half = width // 2
    low = group_index()
    per = 4 * rows
    for case in range(GROUP):

        @pl.when(low == case)
        def _():
            at = half * (case % 2)
            parts = [
                in_ref[:, per * i + rows * case : per * i + rows * (case + 1)]
                for i in range(ff // per)
            ]
            one_ref[:, :width] = jnp.concatenate(parts, axis=1)
            one_ref[:, width:] = out_ref[:, at : at + half]
            two_ref[...] = down_ref[rows * case : rows * (case + 1)]


def pack_ffn(w_out, w_in, w_down, gates=()):
    rows, width = w_out.shape
    return launch(
        pack_ffn_kernel,
        gates,
        cost=1.0,
        out_shape=(
            jax.ShapeDtypeStruct((rows, width + width // 2), bf16),
            jax.ShapeDtypeStruct((rows, width), bf16),
        ),
        in_specs=[whole()] * 3,
        out_specs=[whole()] * 2,
    )(w_out, w_in, w_down)


def qkv_kernel(length_ref, order_ref, *refs):
    tokens = refs[:GROUP]
    near, cross = refs[GROUP : GROUP + 2]
    q_ref, k_ref, v_ref, first_ref, small_ref, w_ref, w_two_ref, sems = refs[GROUP + 2 :]
    row_count, width = tokens[0].shape
    for copy in load_pieces(near_and_cross(near, cross), w_ref, sems):
        copy.wait()
    w_two_ref[...] = w_ref[:, 384:640]
    small = w_ref[:, 512:640].astype(f32).T
    small_ref[...] = small[64:80]
    gain, shift = small[64:65], small[65:66]
    length = length_ref[0]
    lane = lanes_of((row_count, LANES))
    ones = jnp.where((lane >= 64) & (lane < 67), 1.0, 0.0)
    bias_lane = jnp.where(lane == 67, 1.0, 0.0)
    for d in range(GROUP):
        unit, _ = norm_parts(tokens[d][...].astype(f32))
        first = (unit * gain + shift).astype(bf16)
        part = pl.ds(d * row_count, row_count)
        first_ref[part] = first
        qkv = mm(first, w_ref[...]).astype(bf16).astype(f32)

        def head(place):
            block = qkv[:, place // 2 * LANES : (place // 2 + 1) * LANES]
            if place % 2:
                block = pltpu.roll(block, 64, 1)
            return jnp.where(lane < 64, block, 0.0)

        stored = lax.broadcasted_iota(jnp.int32, (row_count, LANES), 0)
        position = position_of(order_ref, d, row_count) + stored
        bias = jnp.where(position < length, 0.0, excluded) * bias_lane
        for h, (at_q, at_k, at_v) in enumerate(((0, 1, 4), (2, 3, 5), (6, 7, 8))):
            q_ref[h, part] = (head(at_q) * 0.125 + bias_lane).astype(bf16)
            k_ref[h, part] = (head(at_k) + ones + bias).astype(bf16)
            v_ref[h, part] = (head(at_v) + ones).astype(bf16)


def project(length, order, tokens, near, cross, gates=()):
    row_count, width = tokens[0].shape
    total = GROUP * row_count
    wide = near.shape[2]
    head_out = jax.ShapeDtypeStruct((3, total, LANES), bf16)
    return launch(
        qkv_kernel,
        gates,
        cost=10.0,
        out_shape=(
            head_out,
            head_out,
            head_out,
            jax.ShapeDtypeStruct((total, width), bf16),
            jax.ShapeDtypeStruct((16, width), f32),
            jax.ShapeDtypeStruct((width, wide), bf16),
            jax.ShapeDtypeStruct((width, 256), bf16),
        ),
        in_specs=[whole(pltpu.SMEM)] * 2 + [whole()] * GROUP + [whole(pl.ANY)] * 2,
        out_specs=[whole()] * 7,
        scratch_shapes=[pltpu.SemaphoreType.DMA((2 * near.shape[0],))],
    )(length, order, *tokens, near, cross)


def attend_kernel(block_rows, q_ref, k_ref, v_ref, packed_ref, q_out_ref):
    row_count = q_ref.shape[1]
    half = row_count // 2
    lane = lanes_of((block_rows, LANES))
    for i in range(row_count // block_rows):
        part = pl.ds(i * block_rows, block_rows)
        heads = []
        for h in range(3):
            query = q_ref[h, part]
            scores = mm_nt(query, k_ref[h])
            top = jnp.max(scores, axis=1, keepdims=True)
            weights = jnp.exp(scores - top).astype(bf16)
            result = mm(weights, v_ref[h])
            denom = result[:, 64:65]
            heads.append(jnp.where(lane < 64, result / denom, 0.0))
            log_total = top + jnp.log(denom)
            q_out_ref[h, part] = with_parts(query.astype(f32), -log_total).astype(bf16)
        packed_ref[0, part] = (heads[0] + pltpu.roll(heads[1], 64, 1)).astype(bf16)
        for r in range(0, block_rows, half):
            size = min(half, block_rows)
            row = i * block_rows + r
            side, place = row // half, row % half
            packed_ref[
                0, pl.ds(row_count + place, size), 64 * side : 64 * side + 64
            ] = heads[2][r : r + size, :64].astype(bf16)


def attend(query, keys, values, first_slot, slots, row_count, gates=()):
    total = keys.shape[1]
    block_rows = min(row_count // 2, 256)
    return launch(
        functools.partial(attend_kernel, block_rows),
        gates,
        mark=True,
        cost=5.0 * slots,
        vmem=VMEM_LARGE if total > GROUP * row_count else VMEM_SMALL,
        grid=(slots,),
        out_shape=(
            jax.ShapeDtypeStruct((slots, row_count * 3 // 2, LANES), bf16),
            jax.ShapeDtypeStruct((3, slots * row_count, LANES), bf16),
        ),
        in_specs=[
            pl.BlockSpec((3, row_count, LANES), lambda s: (0, s + first_slot, 0)),
            whole(),
            whole(),
        ],
        out_specs=(
            pl.BlockSpec((1, row_count * 3 // 2, LANES), lambda s: (s, 0, 0)),
            pl.BlockSpec((3, row_count, LANES), lambda s: (0, s, 0)),
        ),
    )(query, keys, values)


def weights_kernel(near_ref, far_ref, k_ref, out_ref):
    query = jnp.where(pl.program_id(1) < 2, near_ref[0], far_ref[0])
    rows = query.shape[0]
    for c in range(k_ref.shape[1] // rows):
        at = pl.ds(c * rows, rows)
        out_ref[0, 0, at] = jnp.exp(mm_nt(k_ref[0, at], query)).astype(bf16)


def attend_weights(near_query, far_query, keys, heads, gates=()):
    row_count = near_query.shape[1] // 2
    total = keys.shape[1]
    first = heads[0]
    return launch(
        weights_kernel,
        gates,
        mark=True,
        cost=3.0 * len(heads),
        grid=(len(heads), GROUP),
        out_shape=jax.ShapeDtypeStruct((len(heads), GROUP, total, row_count), bf16),
        in_specs=[
            pl.BlockSpec((1, row_count, LANES), lambda h, s: (h + first, jnp.minimum(s, 1), 0)),
            pl.BlockSpec((1, row_count, LANES), lambda h, s: (h + first, jnp.maximum(s - 2, 0), 0)),
            pl.BlockSpec((1, total, LANES), lambda h, s: (h + first, 0, 0)),
        ],
        out_specs=pl.BlockSpec((1, 1, total, row_count), lambda h, s: (h, s, 0, 0)),
    )(near_query, far_query, keys)


def group_attn(refs, row_count):
    near, core, over = refs
    packed = (near[0], core[0], over[0], core[1])
    return [jnp.concatenate(unpack_rows(v, row_count), axis=1) for v in packed]


def out_kernel(token_ref, *refs):
    attn_refs, pieces = refs[:3], refs[3:5]
    small_ref, mixed_ref, second_ref, w_o, sems = refs[5:]
    row_count, width = token_ref.shape
    half = width // 2
    number = pieces[0].shape[0]
    low = group_index()
    core = lax.rem(low, 2)
    differences = [2 * k for k in range(number // 2)] + [2 * k + 1 for k in range(number // 2)]
    copies = []
    for side in range(2):
        column = pl.multiple_of((core if side == 0 else 1 - core) * half, LANES)
        target = w_o.at[:, pl.ds(column, half)]
        copies += load_pieces([(pieces[side], differences)], target, sems, side * number)
    mixed = token_ref[...].astype(f32)
    attn = group_attn(attn_refs, row_count)
    for copy in copies:
        copy.wait()
    for d in range(GROUP):
        at = pl.ds(pl.multiple_of(lax.bitwise_xor(low, d) * 192, 16), 192)
        mixed = mixed + mm(attn[d], w_o[at, :])
    mixed_ref[...] = mixed
    unit, _ = norm_parts(mixed)
    second_ref[...] = (unit * small_ref[2:3] + small_ref[3:4]).astype(bf16)


def project_out(tokens, attn, pieces, small, gates=()):
    row_count, width = tokens.shape
    number = pieces[0].shape[0]
    return launch(
        out_kernel,
        gates,
        mark=True,
        cost=4.5,
        out_shape=(
            jax.ShapeDtypeStruct((row_count, width), f32),
            jax.ShapeDtypeStruct((row_count, width), bf16),
            jax.ShapeDtypeStruct((width, width), bf16),
        ),
        in_specs=[whole()] * 4 + [whole(pl.ANY)] * 2 + [whole()],
        out_specs=[whole()] * 3,
        scratch_shapes=[pltpu.SemaphoreType.DMA((2 * number,))],
    )(tokens, *attn, *pieces, small)


def ffn_kernel(slots, gathers, length_ref, order_ref, small_ref, *refs):
    number = len(slots)
    seconds, cots = refs[:number], refs[number : 2 * number]
    refs = refs[2 * number :]
    count = 4 if gathers else 2
    sources, refs = refs[:count], refs[count:]
    outs = [refs[3 * i : 3 + 3 * i] for i in range(number)]
    refs = refs[3 * number :]
    rows, width = seconds[0].shape
    if gathers:
        w_i, w_d, sems = refs
        near, cross, near_down, cross_down = sources
        parts = near_and_cross(*(v.at[:, :, pl.ds(0, width)] for v in (near, cross)))
        in_copies = load_pieces(parts, w_i, sems)
        down_copies = load_pieces(near_and_cross(near_down, cross_down), w_d, sems, 2 * gathers)
        for copy in in_copies:
            copy.wait()
    else:
        w_i, w_d = sources
    bias = small_ref[pl.ds(5 + group_index(), 1)]
    for i, slot in enumerate(slots):
        ds_ref, active_ref, dhid_ref = outs[i]
        row_count = cots[i].shape[0]
        valid = valid_rows(length_ref, order_ref, slot, row_count)
        dlow = (cots[i][...].astype(f32) * valid).astype(bf16)
        hidden = mm(seconds[i][...], w_i[...]) + bias
        squared = hidden * hidden
        bent = jnp.tanh(hidden * (gelu_coeff + gelu_coeff * cubic_term * squared))
        plus = 0.5 + 0.5 * bent
        slope = plus + hidden * (plus * (1.0 - bent)) * (
            gelu_coeff + gelu_coeff * 3.0 * cubic_term * squared
        )
        active_ref[...] = (hidden * plus).astype(bf16)
        if gathers and i == 0:
            for copy in down_copies:
                copy.wait()
        dhid = (mm_nt(dlow, w_d[...]) * slope).astype(bf16)
        dhid_ref[...] = dhid
        ds_ref[...] = mm_nt(dhid, w_i[...]).astype(bf16)


def feed_forward(length, order, small, seconds, cots, weights, slots, gates=()):
    rows, width = seconds[0].shape
    gathers = weights[0].shape[0] if len(weights) == 4 else 0
    number = len(slots)
    block = jax.ShapeDtypeStruct((rows, width), bf16)
    square = jax.ShapeDtypeStruct((width, width), bf16)
    results = launch(
        functools.partial(ffn_kernel, slots, gathers),
        gates,
        cost=3.0 * number,
        out_shape=[block] * (3 * number) + [square] * (2 if gathers else 0),
        in_specs=[whole(pltpu.SMEM)] * 2
        + [whole()] * (1 + 2 * number)
        + [whole(pl.ANY) if gathers else whole()] * len(weights),
        out_specs=[whole()] * (3 * number + (2 if gathers else 0)),
        scratch_shapes=[pltpu.SemaphoreType.DMA((4 * gathers,))] if gathers else [],
    )(length, order, small, *seconds, *cots, *weights)
    grouped = [results[3 * i : 3 * i + 3] for i in range(number)]
    return grouped, results[3 * number :]


def out_part_kernel(*refs):
    w_d = refs[2][...]
    for i in range(2):
        refs[3 + i][...] = mm(refs[i][...], w_d).astype(bf16)


def out_parts(actives, w_down, gates=()):
    return launch(
        out_part_kernel,
        gates,
        mark=True,
        cost=2.0,
        out_shape=[jax.ShapeDtypeStruct(v.shape, bf16) for v in actives],
        in_specs=[whole()] * 3,
        out_specs=[whole()] * 2,
    )(*actives, w_down)


def ffn_grad_kernel(length_ref, order_ref, *refs):
    cots, seconds, actives, dhids = (refs[i : i + GROUP] for i in range(0, 4 * GROUP, GROUP))
    even, odd, bias_ref, g_ref, sems = refs[4 * GROUP :]
    row_count, width = cots[0].shape
    bias = jnp.zeros((1, width), f32)
    grad_in = jnp.zeros((width, width), f32)
    for d in range(GROUP):
        dhid = dhids[d][...]
        bias = bias + jnp.sum(dhid.astype(f32), axis=0, keepdims=True)
        grad_in = grad_in + mm_tn(seconds[d][...], dhid)
    g_ref[:, :width] = grad_in.astype(bf16)
    bias_ref[...] = bias
    grad_down = jnp.zeros((width, width), f32)
    for d in range(GROUP):
        valid = valid_rows(length_ref, order_ref, d, row_count)
        dlow = (cots[d][...].astype(f32) * valid).astype(bf16)
        grad_down = grad_down + mm_tn(actives[d][...], dlow)
    g_ref[:, width:] = grad_down.astype(bf16)
    store_pieces(g_ref, even, odd, sems)


def ffn_grads(length, order, cots, seconds, actives, dhids, dp_size, gates=()):
    width = cots[0].shape[1]
    halves = dp_size // 2
    piece = jax.ShapeDtypeStruct((halves, width // dp_size, 2 * width), bf16)
    return launch(
        ffn_grad_kernel,
        gates,
        mark=True,
        cost=7.0,
        out_shape=(piece, piece, jax.ShapeDtypeStruct((1, width), f32)),
        in_specs=[whole(pltpu.SMEM)] * 2 + [whole()] * (4 * GROUP),
        out_specs=[whole(pl.ANY)] * 2 + [whole()],
        scratch_shapes=[
            pltpu.VMEM((width, 2 * width), bf16),
            pltpu.SemaphoreType.DMA((dp_size,)),
        ],
    )(length, order, *cots, *seconds, *actives, *dhids)


def mixed_back_kernel(length_ref, order_ref, *refs):
    mixed_ref, cot_ref, small_ref, w_o = refs[:4]
    attn_refs = refs[4:7]
    ds_refs = refs[7:10]
    dmixed_ref, small_grad_ref = refs[10:12]
    own, side, over = refs[12:15]
    dattn_refs = (own, side, over.at[0], over.at[1])
    half_refs = refs[15:17]
    g_o = refs[17]
    row_count, width = mixed_ref.shape
    half = row_count // 2
    low = group_index()
    unit, inverse = norm_parts(mixed_ref[...])
    ds = sum(v[...].astype(f32) for v in ds_refs)
    valid = valid_rows(length_ref, order_ref, 0, row_count)
    dout = cot_ref[...].astype(f32) * valid
    dmixed = dout + norm_back(ds * small_ref[2:3], unit, inverse)
    dmixed_ref[...] = dmixed
    dbranch = dmixed.astype(bf16)

    def out_rows(d):
        return pl.ds(pl.multiple_of(lax.bitwise_xor(low, d) * 192, 16), 192)

    for d in range(GROUP):
        dattn = mm_nt(dbranch, w_o[out_rows(d), :])
        dattn_refs[d][pl.ds(0, row_count)] = dattn[:, :LANES].astype(bf16)
        dattn_refs[d][pl.ds(row_count, half), :64] = dattn[:half, LANES:].astype(bf16)
        dattn_refs[d][pl.ds(row_count, half), 64:] = dattn[half:, LANES:].astype(bf16)
    attn = group_attn(attn_refs, row_count)
    for d in range(GROUP):
        g_o[out_rows(d), :] = mm_tn(attn[d], dbranch).astype(bf16)
    core = lax.rem(low, 2)
    for here, half_ref in zip((core, 1 - core), half_refs):
        column = pl.multiple_of(here * (width // 2), LANES)
        half_ref[...] = g_o[:, pl.ds(column, width // 2)]
    small_grad_ref[...] = jnp.zeros_like(small_grad_ref)
    small_grad_ref[2:3] = jnp.sum(ds * unit, axis=0, keepdims=True)
    small_grad_ref[3:4] = jnp.sum(ds, axis=0, keepdims=True)
    small_grad_ref[4:5] = jnp.sum(dout, axis=0, keepdims=True)


def mixed_back(length, order, mixed, cot, small, w_o, attn, ds, gates=()):
    row_count, width = mixed.shape
    results = launch(
        mixed_back_kernel,
        gates,
        cost=7.0,
        out_shape=[
            jax.ShapeDtypeStruct((row_count, width), f32),
            jax.ShapeDtypeStruct((16, width), f32),
        ]
        + [jax.ShapeDtypeStruct((row_count * 3 // 2, LANES), bf16)] * 2
        + [jax.ShapeDtypeStruct((2, row_count * 3 // 2, LANES), bf16)]
        + [jax.ShapeDtypeStruct((width, width // 2), bf16)] * 2,
        in_specs=[whole(pltpu.SMEM)] * 2 + [whole()] * 10,
        out_specs=[whole()] * 7,
        scratch_shapes=[pltpu.VMEM((width, width), bf16)],
    )(length, order, mixed, cot, small, w_o, *attn, *ds)
    return results[0], results[1], results[2:5], results[5:7]


def layer_out_kernel(length_ref, order_ref, mixed_ref, small_ref, *refs):
    own, side, over, out_ref = refs
    row_count = mixed_ref.shape[0]
    valid = valid_rows(length_ref, order_ref, 0, row_count)
    total = mixed_ref[...] + own[...].astype(f32) + side[...].astype(f32) + over[...].astype(f32)
    out_ref[...] = ((total + small_ref[4:5]) * valid).astype(bf16)


def finish_out(length, order, mixed, small, parts, gates=()):
    return launch(
        layer_out_kernel,
        gates,
        mark=True,
        cost=3.0,
        out_shape=jax.ShapeDtypeStruct(mixed.shape, bf16),
        in_specs=[whole(pltpu.SMEM)] * 2 + [whole()] * 5,
        out_specs=whole(),
    )(length, order, mixed, small, *parts)


def attend_back_kernel(mode, heads, slots, row_count, starts, *refs):
    number = len(slots)
    pairs = number // 2
    q_refs, (k_ref, v_ref) = refs[:pairs], refs[pairs : pairs + 2]
    refs = refs[pairs + 2 :]
    if mode != "raw":
        prob_ref, refs = refs[0], refs[1:]
    attn_refs, dattn_refs = refs[:pairs], refs[pairs : pairs + number]
    refs = refs[pairs + number :]
    if starts:
        dk_in, dv_in, dq_in = refs[:3]
        refs = refs[3:]
    outs = refs[:-5]
    grad_ref, k_turned, dq_ref, dk_ref, dv_ref = refs[-5:]
    head, step = pl.program_id(0), pl.program_id(1)
    total = k_ref.shape[1]
    chunk = row_count
    first_slot = slots[0] if mode == "final" else 0

    @pl.when((head == 0) & (step == 0))
    def _():
        lane = lanes_of((row_count, LANES))
        for d in range(number):
            top, tail = unpack_rows(dattn_refs[d][...].astype(f32), row_count)
            top_a, tail_a = unpack_rows(attn_refs[d // 2][d % 2].astype(f32), row_count)
            product = top * top_a
            for i, h in enumerate(heads):
                if h == 0:
                    block = top
                    delta = jnp.sum(jnp.where(lane < 64, product, 0.0), axis=1, keepdims=True)
                elif h == 1:
                    block = pltpu.roll(top, 64, 1)
                    delta = jnp.sum(jnp.where(lane >= 64, product, 0.0), axis=1, keepdims=True)
                else:
                    block = jnp.concatenate([tail, tail], axis=1)
                    delta = jnp.sum(tail * tail_a, axis=1, keepdims=True)
                base = jnp.where(lane < 64, block, 0.0)
                grad_ref[i, pl.ds(d * row_count, row_count)] = with_parts(base, -delta).astype(bf16)

    @pl.when(step == 0)
    def _():
        k_turned[...] = k_ref[0].astype(f32).T.astype(bf16)
        if starts:
            dk_ref[...] = dk_in[0]
            dv_ref[...] = dv_in[0]
            dq_ref[: first_slot * row_count] = dq_in[0]
        else:
            dk_ref[...] = jnp.zeros_like(dk_ref)
            dv_ref[...] = jnp.zeros_like(dv_ref)

    query = q_refs[0][0]
    if pairs > 1:
        query = jnp.where(step < 2, query, q_refs[1][0])
    grad = grad_ref[head, pl.ds(pl.multiple_of(step * row_count, row_count), row_count)]
    turned = jnp.zeros((LANES, row_count), f32)
    for c in range(total // chunk):
        at = pl.ds(c * chunk, chunk)
        if mode == "raw":
            probs = jnp.exp(mm_nt(k_ref[0, at], query)).astype(bf16)
        else:
            probs = prob_ref[0, 0, at]
        dscores = (probs.astype(f32) * mm_nt(v_ref[0, at], grad)).astype(bf16)
        dv_ref[at] += mm(probs, grad)
        dk_ref[at] += mm(dscores, query)
        turned = turned + mm(k_turned[:, at], dscores)
    place = pl.multiple_of((first_slot + step) * row_count, row_count)
    dq_ref[pl.ds(place, row_count)] = turned.T * 0.125

    @pl.when(step == number - 1)
    def _():
        if mode != "final":
            outs[0][0] = dk_ref[...]
            outs[1][0] = dv_ref[...]
            outs[2][0] = dq_ref[...]
            return
        lane = lanes_of((row_count, LANES))
        last_at = LANES * len(heads)
        for i in range(len(heads)):

            @pl.when(head == i)
            def _():
                for d in range(GROUP):
                    at = pl.ds(d * row_count, row_count)
                    pair = jnp.where(lane < 64, dq_ref[at], pltpu.roll(dk_ref[at], 64, 1))
                    out = outs[d // 2].at[d % 2]
                    out[:, i * LANES : (i + 1) * LANES] = pair.astype(bf16)
                    value = dv_ref[at]
                    if i == 0:
                        value = jnp.where(lane < 64, value, 0.0)
                        out[:, last_at : last_at + LANES] = value.astype(bf16)
                    else:
                        out[:, last_at + 64 : last_at + LANES] = value[:, :64].astype(bf16)


def attend_back(queries, keys, values, probs, attn, dattn, heads, slots, mode, begun, gates=()):
    row_count = dattn[0].shape[0] * 2 // 3
    total = keys.shape[1]
    number = len(slots)
    kept = GROUP if mode == "final" else number
    first_head = heads[0]
    if number == 2:
        places = [lambda h, s: (h + first_head, s, 0)]
    else:
        places = [
            lambda h, s: (h + first_head, jnp.minimum(s, 1), 0),
            lambda h, s: (h + first_head, jnp.maximum(s - 2, 0), 0),
        ]

    def per_head(size):
        return (
            jax.ShapeDtypeStruct((len(heads), size, LANES), f32),
            pl.BlockSpec((1, size, LANES), lambda h, s: (h, 0, 0)),
        )

    if mode == "final":
        wide = LANES * (len(heads) + 1)
        outs = [
            (
                jax.ShapeDtypeStruct((2, row_count, wide), bf16),
                pl.BlockSpec((2, row_count, wide), lambda h, s: (0, 0, 0)),
            )
        ] * 2
    else:
        outs = [per_head(total), per_head(total), per_head(number * row_count)]
    begun_specs = []
    if begun:
        begun_specs = [
            pl.BlockSpec((1, v.shape[1], LANES), lambda h, s: (h, 0, 0)) for v in begun
        ]
    return launch(
        functools.partial(attend_back_kernel, mode, heads, slots, row_count, bool(begun)),
        gates,
        mark=True,
        cost=3.2 * number * len(heads),
        vmem=VMEM_LARGE if total > GROUP * row_count else VMEM_SMALL,
        grid=(len(heads), number),
        out_shape=[shape for shape, _ in outs],
        out_specs=[spec for _, spec in outs],
        in_specs=[
            pl.BlockSpec((1, row_count, LANES), place) for place in places
        ]
        + [pl.BlockSpec((1, total, LANES), lambda h, s: (h + first_head, 0, 0))] * 2
        + [
            pl.BlockSpec((1, 1, total, row_count), lambda h, s: (h, s + slots[0], 0, 0))
            for _ in probs
        ]
        + [whole()] * (len(attn) + number)
        + begun_specs,
        scratch_shapes=[
            pltpu.VMEM((len(heads), number * row_count, LANES), bf16),
            pltpu.VMEM((LANES, total), bf16),
            pltpu.VMEM((kept * row_count, LANES), f32),
            pltpu.VMEM((total, LANES), f32),
            pltpu.VMEM((total, LANES), f32),
        ],
    )(*queries, keys, values, *probs, *attn, *dattn, *begun)


def first_grad_kernel(*refs):
    parts, first_ref, w_ref, block_refs = refs[:2], refs[2], refs[3], refs[4:6]
    even, odd, side_ref, d_ref, g_ref, sems = refs[6:]
    _, row_count, wide = parts[0].shape
    for d in range(GROUP):
        d_ref[d * row_count : (d + 1) * row_count] = parts[d // 2][d % 2]
    weights = w_ref[...].astype(f32)
    grad = mm_tn(first_ref[...], d_ref[...])
    g_ref[:, :wide] = grad.astype(bf16)
    columns = jnp.sum(d_ref[...].astype(f32), axis=0, keepdims=True)
    shift = weights[:, 577:578]
    used = weights[:, :wide]
    gain_part = jnp.sum(used * (grad - shift * columns), axis=1, keepdims=True)
    shift_part = jnp.sum(used * columns, axis=1, keepdims=True)
    lane = lanes_of(side_ref.shape)
    side_ref[...] = jnp.where(lane == 64, gain_part, jnp.where(lane == 65, shift_part, 0.0))
    block = block_refs[0][...].astype(f32) + block_refs[1][...].astype(f32)
    g_ref[:, wide:] = block.astype(bf16)
    store_pieces(g_ref, even, odd, sems)


def first_grad(parts, first, weights, blocks, dp_size, gates=()):
    total, width = first.shape
    wide = parts[0].shape[2]
    piece = jax.ShapeDtypeStruct((dp_size // 2, width // dp_size, wide + width // 2), bf16)
    return launch(
        first_grad_kernel,
        gates,
        mark=True,
        cost=5.0,
        out_shape=(piece, piece, jax.ShapeDtypeStruct((width, LANES), f32)),
        in_specs=[whole()] * 6,
        out_specs=[whole(pl.ANY)] * 2 + [whole()],
        scratch_shapes=[
            pltpu.VMEM((total, wide), bf16),
            pltpu.VMEM((width, wide + width // 2), bf16),
            pltpu.SemaphoreType.DMA((dp_size,)),
        ],
    )(*parts, first, weights, *blocks)


def second_grad_kernel(*refs):
    parts = refs[:2]
    first_ref, w_ref, side_ref, small_grad_ref, bias_grad_ref = refs[2:7]
    even, odd, d_ref, g_ref, turn_ref, sems = refs[7:]
    _, row_count, wide = parts[0].shape
    width = first_ref.shape[1]
    for d in range(GROUP):
        d_ref[d * row_count : (d + 1) * row_count] = parts[d // 2][d % 2]
    weights = w_ref[...].astype(f32)
    grad = mm_tn(first_ref[...], d_ref[...])
    columns = jnp.sum(d_ref[...].astype(f32), axis=0, keepdims=True)
    gain, shift = weights[:, 576:577], weights[:, 577:578]
    used = weights[:, 640 - wide :]
    gain_part = jnp.sum(used * (grad - shift * columns), axis=1, keepdims=True)
    shift_part = jnp.sum(used * columns, axis=1, keepdims=True)
    gain_part = (gain_part + side_ref[:, 64:65]) / gain
    shift_part = shift_part + side_ref[:, 65:66]
    turn_ref[...] = jnp.zeros_like(turn_ref)
    turn_ref[64:80] = small_grad_ref[...]
    turn_ref[pl.ds(69 + group_index(), 1)] = bias_grad_ref[...]
    lane = lanes_of((width, LANES))
    last = jnp.where(lane < 64, grad[:, wide - LANES :], turn_ref[...].T)
    last = jnp.where(lane == 64, gain_part, jnp.where(lane == 65, shift_part, last))
    g_ref[:, : wide - LANES] = grad[:, : wide - LANES].astype(bf16)
    g_ref[:, wide - LANES :] = last.astype(bf16)
    store_pieces(g_ref, even, odd, sems)


def second_grad(parts, first, weights, side, small_grad, bias_grad, dp_size, gates=()):
    total, width = first.shape
    wide = parts[0].shape[2]
    piece = jax.ShapeDtypeStruct((dp_size // 2, width // dp_size, wide), bf16)
    return launch(
        second_grad_kernel,
        gates,
        mark=True,
        cost=0.01,
        out_shape=(piece, piece),
        in_specs=[whole()] * 7,
        out_specs=[whole(pl.ANY)] * 2,
        scratch_shapes=[
            pltpu.VMEM((total, wide), bf16),
            pltpu.VMEM((width, wide), bf16),
            pltpu.VMEM((LANES, width), f32),
            pltpu.SemaphoreType.DMA((dp_size,)),
        ],
    )(*parts, first, weights, side, small_grad, bias_grad)


def part_kernel(near, far, w_ref, *outs):
    cut = near.shape[2]
    weights = w_ref[:, :cut]
    for d in range(GROUP):
        outs[d][...] = mm_nt((near, far)[d // 2][d % 2], weights).astype(bf16)


def input_parts(ones, weight, gates=()):
    row_count, width = ones[0].shape[1], weight.shape[0]
    return launch(
        part_kernel,
        gates,
        mark=True,
        cost=2.5,
        out_shape=[jax.ShapeDtypeStruct((row_count, width), bf16)] * GROUP,
        in_specs=[whole()] * 3,
        out_specs=[whole()] * GROUP,
    )(*ones, weight)


def last_kernel(token_ref, dmixed_ref, small_ref, *refs):
    begun, (near, core, over), weights = refs[:3], refs[3:6], refs[6 : 6 + GROUP]
    out_ref = refs[6 + GROUP]
    unit, inverse = norm_parts(token_ref[...].astype(f32))
    df = sum(v[...].astype(f32) for v in begun)
    for d, two in enumerate((near.at[0], core.at[0], over.at[0], core.at[1])):
        df = df + mm_nt(two[...], weights[d][...])
    back = norm_back(df * small_ref[0:1], unit, inverse)
    out_ref[...] = (dmixed_ref[...] + back).astype(bf16)


def finish_input(tokens, dmixed, small, begun, twos, weights, gates=()):
    return launch(
        last_kernel,
        gates,
        mark=True,
        cost=3.0,
        out_shape=jax.ShapeDtypeStruct(tokens.shape, bf16),
        in_specs=[whole()] * (9 + GROUP),
        out_specs=whole(),
    )(tokens, dmixed, small, *begun, *twos, *weights)


def place_ffn_kernel(*refs):
    shares, in_ref, down_ref = refs[:4], refs[4], refs[5]
    rows, ff = in_ref.shape
    width = down_ref.shape[1]
    low = group_index()
    for case in range(GROUP):

        @pl.when(low == case)
        def _():
            for d in range(GROUP):
                whose = case ^ d
                down_ref[rows * whose : rows * (whose + 1)] = shares[d][:, width:].astype(f32)
                part = shares[d][:, :width].astype(f32)
                for i in range(width // rows):
                    at = 4 * rows * i + rows * whose
                    in_ref[:, at : at + rows] = part[:, rows * i : rows * (i + 1)]


def place_ffn(shares, gates=()):
    rows, wide = shares[0].shape
    width = wide // 2
    return launch(
        place_ffn_kernel,
        gates,
        mark=True,
        cost=3.0,
        out_shape=(
            jax.ShapeDtypeStruct((rows, 4 * width), f32),
            jax.ShapeDtypeStruct((4 * rows, width), f32),
        ),
        in_specs=[whole()] * 4,
        out_specs=[whole()] * 2,
    )(*shares)


def place_qkv_kernel(*refs):
    ones, twos, qkv_ref, out_ref = refs[:4], refs[4:8], refs[8], refs[9]
    rows, width = out_ref.shape
    low = group_index()
    vectors = twos[0][:, 128:].astype(f32)
    for d in range(1, GROUP):
        vectors = vectors + twos[d][:, 128:].astype(f32)
    vectors = vectors.T
    for i, vector_ref in enumerate(refs[10:]):
        for part in range(vector_ref.shape[0] // rows):
            at = 64 + i + part
            vector_ref[part * rows : (part + 1) * rows] = vectors[at : at + 1].reshape(rows)
    cut = width // 2
    halves = [
        ones[i][:, 3 * LANES :].astype(f32) + ones[i + 2][:, 3 * LANES :].astype(f32)
        for i in range(2)
    ]
    for case in range(GROUP):

        @pl.when(low == case)
        def _():
            for i in range(2):
                at = cut * ((case % 2) ^ i)
                out_ref[:, at : at + cut] = halves[i]
            for d in range(GROUP):
                whose = case ^ d
                one, two = ones[d][...].astype(f32), twos[d][...].astype(f32)

                def put(kind, h, part):
                    at = kind * width + 192 * whose + 64 * h
                    qkv_ref[:, at : at + 64] = part

                for h in range(2):
                    put(0, h, one[:, LANES * h : LANES * h + 64])
                    put(1, h, one[:, LANES * h + 64 : LANES * h + LANES])
                    put(2, h, one[:, 2 * LANES + 64 * h : 2 * LANES + 64 * h + 64])
                for kind in range(3):
                    put(kind, 2, two[:, 64 * kind : 64 * kind + 64])


def place_qkv(ones, twos, width, gates=()):
    rows = ones[0].shape[0]
    return launch(
        place_qkv_kernel,
        gates,
        cost=2.0,
        out_shape=(
            jax.ShapeDtypeStruct((rows, 3 * width), f32),
            jax.ShapeDtypeStruct((rows, width), f32),
            *[jax.ShapeDtypeStruct((rows,), f32)] * 5,
            jax.ShapeDtypeStruct((4 * rows,), f32),
        ),
        in_specs=[whole()] * 8,
        out_specs=[whole()] * 8,
    )(*ones, *twos)


def on_device(
    tokens,
    attn_gain,
    attn_shift,
    w_qkv,
    w_out,
    ffn_gain,
    ffn_shift,
    w_in,
    b_in,
    w_down,
    b_down,
    cotangent,
    lengths,
    block_order,
):
    mine = tokens[0]
    row_count, width = mine.shape
    ctx_size = lax.axis_size("ctx")
    dp_size = lax.axis_size("dp")
    far = ctx_size // GROUP
    rows = w_qkv.shape[0]
    half = row_count // 2
    assert math.gcd(H, ctx_size) == GROUP and w_down.shape[0] == GROUP * rows
    where = (lengths, block_order)

    vectors = [attn_gain, attn_shift, ffn_gain, ffn_shift, b_down, b_in]
    piece = pack(w_qkv, vectors)
    far_qkv = far_pieces(piece, "qkv")
    tok_side = swap(mine, "ctx", 1, "tokens_core")
    tok_over = swap(mine, "ctx", 2, "tokens_x")
    piece_in, piece_down = pack_ffn(w_out, w_in, w_down, gates=(piece, tok_side))
    near_qkv = jnp.stack(far_qkv)
    cross_qkv = swap(near_qkv, "dp", 1, "qkv_y")
    tok_over = after(tok_over, near_qkv)
    blocks = [mine, tok_side, tok_over, swap(tok_over, "ctx", 1, "tokens_pass")]
    cot = cotangent[0]

    query, keys, values, first, small, qkv_weight, weight_two = project(
        *where, blocks, near_qkv, cross_qkv
    )
    far_in = far_pieces(after(piece_in, near_qkv, blocks[3]), "in")
    cot_over = swap(after(cot, near_qkv), "ctx", 2, "cot_x")
    near_in = jnp.stack(far_in[:-1] + [after(far_in[-1], small)])
    if far > 1:
        groups = [[g * GROUP + i for g in range(far)] for i in range(GROUP)]
        keys = lax.all_gather(keys, "ctx", axis=1, tiled=True, axis_index_groups=groups)
        values = lax.all_gather(values, "ctx", axis=1, tiled=True, axis_index_groups=groups)

    far_attn, far_query, far_mark = attend(
        query, keys, values, 2, 2, row_count, gates=(near_in, cot_over)
    )
    cross_in = swap(near_in, "dp", 1, "in_y")
    weight_over = swap(weight_two, "ctx", 2, "weight_x")
    cot_side = swap(after(cot, far_mark), "ctx", 1, "cot_core")
    far_down = far_pieces(after(piece_down, near_in), "down")
    near_down = jnp.stack(far_down[:-1] + [after(far_down[-1], far_mark)])
    near_attn, near_query, near_mark = attend(
        query, keys, values, 0, 2, row_count, gates=(far_mark, near_down, weight_over)
    )
    over_attn = swap(far_attn, "ctx", 2, "attn_x")
    cross_down = swap(near_down, "dp", 1, "down_y")
    held_in = after(cross_in, near_mark)
    out_piece = jnp.concatenate([near_in[:, :, width:], held_in[:, :, width:]])
    out_pieces = [out_piece, swap(out_piece, "ctx", 1, "out_core")]
    core_attn = swap(jnp.stack([near_attn[1], over_attn[1]]), "ctx", 1, "attn_core")
    attn = [near_attn, core_attn, over_attn]

    mixed, second, w_o, mixed_mark = project_out(
        mine, attn, out_pieces, small, gates=(cross_down, cot_side)
    )
    side = swap(second, "ctx", 1, "second_core")
    cot_pass = swap(after(cot_over, mixed_mark), "ctx", 1, "cot_pass")
    cots = [cot, cot_side, cot_over, cot_pass]
    if far == 1:
        probs_one, mixed_mark = attend_weights(
            near_query, far_query, keys, (0, 1), gates=(mixed_mark,)
        )
    (own_part, side_part), weights = feed_forward(
        *where,
        small,
        [second, side],
        cots[:2],
        [near_in, held_in, near_down, cross_down],
        (0, 1),
        gates=(mixed_mark,),
    )
    *outs_near, out_mark = out_parts([own_part[1], side_part[1]], weights[1])
    over = after(swap(second, "ctx", 2, "second_x"), out_mark)
    ds_side = swap(side_part[0], "ctx", 1, "ds_core")
    weight_over = after(weight_over, out_mark)
    weight_pair = swap(jnp.stack([weight_two, weight_over]), "ctx", 1, "weight_core")
    two_weights = [weight_two, weight_pair[0], weight_over, weight_pair[1]]
    (over_part,), _ = feed_forward(
        *where, small, [over], cots[2:3], weights, (2,), gates=(out_mark, cot_pass, weight_pair)
    )
    cross = after(swap(over, "ctx", 1, "second_pass"), over_part[0])
    (cross_part,), _ = feed_forward(*where, small, [cross], cots[3:], weights, (3,))
    parts = [own_part, side_part, over_part, cross_part]
    ds_sum = add(over_part[0], swap(cross_part[0], "ctx", 1, "ds_side"))
    even_ff, odd_ff, bias_grad, far_mark = ffn_grads(
        *where,
        cots,
        [second, side, over, cross],
        [part[1] for part in parts],
        [part[2] for part in parts],
        dp_size,
        gates=(ds_sum, ds_side),
    )
    *outs_far, far_mark = out_parts(
        [over_part[1], cross_part[1]], weights[1], gates=(far_mark,)
    )
    if far == 1:
        probs_two, far_mark = attend_weights(
            near_query, far_query, keys, (2,), gates=(far_mark,)
        )
    ds_over = swap(ds_sum, "ctx", 2, "ds_x")
    outs_own, outs_one = outs_near
    outs_two, outs_three = outs_far
    dmixed, small_grad, dattn, out_halves = mixed_back(
        *where,
        mixed,
        cot,
        small,
        w_o,
        attn,
        [own_part[0], ds_side, ds_over],
        gates=(far_mark,),
    )
    dattn_side = swap(dattn[1], "ctx", 1, "dattn_core")
    odd_sent = swap(odd_ff, "dp", 1, "ffn_y")
    outs_side = swap(after(outs_one, dattn_side), "ctx", 1, "outs_core")
    outs_back = swap(after(outs_three, dattn_side), "ctx", 1, "outs_side")

    out_sent = swap(after(out_halves[1], dattn_side), "ctx", 1, "dw_out_core")

    if far > 1:
        over = swap(dattn[2], "ctx", 2, "dattn_x")
        dattn = [dattn[0], dattn_side, over[0], swap(over[1], "ctx", 1, "dattn_pass")]
        ffn_even = add(even_ff, odd_sent)
        dk, dv, dq, _ = attend_back(
            [near_query, far_query],
            keys,
            values,
            [],
            [near_attn, far_attn],
            dattn,
            (0, 1, 2),
            (0, 1, 2, 3),
            "raw",
            (),
        )
        dk, dv = (
            lax.psum_scatter(v, "ctx", scatter_dimension=1, tiled=True, axis_index_groups=groups)
            for v in (dk, dv)
        )
        dq, dk, dv = (v[..., :64].astype(bf16) for v in (dq, dk, dv))
        one = jnp.concatenate([dq[0], dk[0], dq[1], dk[1], dv[0], dv[1]], axis=1)
        two = jnp.concatenate([dq[2], dk[2], dv[2], jnp.zeros_like(dv[2])], axis=1)
        ones, twos = (v.reshape(2, 2, row_count, v.shape[1]) for v in (one, two))
        ones_mark = ones[0]
        outs_sum = add(outs_two, outs_back)
    else:
        *begun, begun_mark = attend_back(
            [near_query],
            keys,
            values,
            [probs_one],
            [near_attn],
            [dattn[0], dattn_side],
            (0, 1),
            (0, 1),
            "begin",
            (),
        )
        over = after(swap(dattn[2], "ctx", 2, "dattn_x"), begun_mark)
        dattn = [dattn[0], dattn_side, over[0], swap(over[1], "ctx", 1, "dattn_pass")]
        ffn_even = add(even_ff, after(odd_sent, begun_mark, outs_side, outs_back, out_sent))
        outs_sum = add(outs_two, outs_back)
        *ones, ones_mark = attend_back(
            [far_query],
            keys,
            values,
            [probs_one],
            [far_attn],
            dattn[2:],
            (0, 1),
            (2, 3),
            "final",
            begun,
            gates=(ffn_even, outs_sum),
        )
    outs_over = after(swap(outs_sum, "ctx", 2, "outs_x"), ones_mark)
    ffn_share = scatter_far(ffn_even, "ffn", ones_mark)

    even, odd, part_sums, first_mark = first_grad(
        ones,
        first,
        qkv_weight,
        (out_halves[0], out_sent),
        dp_size,
    )
    *parts, _ = input_parts(ones, qkv_weight, gates=(first_mark, ffn_share[0]))
    part_side = swap(parts[1], "ctx", 1, "df_core")
    part_sum = add(parts[2], swap(parts[3], "ctx", 1, "df_side"))
    if far == 1:
        *twos, twos_mark = attend_back(
            [near_query, far_query],
            keys,
            values,
            [probs_two],
            [near_attn, far_attn],
            dattn,
            (2,),
            (0, 1, 2, 3),
            "final",
            (),
            gates=(first_mark, part_sum, outs_over, part_side),
        )
    else:
        twos_mark = twos[0]
    part_over = swap(part_sum, "ctx", 2, "df_x")
    ffn_share = ffn_share[1](twos_mark)
    one_even = add(even, after(swap(odd, "dp", 1, "one_y"), twos_mark))
    ffn_share = sum_groups(ffn_share)
    even, odd, second_mark = second_grad(
        twos,
        first,
        qkv_weight,
        part_sums,
        small_grad,
        bias_grad,
        dp_size,
        gates=(ffn_share,),
    )
    one_share = scatter_far(one_even, "one", second_mark)
    two_even = add(even, swap(odd, "dp", 1, "two_y"))
    part_over = after(part_over, second_mark)
    two_even = after(two_even, one_share[0], part_over)
    ffn_over = swap(ffn_share, "ctx", 2, "ffn_x")
    layer_out, out_mark = finish_out(
        *where, mixed, small, [outs_own, outs_side, outs_over], gates=(two_even,)
    )
    two_share = scatter_far(two_even, "two", out_mark)
    one_share = sum_groups(one_share[1](None))
    two_share = sum_groups(two_share[1](None))
    two_shares = gather_group(two_share, "two")
    ffn_over = after(ffn_over, two_shares[2])
    dtwos = exchange_pairs(*twos, "dtwos", two_share)
    ffn_pair = swap(jnp.stack([ffn_share, ffn_over]), "ctx", 1, "ffn_core")
    ffn_shares = [ffn_share, ffn_pair[0], ffn_over, ffn_pair[1]]
    input_grad, input_mark = finish_input(
        mine,
        dmixed,
        small,
        [parts[0], part_side, part_over],
        dtwos,
        two_weights,
    )
    grad_w_in, grad_w_down, ffn_mark = place_ffn(ffn_shares, gates=(input_mark,))
    one_shares = gather_pairs(one_share, "one", two_share)
    grad_w_qkv, grad_w_out, *vector_grads, grad_b_in = place_qkv(
        one_shares, two_shares, width, gates=(ffn_mark,)
    )
    return (
        layer_out[None],
        input_grad[None],
        vector_grads[0],
        vector_grads[1],
        grad_w_qkv,
        grad_w_out,
        vector_grads[2],
        vector_grads[3],
        grad_w_in,
        grad_b_in,
        grad_w_down,
        vector_grads[4],
    )


def solution(mesh):
    placed = (
        P("dp", "ctx", None),
        P("dp"),
        P("dp"),
        P("dp", None),
        P("dp", None),
        P("dp"),
        P("dp"),
        P("dp", None),
        P("dp"),
        P("dp", None),
        P("dp"),
        P("dp", "ctx", None),
        P("dp"),
        P("dp", None),
    )
    return jax.shard_map(
        on_device,
        mesh=mesh,
        in_specs=placed,
        out_specs=(
            P("dp", "ctx", None),
            P("dp", "ctx", None),
            P("dp"),
            P("dp"),
            P("dp", None),
            P("dp", None),
            P("dp"),
            P("dp"),
            P("dp", None),
            P("dp"),
            P("dp", None),
            P("dp"),
        ),
        check_vma=False,
    )
```
